128 devices in a mesh: tm: 64 (over z, y, x), tile: 2 (over core).
Axes of the slice: x: 4, y: 4, z: 4, core: 2. Of those that a mesh axis runs over, the one named last changes fastest.
Arguments:
- prior_space: float32 [1536, 1536], P('tile'), as said below
- node_gain: float32 [1536], replicated, may hold values from 0.4 to 1
- time_diag: float32 [128], P('tm'), may hold values from 0.6 to 1.5
- rho: float32 [128], P('tm'), may hold values from 0.2 to 0.95
- obs_values: float32 [2, 8192, 16, 768], P('tile', 'tm'), may hold values from -0.5 to 0.5
- obs_weight: float32 [2, 8192, 16], P('tile', 'tm'), may hold values from 0.25 to 4
- obs_step: int32 [2, 64, 128], P('tile', 'tm'), may hold values from 0 to 127, each once within a row
Outputs:
- separator_block: float32 [64, 1536, 1536], P('tm', 'tile')
- separator_coupling: float32 [64, 1536, 1536], P('tm', 'tile')
- interior_logdet: float32 [64], P('tm')
The draws below stay inside these ranges and needn't reach their ends.
Inputs may be any that keep to these rules, and one draw needn't show every extreme that they name: prior_space is symmetric and each diagonal entry exceeds the sum of magnitudes of the other entries of its row. For each node block c and each index m of tm, obs_step[c, m] names every time step exactly once.
All inputs are finite; a program needn't handle non-finite values.
Results may differ from the reference program's by a relative error of at most 0.00013.
Values sent between devices are 32-bit elements; how exact they have to be, the bound alone decides.
No kernel may reach another device: no remote copies, remote signals or barrier semaphores. Data moves between devices by JAX's collectives and lax.ppermute only.
A program may use at most 192 MiB of HBM per device.

```python
import math
import jax
import jax.numpy as jnp
from jax import lax

NODES = 1536
OBS_BLK = 16
BLOCK = 768
STEPS = 128
OBS_DEV = 128
N_TM = 64
N_TILE = 2


def draw_prior_space(key, part):
    key_mod, key_diag = jax.random.split(key, 2)
    strength = 4.0
    reach = NODES / 64.0
    bound_total = 2.0 / (math.exp(1.0 / reach) - 1.0)
    order = jnp.arange(NODES, dtype=jnp.float32)
    modulate = jax.random.uniform(key_mod, (NODES, NODES), jnp.float32, 0.8, 1.0)
    symmetric = 0.5 * (modulate + modulate.T)
    distance = jnp.abs(order[:, None] - order[None, :])
    off_part = -(strength / bound_total) * jnp.exp(-distance / reach) * symmetric
    diag_vals = strength * jax.random.uniform(key_diag, (NODES,), jnp.float32, 1.02, 1.25)
    row_ids = lax.broadcasted_iota(jnp.int32, (NODES, NODES), 0)
    col_ids = lax.broadcasted_iota(jnp.int32, (NODES, NODES), 1)
    return jnp.where(row_ids == col_ids, diag_vals[:, None] * jnp.ones((1, NODES), jnp.float32), off_part)


def level_of(key, dims, cuts, least, top_value):
    level, own = 1.0, jax.random.fold_in(key, 6)
    for axis_at, blocks in cuts:
        draws = jnp.exp(jax.random.uniform(jax.random.fold_in(own, axis_at), (blocks,), jnp.float32, least / len(cuts), top_value / len(cuts)))
        level = level * jnp.repeat(draws, dims[axis_at] // blocks).reshape([-1 if axis == axis_at else 1 for axis in range(len(dims))])
    return level


def centred(stream_key, extent, width, limit, shards=(), kind=jnp.bfloat16):
    array = width * jax.random.normal(stream_key, extent, jnp.float32)
    if shards:
        array = array * level_of(stream_key, extent, shards, -0.22, 0.18)
    return jnp.clip(array, -limit, limit).astype(kind)


def setup_inputs(seed: int = 0) -> dict:
    key_list = jax.random.split(jax.random.key(seed), 8)
    prior_space = draw_prior_space(jax.random.fold_in(key_list[7], 71), 0)
    node_gain = jnp.clip(jax.random.uniform(key_list[1], (NODES,), jnp.float32, 0.4, 1.0), 0.4, 1.0)
    time_diag = jnp.clip(jnp.exp(math.log(1.5) - 0.9162907 * jax.random.uniform(key_list[2], (STEPS,), jnp.float32) ** level_of(key_list[2], (STEPS,), ((0, 64),), -0.2, 0.2)), 0.6, 1.5)
    rho = jnp.clip(0.2 + 0.75 * jax.random.uniform(key_list[3], (STEPS,), jnp.float32) ** level_of(key_list[3], (STEPS,), ((0, 64),), -0.2, 0.2), 0.2, 0.95)
    obs_values = centred(key_list[4], (N_TILE, N_TM * OBS_DEV, OBS_BLK, BLOCK), (1.0 / (N_TM * OBS_BLK) ** 0.5), 0.5, ((0, 2), (1, 64)), jnp.float32)
    obs_weight = jnp.clip(jnp.exp(math.log(4.0) - 2.7725887 * jax.random.uniform(key_list[5], (N_TILE, N_TM * OBS_DEV, OBS_BLK), jnp.float32) ** level_of(key_list[5], (N_TILE, N_TM * OBS_DEV, OBS_BLK), ((0, 2), (1, 64)), -0.2, 0.2)), 0.25, 4.0)
    obs_step = jax.vmap(lambda own: jax.random.permutation(own, STEPS))(jax.random.split(key_list[6], N_TILE * N_TM)).reshape((N_TILE, N_TM, STEPS)).astype(jnp.int32)
    return {"prior_space": prior_space, "node_gain": node_gain, "time_diag": time_diag, "rho": rho, "obs_values": obs_values, "obs_weight": obs_weight, "obs_step": obs_step}


def reference(prior_space, node_gain, time_diag, rho, obs_values, obs_weight, obs_step):
    precise = lax.Precision.HIGHEST
    scaled = obs_values * obs_weight[..., None]
    tile_steps = obs_step.reshape(N_TILE, N_TM * OBS_DEV)

    def add_tile(grams, inputs):
        scaled_tile, plain_tile, step_ids = inputs
        terms = jnp.einsum('crb,crd->cbd', scaled_tile, plain_tile, precision=precise)

        def place(gram_block, step_id, term_block):
            current = lax.dynamic_index_in_dim(gram_block, step_id, 0, keepdims=False)
            return lax.dynamic_update_index_in_dim(gram_block, current + term_block, step_id, 0)
        return (jax.vmap(place)(grams, step_ids, terms), None)
    start_grams = jnp.zeros((N_TILE, STEPS, BLOCK, BLOCK), jnp.float32)
    grams, unused = lax.scan(add_tile, start_grams, (jnp.swapaxes(scaled, 0, 1), jnp.swapaxes(obs_values, 0, 1), jnp.swapaxes(tile_steps, 0, 1)))
    grams = jnp.transpose(grams.reshape(N_TILE, N_TM, 2, BLOCK, BLOCK), (1, 2, 0, 3, 4))
    picker = jnp.eye(N_TILE, dtype=jnp.float32)

    def assemble(coef, gram_step):
        placed = gram_step[:, :, None, :] * picker[:, None, :, None]
        return coef * prior_space + placed.reshape(NODES, NODES)
    coefs = time_diag.reshape(N_TM, 2)
    rates = rho.reshape(N_TM, 2)
    gain_matrix = jnp.diag(node_gain)

    def interior(inputs):
        coef, gram_step = inputs
        matrix = assemble(coef, gram_step)
        lower_factor = jnp.linalg.cholesky(matrix)
        log_det = 2.0 * jnp.sum(jnp.log(jnp.diagonal(lower_factor))) / NODES
        half_solve = lax.linalg.triangular_solve(lower_factor, gain_matrix, left_side=True, lower=True)
        inverse_cols = lax.linalg.triangular_solve(lower_factor, half_solve, left_side=True, lower=True, transpose_a=True)
        return (node_gain[:, None] * inverse_cols, log_det)
    schur_all, interior_logdet = lax.map(interior, (coefs[:, 0], grams[:, 0]))
    shifted = rates[1:, 0][:, None, None] ** 2 * schur_all[1:]
    following = jnp.concatenate([shifted, jnp.zeros((1, NODES, NODES), jnp.float32)], axis=0)
    separators = lax.map(lambda inputs: assemble(inputs[0], inputs[1]), (coefs[:, 1], grams[:, 1]))
    separator_block = separators - rates[:, 1][:, None, None] ** 2 * schur_all - following
    separator_coupling = -(rates[:, 0] * rates[:, 1])[:, None, None] * schur_all
    return (separator_block, separator_coupling, interior_logdet)
```

```python
import functools

import jax
import jax.numpy as jnp
from jax import lax
from jax.experimental import pallas as pl
from jax.experimental.pallas import tpu as pltpu
from jax.sharding import PartitionSpec as P

F32, BF16 = jnp.float32, jnp.bfloat16
BASE = 128
MIB = 1 << 20
NN = (((1,), (0,)), ((), ()))
NT = (((1,), (1,)), ((), ()))
TN = (((0,), (0,)), ((), ()))


def halves(x):
    high = x.astype(BF16)
    return high, (x - high.astype(F32)).astype(BF16)


def product(a, b, dims):
    dot = functools.partial(lax.dot_general, dimension_numbers=dims, preferred_element_type=F32)
    return dot(a[0], b[0]) + (dot(a[0], b[1]) + dot(a[1], b[0]))


def reorder_kernel(steps, weights_t, values, interior, separator, held, in_sems, out_sems):
    tiles = held.shape[0]
    chunks = in_sems.shape[0]
    per = tiles // chunks
    for chunk in range(chunks):
        rows = pl.ds(chunk * per, per)
        pltpu.make_async_copy(values.at[rows], held.at[rows], in_sems.at[chunk]).start()
    root = jnp.sqrt(weights_t[...])
    for chunk in range(chunks):
        rows = pl.ds(chunk * per, per)
        pltpu.make_async_copy(values.at[rows], held.at[rows], in_sems.at[chunk]).wait()
        for tile in range(chunk * per, (chunk + 1) * per):
            held[tile] = held[tile] * root[:, tile : tile + 1]
            step = steps[tile]
            partition = lax.shift_right_logical(step, 1)
            odd = lax.bitwise_and(step, 1)

            @pl.when(odd == 0)
            def _():
                pltpu.make_async_copy(held.at[tile], interior.at[partition], out_sems.at[0]).start()

            @pl.when(odd == 1)
            def _():
                pltpu.make_async_copy(held.at[tile], separator.at[partition], out_sems.at[1]).start()

    half = pl.ds(0, tiles // 2)
    pltpu.make_async_copy(held.at[half], interior, out_sems.at[0]).wait()
    pltpu.make_async_copy(held.at[half], separator, out_sems.at[1]).wait()


def reorder(steps, weights_t, values):
    tiles, rows, cols = values.shape
    half = jax.ShapeDtypeStruct((tiles // 2, rows, cols), F32)
    anywhere = pl.BlockSpec(memory_space=pl.ANY)
    return pl.pallas_call(
        reorder_kernel,
        out_shape=(half, half),
        in_specs=[
            pl.BlockSpec(memory_space=pltpu.SMEM),
            pl.BlockSpec(memory_space=pltpu.VMEM),
            anywhere,
        ],
        out_specs=(anywhere, anywhere),
        scratch_shapes=[
            pltpu.VMEM((tiles, rows, cols), F32),
            pltpu.SemaphoreType.DMA((8,)),
            pltpu.SemaphoreType.DMA((2,)),
        ],
        compiler_params=pltpu.CompilerParams(vmem_limit_bytes=16 * MIB),
        name="reorder",
    )(steps, weights_t, values)


def wide(x):
    return jnp.broadcast_to(x, (8, BASE))


def sweep_small(entries, size):
    at = lambda i, j: (min(i, j), max(i, j))
    dets = []
    for p in range(0, size, 2):
        a, b, d = entries[p, p], entries[p, p + 1], entries[p + 1, p + 1]
        det = a * d - b * b
        dets.append(det)
        scale = 1.0 / det
        inv_a, inv_b, inv_d = d * scale, b * scale, a * scale
        others = [i for i in range(size) if i not in (p, p + 1)]
        u = {i: entries[at(i, p)] for i in others}
        v = {i: entries[at(i, p + 1)] for i in others}
        new_u = {i: inv_a * u[i] - inv_b * v[i] for i in others}
        new_v = {i: inv_d * v[i] - inv_b * u[i] for i in others}
        for i in others:
            for j in others:
                if i <= j:
                    entries[i, j] = entries[i, j] - u[i] * new_u[j] - v[i] * new_v[j]
        for i in others:
            entries[at(i, p)] = new_u[i]
            entries[at(i, p + 1)] = new_v[i]
        entries[p, p], entries[p, p + 1], entries[p + 1, p + 1] = -inv_a, inv_b, -inv_d
    return dets


def sweep_base(x):
    lane = lax.broadcasted_iota(jnp.int32, (8, BASE), 1)
    sub = lax.broadcasted_iota(jnp.int32, (8, BASE), 0)
    x = list(x)
    groups = len(x)
    dets = jnp.ones((8, BASE), F32)
    for q in range(groups):
        panel = x[q]
        inside = (lane // 8) == q
        first = 8 * q
        entries = {
            (i, j): wide(panel[i : i + 1, first + j : first + j + 1])
            for i in range(8)
            for j in range(i, 8)
        }
        marked = jnp.where(inside, jnp.where(lane == first + sub, -1.0, 0.0), panel)
        rows = [wide(marked[j : j + 1, :]) for j in range(8)]
        for at, det in enumerate(sweep_small(entries, 8)):
            dets = jnp.where(lane == 4 * q + at, det, dets)
        new_rows = []
        for i in range(8):
            total = entries[0, i] * rows[0]
            for j in range(1, 8):
                total = total + entries[min(i, j), max(i, j)] * rows[j]
            new_rows.append(total)
        new_panel = new_rows[7]
        for i in range(7):
            new_panel = jnp.where(sub == i, new_rows[i], new_panel)
        for i in [(q + d) % groups for d in range(1, groups)]:
            total = jnp.where(inside, 0.0, x[i])
            for j in range(8):
                total = total + wide(x[i][:, first + j : first + j + 1]) * new_rows[j]
            x[i] = total
        x[q] = -new_panel
    return x, dets


def unit_scales(m, size):
    eye = lax.broadcasted_iota(jnp.int32, (BASE, BASE), 0) == lax.broadcasted_iota(
        jnp.int32, (BASE, BASE), 1
    )
    columns, rows = [], []
    for k in range(size // BASE):
        here = pl.ds(k * BASE, BASE)
        diagonal = jnp.where(eye, m[here, here], 0.0)
        columns.append(lax.rsqrt(jnp.sum(diagonal, axis=1, keepdims=True)))
        rows.append(lax.rsqrt(jnp.sum(diagonal, axis=0, keepdims=True)))
    return columns, jnp.concatenate(rows, axis=1)


def invert(m, panel, left, right, size):
    def step(k, logs):
        here = pl.ds(pl.multiple_of(k * BASE, BASE), BASE)
        groups = [
            m[pl.ds(pl.multiple_of(k * BASE + 8 * q, 8), 8), here] for q in range(BASE // 8)
        ]
        swept, dets = sweep_base(groups)
        swept = jnp.concatenate(swept, axis=0)
        inverse = halves(-swept)
        panel[...] = product(inverse, halves(m[here, :]), NN)
        panel[:, here] = swept
        high, low = halves(panel[...])
        right[0, :BASE], right[0, BASE:] = high, high
        right[1, :BASE], right[1, BASE:] = low, low
        high, low = halves(m[:, here])
        left[:, :BASE], left[:, BASE:] = high, low
        m[:, here] = jnp.zeros((size, BASE), F32)
        rows = 256
        for first in range(0, size, rows):
            part = left[first : first + rows, :]
            dot = functools.partial(lax.dot_general, dimension_numbers=NN, preferred_element_type=F32)
            m[first : first + rows, :] -= dot(part, right[0]) + dot(part, right[1])
        m[here, :] = panel[...]
        return logs + jnp.log(dets[0:1, :])

    logs = lax.fori_loop(0, size // BASE, step, jnp.zeros((1, BASE), F32))
    return jnp.sum(logs, axis=1, keepdims=True)


def own_kernel(place, time_diag, tiles, prior, block, inverse, logdet, split, panel, left, right):
    size = block.shape[0]
    own = place[0]
    scale = time_diag[0]
    high, low = halves(tiles[...])
    split[0], split[1] = high, low
    rows = 256
    for first in range(0, size, rows):
        part = (split[0, :, first : first + rows], split[1, :, first : first + rows])
        gram = product(part, (split[0], split[1]), TN)
        columns = pl.ds(pl.multiple_of(own * size, size), size)
        block[first : first + rows, :] = scale * prior[first : first + rows, columns] + gram
    by_row, by_column = unit_scales(block, size)
    for k, row_scale in enumerate(by_row):
        here = pl.ds(k * BASE, BASE)
        inverse[here, :] = block[here, :] * row_scale * by_column
    log_total = invert(inverse, panel, left, right, size)
    logdet[...] = log_total - 2.0 * jnp.sum(jnp.log(by_column), axis=1, keepdims=True)
    for k, row_scale in enumerate(by_row):
        here = pl.ds(k * BASE, BASE)
        inverse[here, :] = inverse[here, :] * (-row_scale) * by_column


def scratch_of(size):
    return [
        pltpu.VMEM((BASE, size), F32),
        pltpu.VMEM((size, 2 * BASE), BF16),
        pltpu.VMEM((2, 2 * BASE, size), BF16),
    ]


def invert_own(place, time_diag, tiles, prior):
    size = prior.shape[0]
    square = jax.ShapeDtypeStruct((size, size), F32)
    smem = pl.BlockSpec(memory_space=pltpu.SMEM)
    vmem = pl.BlockSpec(memory_space=pltpu.VMEM)
    return pl.pallas_call(
        own_kernel,
        out_shape=(square, square, jax.ShapeDtypeStruct((1, 1), F32)),
        in_specs=[smem, smem, vmem, vmem],
        out_specs=(vmem, vmem, vmem),
        scratch_shapes=[pltpu.VMEM((2, *tiles.shape), BF16)] + scratch_of(size),
        compiler_params=pltpu.CompilerParams(vmem_limit_bytes=48 * MIB),
        cost_estimate=pl.CostEstimate(flops=40 * size**3, bytes_accessed=16 * MIB, transcendentals=0),
        name="invert_own",
    )(place, time_diag, tiles, prior)


def rest_kernel(
    place, time_diag, other_inverse, block, prior, gain_row, gain_column, schur, logdet,
    reached, work, split_a, split_b, panel, left, right,
):
    size = block.shape[0]
    own = place[0]
    scale = time_diag[0]
    own_columns = pl.ds(pl.multiple_of(own * size, size), size)
    other_columns = pl.ds(pl.multiple_of((1 - own) * size, size), size)
    split_a[0], split_a[1] = halves(scale * prior[:, other_columns])
    split_b[0], split_b[1] = halves(other_inverse[...])
    rows = 256
    for first in range(0, size, rows):
        here = slice(first, first + rows)
        reached[here, :] = product((split_a[0, here], split_a[1, here]), (split_b[0], split_b[1]), NN)
        part = halves(reached[here, :])
        work[here, :] = block[here, :] - product(part, (split_a[0], split_a[1]), NT)
    by_row, by_column = unit_scales(work, size)
    for k, row_scale in enumerate(by_row):
        here = pl.ds(k * BASE, BASE)
        work[here, :] = work[here, :] * row_scale * by_column
    log_total = invert(work, panel, left, right, size)
    logdet[...] = log_total - 2.0 * jnp.sum(jnp.log(by_column), axis=1, keepdims=True)
    split_b[0], split_b[1] = halves(reached[...])
    own_gain = gain_row[:, own_columns]
    other_gain = gain_row[:, other_columns]
    for k, row_scale in enumerate(by_row):
        here = pl.ds(k * BASE, BASE)
        rows_out = work[here, :] * (-row_scale * gain_column[here, :]) * by_column
        schur[here, own_columns] = rows_out * own_gain
        schur[here, other_columns] = product(halves(rows_out), (split_b[0], split_b[1]), NN) * -other_gain


def invert_rest(place, time_diag, other_inverse, block, prior, gain_row, gain_column):
    size = prior.shape[0]
    smem = pl.BlockSpec(memory_space=pltpu.SMEM)
    vmem = pl.BlockSpec(memory_space=pltpu.VMEM)
    return pl.pallas_call(
        rest_kernel,
        out_shape=(jax.ShapeDtypeStruct(prior.shape, F32), jax.ShapeDtypeStruct((1, 1), F32)),
        in_specs=[smem, smem] + [vmem] * 5,
        out_specs=(vmem, vmem),
        scratch_shapes=[
            pltpu.VMEM((size, size), F32),
            pltpu.VMEM((size, size), F32),
            pltpu.VMEM((2, size, size), BF16),
            pltpu.VMEM((2, size, size), BF16),
        ]
        + scratch_of(size),
        compiler_params=pltpu.CompilerParams(vmem_limit_bytes=48 * MIB),
        cost_estimate=pl.CostEstimate(flops=40 * size**3, bytes_accessed=16 * MIB, transcendentals=0),
        name="invert_rest",
    )(place, time_diag, other_inverse, block, prior, gain_row, gain_column)


def separator_kernel(place, time_diag, rho, tiles, prior, schur, reduced, coupling, split):
    size = prior.shape[0]
    own = place[0]
    split[0], split[1] = halves(tiles[...])
    own_columns = pl.ds(pl.multiple_of(own * size, size), size)
    other_columns = pl.ds(pl.multiple_of((1 - own) * size, size), size)
    rows = 256
    for first in range(0, size, rows):
        here = slice(first, first + rows)
        gram = product((split[0, :, here], split[1, :, here]), (split[0], split[1]), TN)
        for columns, term in ((own_columns, gram), (other_columns, 0.0)):
            part = schur[here, columns]
            reduced[here, columns] = time_diag[1] * prior[here, columns] + term - rho[1] * rho[1] * part
            coupling[here, columns] = -(rho[0] * rho[1]) * part


def separator_rows(place, time_diag, rho, tiles, prior, schur):
    out = jax.ShapeDtypeStruct(prior.shape, F32)
    smem = pl.BlockSpec(memory_space=pltpu.SMEM)
    vmem = pl.BlockSpec(memory_space=pltpu.VMEM)
    return pl.pallas_call(
        separator_kernel,
        out_shape=(out, out),
        in_specs=[smem] * 3 + [vmem] * 3,
        out_specs=(vmem, vmem),
        scratch_shapes=[pltpu.VMEM((2, *tiles.shape), BF16)],
        compiler_params=pltpu.CompilerParams(vmem_limit_bytes=48 * MIB),
        cost_estimate=pl.CostEstimate(flops=6 * prior.size * tiles.shape[0], bytes_accessed=24 * MIB, transcendentals=0),
        name="separator",
    )(place, time_diag, rho, tiles, prior, schur)


def from_next(x):
    count = lax.axis_size("tm")
    return lax.ppermute(x, "tm", [(i, i - 1) for i in range(1, count)])


def from_other(x):
    return lax.ppermute(x, "tile", [(0, 1), (1, 0)])


def to_partitions(x):
    return lax.all_to_all(x, "tm", split_axis=0, concat_axis=0, tiled=True).reshape(-1, x.shape[-1])


def on_device(prior, node_gain, time_diag, rho, values, weights, steps):
    size, nodes = prior.shape
    own = lax.axis_index("tile")
    place = own.reshape(1).astype(jnp.int32)
    interior, separator = reorder(steps[0, 0], weights[0].T, values[0])
    next_rho = from_next(rho)
    gain_row = node_gain.reshape(1, nodes)
    gain_column = lax.dynamic_slice_in_dim(node_gain, own * size, size).reshape(size, 1)
    interior = to_partitions(interior)
    interior, separator = lax.optimization_barrier((interior, separator))
    separator = to_partitions(separator)
    block, own_inverse, own_log = invert_own(place, time_diag, interior, prior)
    other_inverse = from_other(own_inverse)
    schur, rest_log = invert_rest(place, time_diag, other_inverse, block, prior, gain_row, gain_column)
    incoming = from_next(schur)
    log = jnp.where(own == 0, own_log, rest_log).reshape(1)
    interior_logdet = (log + from_other(log)) / nodes
    reduced, coupling = separator_rows(place, time_diag, rho, separator, prior, schur)
    separator_block = reduced - next_rho[0] * next_rho[0] * incoming
    return separator_block[None], coupling[None], interior_logdet


def solution(mesh):
    in_specs = (
        P("tile", None),
        P(),
        P("tm"),
        P("tm"),
        P("tile", "tm", None, None),
        P("tile", "tm", None),
        P("tile", "tm", None),
    )
    out_specs = (P("tm", "tile", None), P("tm", "tile", None), P("tm"))
    return jax.shard_map(on_device, mesh=mesh, in_specs=in_specs, out_specs=out_specs, check_vma=False)
```

```python
import functools

import jax
import jax.numpy as jnp
from jax import lax
from jax.experimental import pallas as pl
from jax.experimental.pallas import tpu as pltpu
from jax.sharding import PartitionSpec as P

F32, BF16 = jnp.float32, jnp.bfloat16
BASE = 128
MIB = 1 << 20
NN = (((1,), (0,)), ((), ()))
NT = (((1,), (1,)), ((), ()))
TN = (((0,), (0,)), ((), ()))


def halves(x):
    high = x.astype(BF16)
    return high, (x - high.astype(F32)).astype(BF16)


def product(a, b, dims):
    dot = functools.partial(lax.dot_general, dimension_numbers=dims, preferred_element_type=F32)
    return dot(a[0], b[0]) + (dot(a[0], b[1]) + dot(a[1], b[0]))


def reorder_kernel(steps, weights_t, values, interior, separator, held, in_sems, out_sems):
    tiles = held.shape[0]
    chunks = in_sems.shape[0]
    per = tiles // chunks
    for chunk in range(chunks):
        rows = pl.ds(chunk * per, per)
        pltpu.make_async_copy(values.at[rows], held.at[rows], in_sems.at[chunk]).start()
    root = jnp.sqrt(weights_t[...])
    for chunk in range(chunks):
        rows = pl.ds(chunk * per, per)
        pltpu.make_async_copy(values.at[rows], held.at[rows], in_sems.at[chunk]).wait()
        for tile in range(chunk * per, (chunk + 1) * per):
            held[tile] = held[tile] * root[:, tile : tile + 1]
            step = steps[tile]
            partition = lax.shift_right_logical(step, 1)
            odd = lax.bitwise_and(step, 1)

            @pl.when(odd == 0)
            def _():
                pltpu.make_async_copy(held.at[tile], interior.at[partition], out_sems.at[0]).start()

            @pl.when(odd == 1)
            def _():
                pltpu.make_async_copy(held.at[tile], separator.at[partition], out_sems.at[1]).start()

    half = pl.ds(0, tiles // 2)
    pltpu.make_async_copy(held.at[half], interior, out_sems.at[0]).wait()
    pltpu.make_async_copy(held.at[half], separator, out_sems.at[1]).wait()


def reorder(steps, weights_t, values):
    tiles, rows, cols = values.shape
    half = jax.ShapeDtypeStruct((tiles // 2, rows, cols), F32)
    anywhere = pl.BlockSpec(memory_space=pl.ANY)
    return pl.pallas_call(
        reorder_kernel,
        out_shape=(half, half),
        in_specs=[
            pl.BlockSpec(memory_space=pltpu.SMEM),
            pl.BlockSpec(memory_space=pltpu.VMEM),
            anywhere,
        ],
        out_specs=(anywhere, anywhere),
        scratch_shapes=[
            pltpu.VMEM((tiles, rows, cols), F32),
            pltpu.SemaphoreType.DMA((8,)),
            pltpu.SemaphoreType.DMA((2,)),
        ],
        compiler_params=pltpu.CompilerParams(vmem_limit_bytes=56 * MIB),
        name="reorder",
    )(steps, weights_t, values)


def wide(x):
    return jnp.broadcast_to(x, (8, BASE))


def sweep_small(entries, size):
    at = lambda i, j: (min(i, j), max(i, j))
    dets = []
    for p in range(0, size, 2):
        a, b, d = entries[p, p], entries[p, p + 1], entries[p + 1, p + 1]
        det = a * d - b * b
        dets.append(det)
        scale = 1.0 / det
        inv_a, inv_b, inv_d = d * scale, b * scale, a * scale
        others = [i for i in range(size) if i not in (p, p + 1)]
        u = {i: entries[at(i, p)] for i in others}
        v = {i: entries[at(i, p + 1)] for i in others}
        new_u = {i: inv_a * u[i] - inv_b * v[i] for i in others}
        new_v = {i: inv_d * v[i] - inv_b * u[i] for i in others}
        for i in others:
            for j in others:
                if i <= j:
                    entries[i, j] = entries[i, j] - u[i] * new_u[j] - v[i] * new_v[j]
        for i in others:
            entries[at(i, p)] = new_u[i]
            entries[at(i, p + 1)] = new_v[i]
        entries[p, p], entries[p, p + 1], entries[p + 1, p + 1] = -inv_a, inv_b, -inv_d
    return dets


def sweep_base(x):
    lane = lax.broadcasted_iota(jnp.int32, (8, BASE), 1)
    sub = lax.broadcasted_iota(jnp.int32, (8, BASE), 0)
    x = list(x)
    groups = len(x)
    dets = jnp.ones((8, BASE), F32)
    for q in range(groups):
        panel = x[q]
        inside = (lane // 8) == q
        first = 8 * q
        entries = {
            (i, j): wide(panel[i : i + 1, first + j : first + j + 1])
            for i in range(8)
            for j in range(i, 8)
        }
        marked = jnp.where(inside, jnp.where(lane == first + sub, -1.0, 0.0), panel)
        rows = [wide(marked[j : j + 1, :]) for j in range(8)]
        for at, det in enumerate(sweep_small(entries, 8)):
            dets = jnp.where(lane == 4 * q + at, det, dets)
        new_rows = []
        for i in range(8):
            total = entries[0, i] * rows[0]
            for j in range(1, 8):
                total = total + entries[min(i, j), max(i, j)] * rows[j]
            new_rows.append(total)
        new_panel = new_rows[7]
        for i in range(7):
            new_panel = jnp.where(sub == i, new_rows[i], new_panel)
        for i in [(q + d) % groups for d in range(1, groups)]:
            total = jnp.where(inside, 0.0, x[i])
            for j in range(8):
                total = total + wide(x[i][:, first + j : first + j + 1]) * new_rows[j]
            x[i] = total
        x[q] = -new_panel
    return x, dets


def unit_scales(m, size):
    eye = lax.broadcasted_iota(jnp.int32, (BASE, BASE), 0) == lax.broadcasted_iota(
        jnp.int32, (BASE, BASE), 1
    )
    columns, rows = [], []
    for k in range(size // BASE):
        here = pl.ds(k * BASE, BASE)
        diagonal = jnp.where(eye, m[here, here], 0.0)
        columns.append(lax.rsqrt(jnp.sum(diagonal, axis=1, keepdims=True)))
        rows.append(lax.rsqrt(jnp.sum(diagonal, axis=0, keepdims=True)))
    return columns, jnp.concatenate(rows, axis=1)


def invert(m, panel, left, right, size, pivots):
    def step(k, logs):
        here = pl.ds(pl.multiple_of(k * BASE, BASE), BASE)
        groups = [
            m[pl.ds(pl.multiple_of(k * BASE + 8 * q, 8), 8), here] for q in range(BASE // 8)
        ]
        swept, dets = sweep_base(groups)
        swept = jnp.concatenate(swept, axis=0)
        inverse = halves(-swept)
        panel[...] = product(inverse, halves(m[here, :]), NN)
        panel[:, here] = swept
        high, low = halves(panel[...])
        right[0, :BASE], right[0, BASE:] = high, high
        right[1, :BASE], right[1, BASE:] = low, low
        high, low = halves(m[:, here])
        left[:, :BASE], left[:, BASE:] = high, low
        m[:, here] = jnp.zeros((size, BASE), F32)
        rows = 256 if size % 256 == 0 else BASE
        for first in range(0, size, rows):
            part = left[first : first + rows, :]
            dot = functools.partial(lax.dot_general, dimension_numbers=NN, preferred_element_type=F32)
            m[first : first + rows, :] -= dot(part, right[0]) + dot(part, right[1])
        m[here, :] = panel[...]
        return logs + jnp.log(dets[0:1, :])

    logs = lax.fori_loop(0, pivots // BASE, step, jnp.zeros((1, BASE), F32))
    return jnp.sum(logs, axis=1, keepdims=True)


def own_kernel(place, time_diag, tiles, prior, block, inverse, logdet, split, panel, left, right):
    size = block.shape[0]
    own = place[0]
    scale = time_diag[0]
    high, low = halves(tiles[...])
    split[0], split[1] = high, low
    rows = 256
    for first in range(0, size, rows):
        part = (split[0, :, first : first + rows], split[1, :, first : first + rows])
        gram = product(part, (split[0], split[1]), TN)
        columns = pl.ds(pl.multiple_of(own * size, size), size)
        block[first : first + rows, :] = scale * prior[first : first + rows, columns] + gram
    by_row, by_column = unit_scales(block, size)
    for k, row_scale in enumerate(by_row):
        here = pl.ds(k * BASE, BASE)
        inverse[here, :] = block[here, :] * row_scale * by_column
    log_total = invert(inverse, panel, left, right, size, size)
    logdet[...] = log_total - 2.0 * jnp.sum(jnp.log(by_column), axis=1, keepdims=True)
    for k, row_scale in enumerate(by_row):
        here = pl.ds(k * BASE, BASE)
        inverse[here, :] = inverse[here, :] * (-row_scale) * by_column


def scratch_of(size):
    return [
        pltpu.VMEM((BASE, size), F32),
        pltpu.VMEM((size, 2 * BASE), BF16),
        pltpu.VMEM((2, 2 * BASE, size), BF16),
    ]


def invert_own(place, time_diag, tiles, prior):
    size = prior.shape[0]
    square = jax.ShapeDtypeStruct((size, size), F32)
    smem = pl.BlockSpec(memory_space=pltpu.SMEM)
    vmem = pl.BlockSpec(memory_space=pltpu.VMEM)
    return pl.pallas_call(
        own_kernel,
        out_shape=(square, square, jax.ShapeDtypeStruct((1, 1), F32)),
        in_specs=[smem, smem, vmem, vmem],
        out_specs=(vmem, vmem, vmem),
        scratch_shapes=[pltpu.VMEM((2, *tiles.shape), BF16)] + scratch_of(size),
        compiler_params=pltpu.CompilerParams(vmem_limit_bytes=48 * MIB),
        cost_estimate=pl.CostEstimate(flops=40 * size**3, bytes_accessed=16 * MIB, transcendentals=0),
        name="invert_own",
    )(place, time_diag, tiles, prior)


def head_kernel(place, time_diag, other_inverse, block, prior, reached, early, rest, logdet, work, split_a, split_b, panel, left, right):
    size = block.shape[0]
    head = early.shape[1]
    scale = time_diag[0]
    other_columns = pl.ds(pl.multiple_of((1 - place[0]) * size, size), size)
    split_a[0], split_a[1] = halves(scale * prior[:, other_columns])
    split_b[0], split_b[1] = halves(other_inverse[...])
    rows = 256
    for first in range(0, size, rows):
        here = slice(first, first + rows)
        reached[here, :] = product((split_a[0, here], split_a[1, here]), (split_b[0], split_b[1]), NN)
        part = halves(reached[here, :])
        work[here, :] = block[here, :] - product(part, (split_a[0], split_a[1]), NT)
    by_row, by_column = unit_scales(work, size)
    for k, row_scale in enumerate(by_row):
        here = pl.ds(k * BASE, BASE)
        work[here, :] = work[here, :] * row_scale * by_column
    log_total = invert(work, panel, left, right, size, head)
    by_head = by_column[:, :head]
    logdet[...] = log_total - 2.0 * jnp.sum(jnp.log(by_head), axis=1, keepdims=True)
    back = 1.0 / by_column[:, head:]
    for k, row_scale in enumerate(by_row):
        here = pl.ds(k * BASE, BASE)
        if k * BASE < head:
            early[here, :] = work[here, :head] * (-row_scale) * by_head
        else:
            row_back = 1.0 / row_scale
            early[here, :] = work[here, :head] * row_back * by_head
            rest[pl.ds(k * BASE - head, BASE), :] = work[here, head:] * row_back * back


def invert_head(place, time_diag, other_inverse, block, prior, head):
    size = prior.shape[0]
    shape = lambda *dims: jax.ShapeDtypeStruct(dims, F32)
    smem = pl.BlockSpec(memory_space=pltpu.SMEM)
    vmem = pl.BlockSpec(memory_space=pltpu.VMEM)
    return pl.pallas_call(
        head_kernel,
        out_shape=(shape(size, size), shape(size, head), shape(size - head, size - head), shape(1, 1)),
        in_specs=[smem, smem] + [vmem] * 3,
        out_specs=(vmem,) * 4,
        scratch_shapes=[
            pltpu.VMEM((size, size), F32),
            pltpu.VMEM((2, size, size), BF16),
            pltpu.VMEM((2, size, size), BF16),
        ]
        + scratch_of(size),
        compiler_params=pltpu.CompilerParams(vmem_limit_bytes=44 * MIB),
        cost_estimate=pl.CostEstimate(flops=80 * size**3, bytes_accessed=16 * MIB, transcendentals=0),
        name="invert_head",
    )(place, time_diag, other_inverse, block, prior)


def tail_kernel(rest, inverse, logdet, panel, left, right):
    size = rest.shape[0]
    by_row, by_column = unit_scales(rest, size)
    for k, row_scale in enumerate(by_row):
        here = pl.ds(k * BASE, BASE)
        inverse[here, :] = rest[here, :] * row_scale * by_column
    log_total = invert(inverse, panel, left, right, size, size)
    logdet[...] = log_total - 2.0 * jnp.sum(jnp.log(by_column), axis=1, keepdims=True)
    for k, row_scale in enumerate(by_row):
        here = pl.ds(k * BASE, BASE)
        inverse[here, :] = inverse[here, :] * (-row_scale) * by_column


def invert_tail(rest):
    size = rest.shape[0]
    vmem = pl.BlockSpec(memory_space=pltpu.VMEM)
    return pl.pallas_call(
        tail_kernel,
        out_shape=(jax.ShapeDtypeStruct(rest.shape, F32), jax.ShapeDtypeStruct((1, 1), F32)),
        in_specs=[vmem],
        out_specs=(vmem, vmem),
        scratch_shapes=scratch_of(size),
        compiler_params=pltpu.CompilerParams(vmem_limit_bytes=40 * MIB),
        cost_estimate=pl.CostEstimate(flops=200 * size**3, bytes_accessed=4 * MIB, transcendentals=0),
        name="invert_tail",
    )(rest)


def separator_kernel(place, time_diag, tiles, prior, assembled, split):
    size = prior.shape[0]
    own = place[0]
    split[0], split[1] = halves(tiles[...])
    own_columns = pl.ds(pl.multiple_of(own * size, size), size)
    other_columns = pl.ds(pl.multiple_of((1 - own) * size, size), size)
    scale = time_diag[1]
    rows = 256
    for first in range(0, size, rows):
        here = slice(first, first + rows)
        gram = product((split[0, :, here], split[1, :, here]), (split[0], split[1]), TN)
        assembled[here, own_columns] = scale * prior[here, own_columns] + gram
        assembled[here, other_columns] = scale * prior[here, other_columns]


def assemble_separator(place, time_diag, tiles, prior):
    smem = pl.BlockSpec(memory_space=pltpu.SMEM)
    vmem = pl.BlockSpec(memory_space=pltpu.VMEM)
    return pl.pallas_call(
        separator_kernel,
        out_shape=jax.ShapeDtypeStruct(prior.shape, F32),
        in_specs=[smem] * 2 + [vmem] * 2,
        out_specs=vmem,
        scratch_shapes=[pltpu.VMEM((2, *tiles.shape), BF16)],
        compiler_params=pltpu.CompilerParams(vmem_limit_bytes=40 * MIB),
        cost_estimate=pl.CostEstimate(
            flops=6 * prior.size * tiles.shape[0], bytes_accessed=14 * MIB, transcendentals=0
        ),
        name="assemble_separator",
    )(place, time_diag, tiles, prior)


def rows_kernel(place, rho, tail, early, reached, assembled, gain_row, gain_column, reduced, coupling, mine, split_b):
    size, head = early.shape
    own = place[0]
    tail_parts = halves(tail[...])
    lower = early[head:, :]
    split_b[0], split_b[1] = halves(reached[...])
    mine[head:, :head] = -product(tail_parts, halves(lower), NN)
    mine[head:, head:] = tail[...]
    bottom = halves(mine[head:, :])
    mine[:head, :] = -product(halves(lower), bottom, TN)
    mine[:head, :head] += early[:head, :]
    own_columns = pl.ds(pl.multiple_of(own * size, size), size)
    other_columns = pl.ds(pl.multiple_of((1 - own) * size, size), size)
    own_gain = gain_row[:, own_columns]
    other_gain = gain_row[:, other_columns]
    kept, sent = rho[1] * rho[1], rho[0] * rho[1]
    rows = 256
    for first in range(0, size, rows):
        here = slice(first, first + rows)
        part = mine[here, :] * gain_column[here, :]
        here_own = part * own_gain
        here_other = -product(halves(part), (split_b[0], split_b[1]), NN) * other_gain
        for columns, schur in ((own_columns, here_own), (other_columns, here_other)):
            reduced[here, columns] = assembled[here, columns] - kept * schur
            coupling[here, columns] = -sent * schur


def own_rows(place, rho, tail, early, reached, assembled, gain_row, gain_column):
    size = early.shape[0]
    out = jax.ShapeDtypeStruct(assembled.shape, F32)
    smem = pl.BlockSpec(memory_space=pltpu.SMEM)
    vmem = pl.BlockSpec(memory_space=pltpu.VMEM)
    return pl.pallas_call(
        rows_kernel,
        out_shape=(out, out),
        in_specs=[smem] * 2 + [vmem] * 6,
        out_specs=(vmem, vmem),
        scratch_shapes=[pltpu.VMEM((size, size), F32), pltpu.VMEM((2, size, size), BF16)],
        compiler_params=pltpu.CompilerParams(vmem_limit_bytes=44 * MIB),
        cost_estimate=pl.CostEstimate(flops=20 * size**3, bytes_accessed=24 * MIB, transcendentals=0),
        name="own_rows",
    )(place, rho, tail, early, reached, assembled, gain_row, gain_column)


def next_kernel(
    place, scalars, inverse_1, inverse_0, early_0, early_1, prior, gain_row, gain_column, reduced_in,
    reduced, factor, split_p, split_t, split_l, last,
):
    size, head = early_0.shape
    own = place[0]
    weight, scale = scalars[0] * scalars[0], scalars[2]
    rows = 256

    def both(inverse, early, transposed):
        columns = slice(0, size) if transposed else slice(size, 2 * size)
        split_p[0], split_p[1] = halves(inverse[...])
        split_t[0], split_t[1] = halves(scale * prior[:, columns])
        for first in range(0, size, rows):
            here = slice(first, first + rows)
            if transposed:
                part = product((split_t[0, :, here], split_t[1, :, here]), (split_p[0], split_p[1]), TN)
            else:
                part = product((split_t[0, here], split_t[1, here]), (split_p[0], split_p[1]), NN)
            split_l[0, here], split_l[1, here] = halves(part)
            if first + rows > head:
                skip = max(head - first, 0)
                last[first + skip - head : first + rows - head, :] = part[skip:]
        upper = (split_l[0, :head], split_l[1, :head])
        lower = early[head:, :]
        middle = product(halves(early[:head, :]), upper, NN)
        last[...] -= product(halves(lower), upper, NN)
        eye = lax.broadcasted_iota(jnp.int32, (size - head, size - head), 0) == lax.broadcasted_iota(
            jnp.int32, (size - head, size - head), 1
        )
        gain_0, gain_1 = gain_row[:, :size], gain_row[:, size:]
        factor[:, :head] = -lower * gain_0[:, :head]
        factor[:, head:size] = jnp.where(eye, 1.0, 0.0) * gain_0[:, head:]
        factor[:, size:] = -last[...] * gain_1
        if transposed:
            reduced[:, :head] = reduced_in[:, :head] + weight * middle.T * gain_column[...] * gain_0[:, :head]
            reduced[:, head:size] = reduced_in[:, head:size]
            middle_parts = halves(middle)
            for first in range(0, size, rows):
                here = slice(first, first + rows)
                term = inverse[here, :] + product(
                    (split_l[0, :head, here], split_l[1, :head, here]), middle_parts, TN
                )
                reduced[here, size:] = reduced_in[here, size:] - weight * term * gain_column[here, :] * gain_1
        else:
            top = weight * gain_column[:head, :]
            reduced[:head, :head] = reduced_in[:head, :head] - top * early[:head, :] * gain_0[:, :head]
            reduced[:head, head:size] = reduced_in[:head, head:size]
            reduced[:head, size:] = reduced_in[:head, size:] + top * middle * gain_1
            reduced[head:, :] = reduced_in[head:, :]

    @pl.when(own == 0)
    def _():
        both(inverse_0, early_0, False)

    @pl.when(own == 1)
    def _():
        both(inverse_1, early_1, True)


def next_rows(place, scalars, inverse_1, inverse_0, early_0, early_1, prior, gain_row, gain_column, reduced):
    size, head = early_0.shape
    smem = pl.BlockSpec(memory_space=pltpu.SMEM)
    vmem = pl.BlockSpec(memory_space=pltpu.VMEM)
    return pl.pallas_call(
        next_kernel,
        out_shape=(
            jax.ShapeDtypeStruct(prior.shape, F32),
            jax.ShapeDtypeStruct((size - head, 2 * size), F32),
        ),
        in_specs=[smem] * 2 + [vmem] * 8,
        out_specs=(vmem, vmem),
        scratch_shapes=[pltpu.VMEM((2, size, size), BF16)] * 3 + [pltpu.VMEM((size - head, size), F32)],
        compiler_params=pltpu.CompilerParams(vmem_limit_bytes=48 * MIB),
        cost_estimate=pl.CostEstimate(flops=20 * size**3, bytes_accessed=24 * MIB, transcendentals=0),
        name="next_rows",
    )(place, scalars, inverse_1, inverse_0, early_0, early_1, prior, gain_row, gain_column, reduced)


def last_kernel(place, scalars, tail_0, tail_1, factor, reduced_in, reduced, split):
    size = reduced.shape[0]
    own = place[0]
    weight = scalars[0] * scalars[0]
    own_columns = pl.ds(pl.multiple_of(own * size, size), size)
    split[0], split[1] = halves(factor[...])
    tail = jnp.where(own == 0, tail_0[...], tail_1[...])
    solved = halves(product(halves(tail), halves(factor[:, own_columns]), NN))
    rows = 256
    for first in range(0, size, rows):
        here = slice(first, first + rows)
        part = product((solved[0][:, here], solved[1][:, here]), (split[0], split[1]), TN)
        reduced[here, :] = reduced_in[here, :] - weight * part


def last_rows(place, scalars, tail_0, tail_1, factor, reduced):
    smem = pl.BlockSpec(memory_space=pltpu.SMEM)
    vmem = pl.BlockSpec(memory_space=pltpu.VMEM)
    return pl.pallas_call(
        last_kernel,
        out_shape=jax.ShapeDtypeStruct(reduced.shape, F32),
        in_specs=[smem] * 2 + [vmem] * 4,
        out_specs=vmem,
        scratch_shapes=[pltpu.VMEM((2, *factor.shape), BF16)],
        compiler_params=pltpu.CompilerParams(vmem_limit_bytes=44 * MIB),
        cost_estimate=pl.CostEstimate(
            flops=6 * reduced.size * factor.shape[0], bytes_accessed=12 * MIB, transcendentals=0
        ),
        name="last_rows",
    )(place, scalars, tail_0, tail_1, factor, reduced)


def from_next(x):
    count = lax.axis_size("tm")
    return lax.ppermute(x, "tm", [(i, i - 1) for i in range(1, count)])


def from_other(x):
    return lax.ppermute(x, "tile", [(0, 1), (1, 0)])


def to_partitions(x):
    return lax.all_to_all(x, "tm", split_axis=0, concat_axis=0, tiled=True).reshape(-1, x.shape[-1])


def from_next_core(x, core):
    count = lax.axis_size("tm")
    pairs = [(2 * i + core, 2 * (i - 1) + core) for i in range(1, count)]
    return lax.ppermute(x, ("tm", "tile"), pairs)


def across(x, core):
    return lax.ppermute(x, "tile", [(core, 1 - core)])


def after(x, *others):
    return lax.optimization_barrier((x, *others))[0]


def on_device(prior, node_gain, time_diag, rho, values, weights, steps):
    size, nodes = prior.shape
    head = size // 2
    own = lax.axis_index("tile")
    place = own.reshape(1).astype(jnp.int32)
    interior, separator = reorder(steps[0, 0], weights[0].T, values[0])
    scalars = from_next(jnp.concatenate([rho, time_diag]))
    gain_row = node_gain.reshape(1, nodes)
    gain_column = lax.dynamic_slice_in_dim(node_gain, own * size, size).reshape(size, 1)
    interior = to_partitions(interior)
    interior, separator, scalars, gain_row, gain_column = lax.optimization_barrier(
        (interior, separator, scalars, gain_row, gain_column)
    )
    separator = to_partitions(separator)
    block, own_inverse, own_log = invert_own(place, time_diag, interior, prior)
    other_inverse = from_other(own_inverse)
    next_inverse_1 = from_next_core(own_inverse, 1)
    assembled = assemble_separator(place, time_diag, after(separator, own_log), prior)
    other_inverse = after(other_inverse, assembled)
    reached, early, rest, head_log = invert_head(place, time_diag, other_inverse, block, prior, head)
    next_early_0 = from_next_core(early, 0)
    next_inverse_1 = after(next_inverse_1, head_log)
    next_inverse_0 = across(next_inverse_1, 1)
    tail, tail_log = invert_tail(after(rest, next_inverse_1))
    log = jnp.where(own == 0, own_log, head_log + tail_log).reshape(1)
    other_log = from_other(log)
    next_tail_0 = from_next_core(tail, 0)
    next_early_1 = across(next_early_0, 0)
    tail = after(tail, next_early_0)
    reduced, coupling = own_rows(place, rho, tail, early, reached, assembled, gain_row, gain_column)
    reduced = after(reduced, other_log)
    reduced, factor = next_rows(
        place, scalars, next_inverse_1, next_inverse_0, next_early_0, next_early_1, prior, gain_row, gain_column, reduced
    )
    next_tail_1 = across(next_tail_0, 0)
    reduced = last_rows(place, scalars, next_tail_0, next_tail_1, factor, reduced)
    interior_logdet = (log + other_log) / nodes
    return reduced[None], coupling[None], interior_logdet


def solution(mesh):
    in_specs = (
        P("tile", None),
        P(),
        P("tm"),
        P("tm"),
        P("tile", "tm", None, None),
        P("tile", "tm", None),
        P("tile", "tm", None),
    )
    out_specs = (P("tm", "tile", None), P("tm", "tile", None), P("tm"))
    return jax.shard_map(on_device, mesh=mesh, in_specs=in_specs, out_specs=out_specs, check_vma=False)
```

```python
import functools

import jax
import jax.numpy as jnp
from jax import lax
from jax.experimental import pallas as pl
from jax.experimental.pallas import tpu as pltpu
from jax.sharding import PartitionSpec as P

F32, BF16 = jnp.float32, jnp.bfloat16
BASE = 128
MIB = 1 << 20
SMEM = pl.BlockSpec(memory_space=pltpu.SMEM)
VMEM = pl.BlockSpec(memory_space=pltpu.VMEM)
ANY = pl.BlockSpec(memory_space=pl.ANY)
HBM = pl.BlockSpec(memory_space=pltpu.HBM)
NN = (((1,), (0,)), ((), ()))
NT = (((1,), (1,)), ((), ()))
TN = (((0,), (0,)), ((), ()))


def halves(x):
    high = x.astype(BF16)
    return high, (x - high.astype(F32)).astype(BF16)


def product(a, b, dims):
    dot = functools.partial(lax.dot_general, dimension_numbers=dims, preferred_element_type=F32)
    return dot(a[0], b[0]) + (dot(a[0], b[1]) + dot(a[1], b[0]))


def reorder_kernel(steps, weights_t, values, interior, separator, held, in_sems, out_sems):
    tiles = held.shape[0]
    chunks = in_sems.shape[0]
    per = tiles // chunks
    for chunk in range(chunks):
        rows = pl.ds(chunk * per, per)
        pltpu.make_async_copy(values.at[rows], held.at[rows], in_sems.at[chunk]).start()
    root = jnp.sqrt(weights_t[...])
    for chunk in range(chunks):
        rows = pl.ds(chunk * per, per)
        pltpu.make_async_copy(values.at[rows], held.at[rows], in_sems.at[chunk]).wait()
        for tile in range(chunk * per, (chunk + 1) * per):
            held[tile] = held[tile] * root[:, tile : tile + 1]
            step = steps[tile]
            partition = lax.shift_right_logical(step, 1)
            odd = lax.bitwise_and(step, 1)

            @pl.when(odd == 0)
            def _():
                pltpu.make_async_copy(held.at[tile], interior.at[partition], out_sems.at[0]).start()

            @pl.when(odd == 1)
            def _():
                pltpu.make_async_copy(held.at[tile], separator.at[partition], out_sems.at[1]).start()

    half = pl.ds(0, tiles // 2)
    pltpu.make_async_copy(held.at[half], interior, out_sems.at[0]).wait()
    pltpu.make_async_copy(held.at[half], separator, out_sems.at[1]).wait()


def reorder(steps, weights_t, values):
    tiles, rows, cols = values.shape
    half = jax.ShapeDtypeStruct((tiles // 2, rows, cols), F32)
    return pl.pallas_call(
        reorder_kernel,
        out_shape=(half, half),
        in_specs=[SMEM, VMEM, ANY],
        out_specs=(HBM, HBM),
        scratch_shapes=[
            pltpu.VMEM((tiles, rows, cols), F32),
            pltpu.SemaphoreType.DMA((8,)),
            pltpu.SemaphoreType.DMA((2,)),
        ],
        compiler_params=pltpu.CompilerParams(vmem_limit_bytes=60 * MIB),
        name="reorder",
    )(steps, weights_t, values)


def wide(x):
    return jnp.broadcast_to(x, (8, BASE))


def sweep_small(entries, size):
    at = lambda i, j: (min(i, j), max(i, j))
    dets = []
    for p in range(0, size, 2):
        a, b, d = entries[p, p], entries[p, p + 1], entries[p + 1, p + 1]
        det = a * d - b * b
        dets.append(det)
        scale = 1.0 / det
        inv_a, inv_b, inv_d = d * scale, b * scale, a * scale
        others = [i for i in range(size) if i not in (p, p + 1)]
        u = {i: entries[at(i, p)] for i in others}
        v = {i: entries[at(i, p + 1)] for i in others}
        new_u = {i: inv_a * u[i] - inv_b * v[i] for i in others}
        new_v = {i: inv_d * v[i] - inv_b * u[i] for i in others}
        for i in others:
            for j in others:
                if i <= j:
                    entries[i, j] = entries[i, j] - u[i] * new_u[j] - v[i] * new_v[j]
        for i in others:
            entries[at(i, p)] = new_u[i]
            entries[at(i, p + 1)] = new_v[i]
        entries[p, p], entries[p, p + 1], entries[p + 1, p + 1] = -inv_a, inv_b, -inv_d
    return dets


def sweep_base(x):
    lane = lax.broadcasted_iota(jnp.int32, (8, BASE), 1)
    sub = lax.broadcasted_iota(jnp.int32, (8, BASE), 0)
    x = list(x)
    groups = len(x)
    dets = jnp.ones((8, BASE), F32)
    for q in range(groups):
        panel = x[q]
        inside = (lane // 8) == q
        first = 8 * q
        entries = {
            (i, j): wide(panel[i : i + 1, first + j : first + j + 1])
            for i in range(8)
            for j in range(i, 8)
        }
        marked = jnp.where(inside, jnp.where(lane == first + sub, -1.0, 0.0), panel)
        rows = [wide(marked[j : j + 1, :]) for j in range(8)]
        for at, det in enumerate(sweep_small(entries, 8)):
            dets = jnp.where(lane == 4 * q + at, det, dets)
        new_rows = []
        for i in range(8):
            total = entries[0, i] * rows[0]
            for j in range(1, 8):
                total = total + entries[min(i, j), max(i, j)] * rows[j]
            new_rows.append(total)
        new_panel = new_rows[7]
        for i in range(7):
            new_panel = jnp.where(sub == i, new_rows[i], new_panel)
        for i in [(q + d) % groups for d in range(1, groups)]:
            total = jnp.where(inside, 0.0, x[i])
            for j in range(8):
                total = total + wide(x[i][:, first + j : first + j + 1]) * new_rows[j]
            x[i] = total
        x[q] = -new_panel
    return x, dets


def unit_scales(m, size):
    eye = lax.broadcasted_iota(jnp.int32, (BASE, BASE), 0) == lax.broadcasted_iota(
        jnp.int32, (BASE, BASE), 1
    )
    columns, rows = [], []
    for k in range(size // BASE):
        here = pl.ds(k * BASE, BASE)
        diagonal = jnp.where(eye, m[here, here], 0.0)
        columns.append(lax.rsqrt(jnp.sum(diagonal, axis=1, keepdims=True)))
        rows.append(lax.rsqrt(jnp.sum(diagonal, axis=0, keepdims=True)))
    return columns, jnp.concatenate(rows, axis=1)


def invert(m, panel, left, right, size, pivots):
    def step(k, logs):
        here = pl.ds(pl.multiple_of(k * BASE, BASE), BASE)
        groups = [
            m[pl.ds(pl.multiple_of(k * BASE + 8 * q, 8), 8), here] for q in range(BASE // 8)
        ]
        swept, dets = sweep_base(groups)
        swept = jnp.concatenate(swept, axis=0)
        inverse = halves(-swept)
        panel[...] = product(inverse, halves(m[here, :]), NN)
        panel[:, here] = swept
        high, low = halves(panel[...])
        right[0, :BASE], right[0, BASE:] = high, high
        right[1, :BASE], right[1, BASE:] = low, low
        high, low = halves(m[:, here])
        left[:, :BASE], left[:, BASE:] = high, low
        m[:, here] = jnp.zeros((size, BASE), F32)
        rows = 256 if size % 256 == 0 else BASE
        for first in range(0, size, rows):
            part = left[first : first + rows, :]
            dot = functools.partial(lax.dot_general, dimension_numbers=NN, preferred_element_type=F32)
            m[first : first + rows, :] -= dot(part, right[0]) + dot(part, right[1])
        m[here, :] = panel[...]
        return logs + jnp.log(dets[0:1, :])

    logs = lax.fori_loop(0, pivots // BASE, step, jnp.zeros((1, BASE), F32))
    return jnp.sum(logs, axis=1, keepdims=True)


def begin(source, target, sem):
    copy = pltpu.make_async_copy(source, target, sem)
    copy.start()
    return copy


def own_kernel(
    place, time_diag, tiles_in, prior_in, block_out, inverse_out, logdet,
    tiles, prior, block, inverse, split, panel, left, right, sems,
):
    size = block.shape[0]
    scale = time_diag[0]
    columns = pl.ds(pl.multiple_of(place[0] * size, size), size)
    depth = tiles.shape[0]
    per = depth // 4
    tile_copies = [
        begin(tiles_in.at[pl.ds(c * per, per)], tiles.at[pl.ds(c * per, per)], sems.at[c]) for c in range(4)
    ]
    prior_copy = begin(prior_in.at[:, columns], prior, sems.at[4])
    for c, copy in enumerate(tile_copies):
        copy.wait()
        here = slice(c * per, (c + 1) * per)
        split[0, here], split[1, here] = halves(tiles[here])
    prior_copy.wait()
    rows = 256
    for first in range(0, size, rows):
        here = slice(first, first + rows)
        gram = product((split[0, :, here], split[1, :, here]), (split[0], split[1]), TN)
        block[here, :] = scale * prior[here, :] + gram
    block_copy = begin(block, block_out, sems.at[0])
    by_row, by_column = unit_scales(block, size)
    for k, row_scale in enumerate(by_row):
        here = pl.ds(k * BASE, BASE)
        inverse[here, :] = block[here, :] * row_scale * by_column
    log_total = invert(inverse, panel, left, right, size, size)
    logdet[...] = log_total - 2.0 * jnp.sum(jnp.log(by_column), axis=1, keepdims=True)
    copies = []
    for k, row_scale in enumerate(by_row):
        here = pl.ds(k * BASE, BASE)
        inverse[here, :] = inverse[here, :] * (-row_scale) * by_column
        copies.append(begin(inverse.at[here], inverse_out.at[here], sems.at[1 + k]))
    for copy in copies + [block_copy]:
        copy.wait()


def scratch_of(size):
    return [
        pltpu.VMEM((BASE, size), F32),
        pltpu.VMEM((size, 2 * BASE), BF16),
        pltpu.VMEM((2, 2 * BASE, size), BF16),
    ]


def shape(*dims):
    return jax.ShapeDtypeStruct(dims, F32)


def invert_own(place, time_diag, tiles, prior):
    size = prior.shape[0]
    return pl.pallas_call(
        own_kernel,
        out_shape=(shape(size, size), shape(size, size), shape(1, 1)),
        in_specs=[SMEM, SMEM, ANY, ANY],
        out_specs=(HBM, HBM, VMEM),
        scratch_shapes=[
            pltpu.VMEM(tiles.shape, F32),
            pltpu.VMEM((size, size), F32),
            pltpu.VMEM((size, size), F32),
            pltpu.VMEM((size, size), F32),
            pltpu.VMEM((2, *tiles.shape), BF16),
        ]
        + scratch_of(size)
        + [pltpu.SemaphoreType.DMA((1 + size // BASE,))],
        compiler_params=pltpu.CompilerParams(vmem_limit_bytes=54 * MIB),
        cost_estimate=pl.CostEstimate(flops=120 * size**3, bytes_accessed=16 * MIB, transcendentals=0),
        name="invert_own",
    )(place, time_diag, tiles, prior)


def head_kernel(
    place, time_diag, other_in, block_in, prior_in, reached_out, early, rest, logdet,
    other_inverse, block, prior, reached, work, split_a, split_b, panel, left, right, sems,
):
    size = block.shape[0]
    head = early.shape[1]
    scale = time_diag[0]
    other_columns = pl.ds(pl.multiple_of((1 - place[0]) * size, size), size)
    copies = [
        begin(prior_in.at[:, other_columns], prior, sems.at[0]),
        begin(other_in, other_inverse, sems.at[1]),
        begin(block_in, block, sems.at[2]),
    ]
    copies[0].wait()
    split_a[0], split_a[1] = halves(scale * prior[...])
    copies[1].wait()
    split_b[0], split_b[1] = halves(other_inverse[...])
    copies[2].wait()
    rows = 256
    for first in range(0, size, rows):
        here = slice(first, first + rows)
        reached[here, :] = product((split_a[0, here], split_a[1, here]), (split_b[0], split_b[1]), NN)
        part = halves(reached[here, :])
        work[here, :] = block[here, :] - product(part, (split_a[0], split_a[1]), NT)
    reached_copy = begin(reached, reached_out, sems.at[0])
    by_row, by_column = unit_scales(work, size)
    for k, row_scale in enumerate(by_row):
        here = pl.ds(k * BASE, BASE)
        work[here, :] = work[here, :] * row_scale * by_column
    log_total = invert(work, panel, left, right, size, head)
    by_head = by_column[:, :head]
    logdet[...] = log_total - 2.0 * jnp.sum(jnp.log(by_head), axis=1, keepdims=True)
    back = 1.0 / by_column[:, head:]
    for k, row_scale in enumerate(by_row):
        here = pl.ds(k * BASE, BASE)
        if k * BASE < head:
            early[here, :] = work[here, :head] * (-row_scale) * by_head
        else:
            row_back = 1.0 / row_scale
            early[here, :] = work[here, :head] * row_back * by_head
            rest[pl.ds(k * BASE - head, BASE), :] = work[here, head:] * row_back * back
    reached_copy.wait()


def invert_head(place, time_diag, other_inverse, block, prior, head):
    size = prior.shape[0]
    return pl.pallas_call(
        head_kernel,
        out_shape=(shape(size, size), shape(size, head), shape(size - head, size - head), shape(1, 1)),
        in_specs=[SMEM, SMEM] + [ANY] * 3,
        out_specs=(HBM, VMEM, VMEM, VMEM),
        scratch_shapes=[pltpu.VMEM((size, size), F32)] * 5
        + [pltpu.VMEM((2, size, size), BF16)] * 2
        + scratch_of(size)
        + [pltpu.SemaphoreType.DMA((3,))],
        compiler_params=pltpu.CompilerParams(vmem_limit_bytes=60 * MIB),
        cost_estimate=pl.CostEstimate(flops=120 * size**3, bytes_accessed=16 * MIB, transcendentals=0),
        name="invert_head",
    )(place, time_diag, other_inverse, block, prior)


def tail_kernel(rest, inverse, logdet, panel, left, right):
    size = rest.shape[0]
    by_row, by_column = unit_scales(rest, size)
    for k, row_scale in enumerate(by_row):
        here = pl.ds(k * BASE, BASE)
        inverse[here, :] = rest[here, :] * row_scale * by_column
    log_total = invert(inverse, panel, left, right, size, size)
    logdet[...] = log_total - 2.0 * jnp.sum(jnp.log(by_column), axis=1, keepdims=True)
    for k, row_scale in enumerate(by_row):
        here = pl.ds(k * BASE, BASE)
        inverse[here, :] = inverse[here, :] * (-row_scale) * by_column


def invert_tail(rest):
    size = rest.shape[0]
    vmem = pl.BlockSpec(memory_space=pltpu.VMEM)
    return pl.pallas_call(
        tail_kernel,
        out_shape=(jax.ShapeDtypeStruct(rest.shape, F32), jax.ShapeDtypeStruct((1, 1), F32)),
        in_specs=[vmem],
        out_specs=(vmem, vmem),
        scratch_shapes=scratch_of(size),
        compiler_params=pltpu.CompilerParams(vmem_limit_bytes=60 * MIB),
        cost_estimate=pl.CostEstimate(flops=100 * size**3, bytes_accessed=4 * MIB, transcendentals=0),
        name="invert_tail",
    )(rest)


def rows_kernel(
    place, rho, tail, early, reached_in, gain_row, gain_column, coupling_out,
    reached, mine, coupling, split, sems,
):
    size, head = early.shape
    own = place[0]
    reached_copy = begin(reached_in, reached, sems.at[0])
    lower = halves(early[head:, :])
    mine[head:, :head] = -product(halves(tail[...]), lower, NN)
    mine[head:, head:] = tail[...]
    mine[:head, :] = -product(lower, halves(mine[head:, :]), TN)
    mine[:head, :head] += early[:head, :]
    own_columns = pl.ds(pl.multiple_of(own * size, size), size)
    other_columns = pl.ds(pl.multiple_of((1 - own) * size, size), size)
    sent = rho[0] * rho[1]
    own_gain = -sent * gain_row[:, own_columns]
    other_gain = sent * gain_row[:, other_columns]
    reached_copy.wait()
    split[0], split[1] = halves(reached[...])
    rows = 256
    copies = []
    for first in range(0, size, rows):
        here = slice(first, first + rows)
        part = mine[here, :] * gain_column[here, :]
        coupling[here, own_columns] = part * own_gain
        coupling[here, other_columns] = product(halves(part), (split[0], split[1]), NN) * other_gain
        place_out = pl.ds(first, rows)
        copies.append(begin(coupling.at[place_out], coupling_out.at[place_out], sems.at[first // rows]))
    for copy in copies:
        copy.wait()


def own_rows(place, rho, tail, early, reached, gain_row, gain_column):
    size = early.shape[0]
    return pl.pallas_call(
        rows_kernel,
        out_shape=shape(size, 2 * size),
        in_specs=[SMEM] * 2 + [VMEM] * 2 + [ANY] + [VMEM] * 2,
        out_specs=HBM,
        scratch_shapes=[
            pltpu.VMEM((size, size), F32),
            pltpu.VMEM((size, size), F32),
            pltpu.VMEM((size, 2 * size), F32),
            pltpu.VMEM((2, size, size), BF16),
            pltpu.SemaphoreType.DMA((size // 256,)),
        ],
        compiler_params=pltpu.CompilerParams(vmem_limit_bytes=60 * MIB),
        cost_estimate=pl.CostEstimate(flops=20 * size**3, bytes_accessed=24 * MIB, transcendentals=0),
        name="own_rows",
    )(place, rho, tail, early, reached, gain_row, gain_column)


def final_kernel(
    place, rho, time_diag, scalars, tiles_in, prior_in, coupling_in, inverse_1, inverse_0, early_0, early_1,
    tail_0, tail_1, gain_row, gain_column, reduced_out,
    tiles, prior, coupling, inverse, early, tail, reduced, last, split_p, split_t, split_l, split_g, split_f, sems,
):
    size, head = early.shape
    own = place[0]
    weight, scale = scalars[0] * scalars[0], scalars[2]
    kept = rho[1] / rho[0]
    rows = 256

    @pl.when(own == 0)
    def _():
        begin(inverse_0, inverse, sems.at[0])
        begin(early_0, early, sems.at[2])
        begin(tail_0, tail, sems.at[3])

    @pl.when(own == 1)
    def _():
        begin(inverse_1, inverse, sems.at[0])
        begin(early_1, early, sems.at[2])
        begin(tail_1, tail, sems.at[3])

    prior_copy = begin(prior_in, prior, sems.at[1])
    tiles_copy = begin(tiles_in, tiles, sems.at[4])
    coupling_copy = begin(coupling_in, coupling, sems.at[5])
    pltpu.make_async_copy(inverse_0, inverse, sems.at[0]).wait()
    prior_copy.wait()
    split_p[0], split_p[1] = halves(inverse[...])
    pltpu.make_async_copy(early_0, early, sems.at[2]).wait()
    pltpu.make_async_copy(tail_0, tail, sems.at[3]).wait()
    gain_0, gain_1 = gain_row[:, :size], gain_row[:, size:]

    def next_part(second):
        columns = slice(0, size) if second else slice(size, 2 * size)
        split_t[0], split_t[1] = halves(scale * prior[:, columns])
        for first in range(0, size, rows):
            here = slice(first, first + rows)
            if second:
                part = product((split_t[0, :, here], split_t[1, :, here]), (split_p[0], split_p[1]), TN)
            else:
                part = product((split_t[0, here], split_t[1, here]), (split_p[0], split_p[1]), NN)
            split_l[0, here], split_l[1, here] = halves(part)
            if first + rows > head:
                skip = max(head - first, 0)
                last[first + skip - head : first + rows - head, :] = part[skip:]
        upper = (split_l[0, :head], split_l[1, :head])
        middle = product(halves(early[:head, :]), upper, NN)
        last[...] -= product(halves(early[head:, :]), upper, NN)
        if second:
            reduced[:, :head] = weight * middle.T * gain_column[...] * gain_0[:, :head]
            reduced[:, head:size] = jnp.zeros((size, size - head), F32)
            middle_parts = halves(middle)
            for first in range(0, size, rows):
                here = slice(first, first + rows)
                term = inverse[here, :] + product(
                    (split_l[0, :head, here], split_l[1, :head, here]), middle_parts, TN
                )
                reduced[here, size:] = term * (-weight * gain_column[here, :]) * gain_1
        else:
            top = weight * gain_column[:head, :]
            reduced[:head, :head] = early[:head, :] * -top * gain_0[:, :head]
            reduced[:head, head:size] = jnp.zeros((head, size - head), F32)
            reduced[:head, size:] = top * middle * gain_1
            reduced[head:, :] = jnp.zeros((size - head, 2 * size), F32)

    @pl.when(own == 0)
    def _():
        next_part(False)

    @pl.when(own == 1)
    def _():
        next_part(True)

    own_columns = pl.ds(pl.multiple_of(own * size, size), size)
    other_columns = pl.ds(pl.multiple_of((1 - own) * size, size), size)
    below = size - head
    eye = lax.broadcasted_iota(jnp.int32, (below, below), 0) == lax.broadcasted_iota(jnp.int32, (below, below), 1)
    split_f[0, :, :head], split_f[1, :, :head] = halves(-early[head:, :] * gain_0[:, :head])
    split_f[0, :, head:size], split_f[1, :, head:size] = halves(jnp.where(eye, 1.0, 0.0) * gain_0[:, head:])
    split_f[0, :, size:], split_f[1, :, size:] = halves(-last[...] * gain_1)
    mine = (split_f[0, :, own_columns], split_f[1, :, own_columns])
    solved = halves(-weight * product(halves(tail[...]), mine, NN))
    tiles_copy.wait()
    split_g[0], split_g[1] = halves(tiles[...])
    coupling_copy.wait()
    copies = []
    for first in range(0, size, rows):
        here = slice(first, first + rows)
        reduced[here, :] += product((solved[0][:, here], solved[1][:, here]), (split_f[0], split_f[1]), TN)
        gram = product((split_g[0, :, here], split_g[1, :, here]), (split_g[0], split_g[1]), TN)
        for columns, term in ((own_columns, gram), (other_columns, 0.0)):
            reduced[here, columns] += time_diag[1] * prior[here, columns] + term + kept * coupling[here, columns]
        place_out = pl.ds(first, rows)
        copies.append(begin(reduced.at[place_out], reduced_out.at[place_out], sems.at[first // rows]))
    for copy in copies:
        copy.wait()


def final_rows(place, rho, time_diag, scalars, tiles, prior, coupling, inverses, earlies, tails, gain_row, gain_column):
    size, head = earlies[0].shape
    below = size - head
    return pl.pallas_call(
        final_kernel,
        out_shape=shape(size, 2 * size),
        in_specs=[SMEM] * 4 + [ANY] * 9 + [VMEM] * 2,
        out_specs=HBM,
        scratch_shapes=[
            pltpu.VMEM(tiles.shape, F32),
            pltpu.VMEM((size, 2 * size), F32),
            pltpu.VMEM((size, 2 * size), F32),
            pltpu.VMEM((size, size), F32),
            pltpu.VMEM((size, head), F32),
            pltpu.VMEM((below, below), F32),
            pltpu.VMEM((size, 2 * size), F32),
            pltpu.VMEM((below, size), F32),
            pltpu.VMEM((2, size, size), BF16),
            pltpu.VMEM((2, size, size), BF16),
            pltpu.VMEM((2, size, size), BF16),
            pltpu.VMEM((2, *tiles.shape), BF16),
            pltpu.VMEM((2, below, 2 * size), BF16),
            pltpu.SemaphoreType.DMA((6,)),
        ],
        compiler_params=pltpu.CompilerParams(vmem_limit_bytes=60 * MIB),
        cost_estimate=pl.CostEstimate(flops=30 * size**3, bytes_accessed=32 * MIB, transcendentals=0),
        name="final_rows",
    )(place, rho, time_diag, scalars, tiles, prior, coupling, *inverses, *earlies, *tails, gain_row, gain_column)


def from_next(x):
    count = lax.axis_size("tm")
    return lax.ppermute(x, "tm", [(i, i - 1) for i in range(1, count)])


def from_other(x):
    return lax.ppermute(x, "tile", [(0, 1), (1, 0)])


def to_partitions(x):
    return lax.all_to_all(x, "tm", split_axis=0, concat_axis=0, tiled=True).reshape(-1, x.shape[-1])


def from_next_core(x, core):
    count = lax.axis_size("tm")
    pairs = [(2 * i + core, 2 * (i - 1) + core) for i in range(1, count)]
    return lax.ppermute(x, ("tm", "tile"), pairs)


def across(x, core):
    return lax.ppermute(x, "tile", [(core, 1 - core)])


def after(x, *others):
    return lax.optimization_barrier((x, *others))[0]


def on_device(prior, node_gain, time_diag, rho, values, weights, steps):
    size, nodes = prior.shape
    head = size // 2
    own = lax.axis_index("tile")
    place = own.reshape(1).astype(jnp.int32)
    interior, separator = reorder(steps[0, 0], weights[0].T, values[0])
    scalars = from_next(jnp.concatenate([rho, time_diag]))
    gain_row = node_gain.reshape(1, nodes)
    gain_column = lax.dynamic_slice_in_dim(node_gain, own * size, size).reshape(size, 1)
    interior = to_partitions(interior)
    interior, scalars, gain_row, gain_column = lax.optimization_barrier((interior, scalars, gain_row, gain_column))
    block, own_inverse, own_log = invert_own(place, time_diag, interior, prior)
    other_inverse = from_other(own_inverse)
    separator = to_partitions(after(separator, own_log))
    next_inverse_1 = from_next_core(own_inverse, 1)
    reached, early, rest, head_log = invert_head(place, time_diag, other_inverse, block, prior, head)
    next_early_0 = from_next_core(early, 0)
    next_inverse_1 = after(next_inverse_1, head_log)
    next_inverse_0 = across(next_inverse_1, 1)
    tail, tail_log = invert_tail(after(rest, next_inverse_1))
    log = jnp.where(own == 0, own_log, head_log + tail_log).reshape(1)
    other_log = from_other(log)
    next_tail_0 = from_next_core(tail, 0)
    tail = after(tail, next_early_0, separator)
    next_early_1 = across(next_early_0, 0)
    coupling = own_rows(place, rho, tail, early, reached, gain_row, gain_column)
    next_tail_0, coupling = lax.optimization_barrier((next_tail_0, coupling))
    next_tail_1 = across(next_tail_0, 0)
    coupling_read = after(coupling, other_log)
    reduced = final_rows(
        place, rho, time_diag, scalars, separator, prior, coupling_read,
        (next_inverse_1, next_inverse_0), (next_early_0, next_early_1), (next_tail_0, next_tail_1),
        gain_row, gain_column,
    )
    interior_logdet = (log + other_log) / nodes
    return reduced[None], coupling[None], interior_logdet


def solution(mesh):
    in_specs = (
        P("tile", None),
        P(),
        P("tm"),
        P("tm"),
        P("tile", "tm", None, None),
        P("tile", "tm", None),
        P("tile", "tm", None),
    )
    out_specs = (P("tm", "tile", None), P("tm", "tile", None), P("tm"))
    return jax.shard_map(on_device, mesh=mesh, in_specs=in_specs, out_specs=out_specs, check_vma=False)
```

```python
import functools

import jax
import jax.numpy as jnp
from jax import lax
from jax.experimental import pallas as pl
from jax.experimental.pallas import tpu as pltpu
from jax.sharding import PartitionSpec as P

F32, BF16 = jnp.float32, jnp.bfloat16
BASE = 128
MIB = 1 << 20
SMEM = pl.BlockSpec(memory_space=pltpu.SMEM)
VMEM = pl.BlockSpec(memory_space=pltpu.VMEM)
ANY = pl.BlockSpec(memory_space=pl.ANY)
HBM = pl.BlockSpec(memory_space=pltpu.HBM)
NN = (((1,), (0,)), ((), ()))
NT = (((1,), (1,)), ((), ()))
TN = (((0,), (0,)), ((), ()))


def halves(x):
    high = x.astype(BF16)
    return high, (x - high.astype(F32)).astype(BF16)


def product(a, b, dims):
    dot = functools.partial(lax.dot_general, dimension_numbers=dims, preferred_element_type=F32)
    return dot(a[0], b[0]) + (dot(a[0], b[1]) + dot(a[1], b[0]))


def reorder_kernel(steps, weights_t, values, interior, separator, held, in_sems, out_sems):
    tiles = held.shape[0]
    chunks = in_sems.shape[0]
    per = tiles // chunks
    for chunk in range(chunks):
        rows = pl.ds(chunk * per, per)
        pltpu.make_async_copy(values.at[rows], held.at[rows], in_sems.at[chunk]).start()
    root = jnp.sqrt(weights_t[...])
    for chunk in range(chunks):
        rows = pl.ds(chunk * per, per)
        pltpu.make_async_copy(values.at[rows], held.at[rows], in_sems.at[chunk]).wait()
        for tile in range(chunk * per, (chunk + 1) * per):
            held[tile] = held[tile] * root[:, tile : tile + 1]
            step = steps[tile]
            partition = lax.shift_right_logical(step, 1)
            odd = lax.bitwise_and(step, 1)

            @pl.when(odd == 0)
            def _():
                pltpu.make_async_copy(held.at[tile], interior.at[partition], out_sems.at[0]).start()

            @pl.when(odd == 1)
            def _():
                pltpu.make_async_copy(held.at[tile], separator.at[partition], out_sems.at[1]).start()

    half = pl.ds(0, tiles // 2)
    pltpu.make_async_copy(held.at[half], interior, out_sems.at[0]).wait()
    pltpu.make_async_copy(held.at[half], separator, out_sems.at[1]).wait()


def reorder(steps, weights_t, values):
    tiles, rows, cols = values.shape
    half = jax.ShapeDtypeStruct((tiles // 2, rows, cols), F32)
    return pl.pallas_call(
        reorder_kernel,
        out_shape=(half, half),
        in_specs=[SMEM, VMEM, ANY],
        out_specs=(HBM, HBM),
        scratch_shapes=[
            pltpu.VMEM((tiles, rows, cols), F32),
            pltpu.SemaphoreType.DMA((8,)),
            pltpu.SemaphoreType.DMA((2,)),
        ],
        compiler_params=pltpu.CompilerParams(vmem_limit_bytes=60 * MIB),
        name="reorder",
    )(steps, weights_t, values)


def wide(x):
    return jnp.broadcast_to(x, (8, BASE))


def sweep_small(entries, size):
    at = lambda i, j: (min(i, j), max(i, j))
    dets = []
    for p in range(0, size, 2):
        a, b, d = entries[p, p], entries[p, p + 1], entries[p + 1, p + 1]
        det = a * d - b * b
        dets.append(det)
        scale = 1.0 / det
        inv_a, inv_b, inv_d = d * scale, b * scale, a * scale
        others = [i for i in range(size) if i not in (p, p + 1)]
        u = {i: entries[at(i, p)] for i in others}
        v = {i: entries[at(i, p + 1)] for i in others}
        new_u = {i: inv_a * u[i] - inv_b * v[i] for i in others}
        new_v = {i: inv_d * v[i] - inv_b * u[i] for i in others}
        for i in others:
            for j in others:
                if i <= j:
                    entries[i, j] = entries[i, j] - u[i] * new_u[j] - v[i] * new_v[j]
        for i in others:
            entries[at(i, p)] = new_u[i]
            entries[at(i, p + 1)] = new_v[i]
        entries[p, p], entries[p, p + 1], entries[p + 1, p + 1] = -inv_a, inv_b, -inv_d
    return dets


def sweep_base(x):
    lane = lax.broadcasted_iota(jnp.int32, (8, BASE), 1)
    sub = lax.broadcasted_iota(jnp.int32, (8, BASE), 0)
    x = list(x)
    groups = len(x)
    dets = jnp.ones((8, BASE), F32)
    for q in range(groups):
        panel = x[q]
        inside = (lane // 8) == q
        first = 8 * q
        entries = {
            (i, j): wide(panel[i : i + 1, first + j : first + j + 1])
            for i in range(8)
            for j in range(i, 8)
        }
        marked = jnp.where(inside, jnp.where(lane == first + sub, -1.0, 0.0), panel)
        rows = [wide(marked[j : j + 1, :]) for j in range(8)]
        for at, det in enumerate(sweep_small(entries, 8)):
            dets = jnp.where(lane == 4 * q + at, det, dets)
        new_rows = []
        for i in range(8):
            total = entries[0, i] * rows[0]
            for j in range(1, 8):
                total = total + entries[min(i, j), max(i, j)] * rows[j]
            new_rows.append(total)
        new_panel = new_rows[7]
        for i in range(7):
            new_panel = jnp.where(sub == i, new_rows[i], new_panel)
        for i in [(q + d) % groups for d in range(1, groups)]:
            total = jnp.where(inside, 0.0, x[i])
            for j in range(8):
                total = total + wide(x[i][:, first + j : first + j + 1]) * new_rows[j]
            x[i] = total
        x[q] = -new_panel
    return x, dets


def unit_scales(m, size):
    eye = lax.broadcasted_iota(jnp.int32, (BASE, BASE), 0) == lax.broadcasted_iota(
        jnp.int32, (BASE, BASE), 1
    )
    columns, rows = [], []
    for k in range(size // BASE):
        here = pl.ds(k * BASE, BASE)
        diagonal = jnp.where(eye, m[here, here], 0.0)
        columns.append(lax.rsqrt(jnp.sum(diagonal, axis=1, keepdims=True)))
        rows.append(lax.rsqrt(jnp.sum(diagonal, axis=0, keepdims=True)))
    return columns, jnp.concatenate(rows, axis=1)


def invert(m, panel, left, right, size, pivots):
    def step(k, logs):
        here = pl.ds(pl.multiple_of(k * BASE, BASE), BASE)
        groups = [
            m[pl.ds(pl.multiple_of(k * BASE + 8 * q, 8), 8), here] for q in range(BASE // 8)
        ]
        swept, dets = sweep_base(groups)
        swept = jnp.concatenate(swept, axis=0)
        inverse = halves(-swept)
        panel[...] = product(inverse, halves(m[here, :]), NN)
        panel[:, here] = swept
        high, low = halves(panel[...])
        right[0, :BASE], right[0, BASE:] = high, high
        right[1, :BASE], right[1, BASE:] = low, low
        high, low = halves(m[:, here])
        left[:, :BASE], left[:, BASE:] = high, low
        m[:, here] = jnp.zeros((size, BASE), F32)
        rows = 256 if size % 256 == 0 else BASE
        for first in range(0, size, rows):
            part = left[first : first + rows, :]
            dot = functools.partial(lax.dot_general, dimension_numbers=NN, preferred_element_type=F32)
            m[first : first + rows, :] -= dot(part, right[0]) + dot(part, right[1])
        m[here, :] = panel[...]
        return logs + jnp.log(dets[0:1, :])

    logs = lax.fori_loop(0, pivots // BASE, step, jnp.zeros((1, BASE), F32))
    return jnp.sum(logs, axis=1, keepdims=True)


def begin(source, target, sem):
    copy = pltpu.make_async_copy(source, target, sem)
    copy.start()
    return copy


def own_kernel(
    place, time_diag, tiles_in, prior_in, block_out, inverse_out, logdet,
    tiles, prior, block, inverse, split, panel, left, right, sems,
):
    size = block.shape[0]
    scale = time_diag[0]
    columns = pl.ds(pl.multiple_of(place[0] * size, size), size)
    depth = tiles.shape[0]
    per = depth // 4
    tile_copies = [
        begin(tiles_in.at[pl.ds(c * per, per)], tiles.at[pl.ds(c * per, per)], sems.at[c]) for c in range(4)
    ]
    prior_copy = begin(prior_in.at[:, columns], prior, sems.at[4])
    for c, copy in enumerate(tile_copies):
        copy.wait()
        here = slice(c * per, (c + 1) * per)
        split[0, here], split[1, here] = halves(tiles[here])
    prior_copy.wait()
    rows = 256
    for first in range(0, size, rows):
        here = slice(first, first + rows)
        gram = product((split[0, :, here], split[1, :, here]), (split[0], split[1]), TN)
        block[here, :] = scale * prior[here, :] + gram
    block_copy = begin(block, block_out, sems.at[0])
    by_row, by_column = unit_scales(block, size)
    for k, row_scale in enumerate(by_row):
        here = pl.ds(k * BASE, BASE)
        inverse[here, :] = block[here, :] * row_scale * by_column
    log_total = invert(inverse, panel, left, right, size, size)
    logdet[...] = log_total - 2.0 * jnp.sum(jnp.log(by_column), axis=1, keepdims=True)
    copies = []
    for k, row_scale in enumerate(by_row):
        here = pl.ds(k * BASE, BASE)
        inverse[here, :] = inverse[here, :] * (-row_scale) * by_column
        copies.append(begin(inverse.at[here], inverse_out.at[here], sems.at[1 + k]))
    for copy in copies + [block_copy]:
        copy.wait()


def scratch_of(size):
    return [
        pltpu.VMEM((BASE, size), F32),
        pltpu.VMEM((size, 2 * BASE), BF16),
        pltpu.VMEM((2, 2 * BASE, size), BF16),
    ]


def shape(*dims):
    return jax.ShapeDtypeStruct(dims, F32)


def invert_own(place, time_diag, tiles, prior):
    size = prior.shape[0]
    return pl.pallas_call(
        own_kernel,
        out_shape=(shape(size, size), shape(size, size), shape(1, 1)),
        in_specs=[SMEM, SMEM, ANY, ANY],
        out_specs=(HBM, HBM, VMEM),
        scratch_shapes=[
            pltpu.VMEM(tiles.shape, F32),
            pltpu.VMEM((size, size), F32),
            pltpu.VMEM((size, size), F32),
            pltpu.VMEM((size, size), F32),
            pltpu.VMEM((2, *tiles.shape), BF16),
        ]
        + scratch_of(size)
        + [pltpu.SemaphoreType.DMA((1 + size // BASE,))],
        compiler_params=pltpu.CompilerParams(vmem_limit_bytes=54 * MIB),
        cost_estimate=pl.CostEstimate(flops=120 * size**3, bytes_accessed=16 * MIB, transcendentals=0),
        name="invert_own",
    )(place, time_diag, tiles, prior)


def head_kernel(
    place, time_diag, other_in, block_in, prior_in, reached_out, early, rest, logdet,
    other_inverse, block, prior, reached, work, split_a, split_b, panel, left, right, sems,
):
    size = block.shape[0]
    head = early.shape[1]
    scale = time_diag[0]
    other_columns = pl.ds(pl.multiple_of((1 - place[0]) * size, size), size)
    copies = [
        begin(prior_in.at[:, other_columns], prior, sems.at[0]),
        begin(other_in, other_inverse, sems.at[1]),
        begin(block_in, block, sems.at[2]),
    ]
    copies[0].wait()
    split_a[0], split_a[1] = halves(scale * prior[...])
    copies[1].wait()
    split_b[0], split_b[1] = halves(other_inverse[...])
    copies[2].wait()
    rows = 256
    for first in range(0, size, rows):
        here = slice(first, first + rows)
        reached[here, :] = product((split_a[0, here], split_a[1, here]), (split_b[0], split_b[1]), NN)
        part = halves(reached[here, :])
        work[here, :] = block[here, :] - product(part, (split_a[0], split_a[1]), NT)
    reached_copy = begin(reached, reached_out, sems.at[0])
    by_row, by_column = unit_scales(work, size)
    for k, row_scale in enumerate(by_row):
        here = pl.ds(k * BASE, BASE)
        work[here, :] = work[here, :] * row_scale * by_column
    log_total = invert(work, panel, left, right, size, head)
    by_head = by_column[:, :head]
    logdet[...] = log_total - 2.0 * jnp.sum(jnp.log(by_head), axis=1, keepdims=True)
    back = 1.0 / by_column[:, head:]
    for k, row_scale in enumerate(by_row):
        here = pl.ds(k * BASE, BASE)
        if k * BASE < head:
            early[here, :] = work[here, :head] * (-row_scale) * by_head
        else:
            row_back = 1.0 / row_scale
            early[here, :] = work[here, :head] * row_back * by_head
            rest[pl.ds(k * BASE - head, BASE), :] = work[here, head:] * row_back * back
    reached_copy.wait()


def invert_head(place, time_diag, other_inverse, block, prior, head):
    size = prior.shape[0]
    return pl.pallas_call(
        head_kernel,
        out_shape=(shape(size, size), shape(size, head), shape(size - head, size - head), shape(1, 1)),
        in_specs=[SMEM, SMEM] + [ANY] * 3,
        out_specs=(HBM, VMEM, VMEM, VMEM),
        scratch_shapes=[pltpu.VMEM((size, size), F32)] * 5
        + [pltpu.VMEM((2, size, size), BF16)] * 2
        + scratch_of(size)
        + [pltpu.SemaphoreType.DMA((3,))],
        compiler_params=pltpu.CompilerParams(vmem_limit_bytes=60 * MIB),
        cost_estimate=pl.CostEstimate(flops=120 * size**3, bytes_accessed=16 * MIB, transcendentals=0),
        name="invert_head",
    )(place, time_diag, other_inverse, block, prior)


def tail_kernel(rest, inverse, logdet, panel, left, right):
    size = rest.shape[0]
    by_row, by_column = unit_scales(rest, size)
    for k, row_scale in enumerate(by_row):
        here = pl.ds(k * BASE, BASE)
        inverse[here, :] = rest[here, :] * row_scale * by_column
    log_total = invert(inverse, panel, left, right, size, size)
    logdet[...] = log_total - 2.0 * jnp.sum(jnp.log(by_column), axis=1, keepdims=True)
    for k, row_scale in enumerate(by_row):
        here = pl.ds(k * BASE, BASE)
        inverse[here, :] = inverse[here, :] * (-row_scale) * by_column


def invert_tail(rest):
    size = rest.shape[0]
    vmem = pl.BlockSpec(memory_space=pltpu.VMEM)
    return pl.pallas_call(
        tail_kernel,
        out_shape=(jax.ShapeDtypeStruct(rest.shape, F32), jax.ShapeDtypeStruct((1, 1), F32)),
        in_specs=[vmem],
        out_specs=(vmem, vmem),
        scratch_shapes=scratch_of(size),
        compiler_params=pltpu.CompilerParams(vmem_limit_bytes=60 * MIB),
        cost_estimate=pl.CostEstimate(flops=100 * size**3, bytes_accessed=4 * MIB, transcendentals=0),
        name="invert_tail",
    )(rest)


def rows_kernel(
    place, rho, tail, early, reached_in, gain_row, gain_column, coupling_out,
    reached, mine, coupling, split, sems,
):
    size, head = early.shape
    own = place[0]
    reached_copy = begin(reached_in, reached, sems.at[0])
    lower = halves(early[head:, :])
    mine[head:, :head] = -product(halves(tail[...]), lower, NN)
    mine[head:, head:] = tail[...]
    mine[:head, :] = -product(lower, halves(mine[head:, :]), TN)
    mine[:head, :head] += early[:head, :]
    own_columns = pl.ds(pl.multiple_of(own * size, size), size)
    other_columns = pl.ds(pl.multiple_of((1 - own) * size, size), size)
    sent = rho[0] * rho[1]
    own_gain = -sent * gain_row[:, own_columns]
    other_gain = sent * gain_row[:, other_columns]
    reached_copy.wait()
    split[0], split[1] = halves(reached[...])
    rows = 256
    copies = []
    for first in range(0, size, rows):
        here = slice(first, first + rows)
        part = mine[here, :] * gain_column[here, :]
        coupling[here, own_columns] = part * own_gain
        coupling[here, other_columns] = product(halves(part), (split[0], split[1]), NN) * other_gain
        place_out = pl.ds(first, rows)
        copies.append(begin(coupling.at[place_out], coupling_out.at[place_out], sems.at[first // rows]))
    for copy in copies:
        copy.wait()


def own_rows(place, rho, tail, early, reached, gain_row, gain_column):
    size = early.shape[0]
    return pl.pallas_call(
        rows_kernel,
        out_shape=shape(size, 2 * size),
        in_specs=[SMEM] * 2 + [VMEM] * 2 + [ANY] + [VMEM] * 2,
        out_specs=HBM,
        scratch_shapes=[
            pltpu.VMEM((size, size), F32),
            pltpu.VMEM((size, size), F32),
            pltpu.VMEM((size, 2 * size), F32),
            pltpu.VMEM((2, size, size), BF16),
            pltpu.SemaphoreType.DMA((size // 256,)),
        ],
        compiler_params=pltpu.CompilerParams(vmem_limit_bytes=60 * MIB),
        cost_estimate=pl.CostEstimate(flops=20 * size**3, bytes_accessed=24 * MIB, transcendentals=0),
        name="own_rows",
    )(place, rho, tail, early, reached, gain_row, gain_column)


def final_kernel(
    place, rho, time_diag, scalars, tiles_in, prior_in, coupling_in, inverse_1, inverse_0, early_0, early_1,
    tail_0, tail_1, gain_row, gain_column, reduced_out,
    tiles, prior, coupling, inverse, early, tail, reduced, last, split_p, split_t, split_l, split_g, split_f, sems,
):
    size, head = early.shape
    own = place[0]
    weight, scale = scalars[0] * scalars[0], scalars[2]
    kept = rho[1] / rho[0]
    rows = 256

    @pl.when(own == 0)
    def _():
        begin(inverse_0, inverse, sems.at[0])
        begin(early_0, early, sems.at[2])
        begin(tail_0, tail, sems.at[3])

    @pl.when(own == 1)
    def _():
        begin(inverse_1, inverse, sems.at[0])
        begin(early_1, early, sems.at[2])
        begin(tail_1, tail, sems.at[3])

    prior_copy = begin(prior_in, prior, sems.at[1])
    tiles_copy = begin(tiles_in, tiles, sems.at[4])
    coupling_copy = begin(coupling_in, coupling, sems.at[5])
    pltpu.make_async_copy(inverse_0, inverse, sems.at[0]).wait()
    prior_copy.wait()
    split_p[0], split_p[1] = halves(inverse[...])
    pltpu.make_async_copy(early_0, early, sems.at[2]).wait()
    pltpu.make_async_copy(tail_0, tail, sems.at[3]).wait()
    gain_0, gain_1 = gain_row[:, :size], gain_row[:, size:]

    def next_part(second):
        columns = slice(0, size) if second else slice(size, 2 * size)
        split_t[0], split_t[1] = halves(scale * prior[:, columns])
        for first in range(0, size, rows):
            here = slice(first, first + rows)
            if second:
                part = product((split_t[0, :, here], split_t[1, :, here]), (split_p[0], split_p[1]), TN)
            else:
                part = product((split_t[0, here], split_t[1, here]), (split_p[0], split_p[1]), NN)
            split_l[0, here], split_l[1, here] = halves(part)
            if first + rows > head:
                skip = max(head - first, 0)
                last[first + skip - head : first + rows - head, :] = part[skip:]
        upper = (split_l[0, :head], split_l[1, :head])
        middle = product(halves(early[:head, :]), upper, NN)
        last[...] -= product(halves(early[head:, :]), upper, NN)
        if second:
            reduced[:, :head] = weight * middle.T * gain_column[...] * gain_0[:, :head]
            reduced[:, head:size] = jnp.zeros((size, size - head), F32)
            middle_parts = halves(middle)
            for first in range(0, size, rows):
                here = slice(first, first + rows)
                term = inverse[here, :] + product(
                    (split_l[0, :head, here], split_l[1, :head, here]), middle_parts, TN
                )
                reduced[here, size:] = term * (-weight * gain_column[here, :]) * gain_1
        else:
            top = weight * gain_column[:head, :]
            reduced[:head, :head] = early[:head, :] * -top * gain_0[:, :head]
            reduced[:head, head:size] = jnp.zeros((head, size - head), F32)
            reduced[:head, size:] = top * middle * gain_1
            reduced[head:, :] = jnp.zeros((size - head, 2 * size), F32)

    @pl.when(own == 0)
    def _():
        next_part(False)

    @pl.when(own == 1)
    def _():
        next_part(True)

    own_columns = pl.ds(pl.multiple_of(own * size, size), size)
    other_columns = pl.ds(pl.multiple_of((1 - own) * size, size), size)
    below = size - head
    eye = lax.broadcasted_iota(jnp.int32, (below, below), 0) == lax.broadcasted_iota(jnp.int32, (below, below), 1)
    split_f[0, :, :head], split_f[1, :, :head] = halves(-early[head:, :] * gain_0[:, :head])
    split_f[0, :, head:size], split_f[1, :, head:size] = halves(jnp.where(eye, 1.0, 0.0) * gain_0[:, head:])
    split_f[0, :, size:], split_f[1, :, size:] = halves(-last[...] * gain_1)
    mine = (split_f[0, :, own_columns], split_f[1, :, own_columns])
    solved = halves(-weight * product(halves(tail[...]), mine, NN))
    tiles_copy.wait()
    split_g[0], split_g[1] = halves(tiles[...])
    coupling_copy.wait()
    copies = []
    for first in range(0, size, rows):
        here = slice(first, first + rows)
        reduced[here, :] += product((solved[0][:, here], solved[1][:, here]), (split_f[0], split_f[1]), TN)
        gram = product((split_g[0, :, here], split_g[1, :, here]), (split_g[0], split_g[1]), TN)
        for columns, term in ((own_columns, gram), (other_columns, 0.0)):
            reduced[here, columns] += time_diag[1] * prior[here, columns] + term + kept * coupling[here, columns]
        place_out = pl.ds(first, rows)
        copies.append(begin(reduced.at[place_out], reduced_out.at[place_out], sems.at[first // rows]))
    for copy in copies:
        copy.wait()


def final_rows(place, rho, time_diag, scalars, tiles, prior, coupling, inverses, earlies, tails, gain_row, gain_column):
    size, head = earlies[0].shape
    below = size - head
    return pl.pallas_call(
        final_kernel,
        out_shape=shape(size, 2 * size),
        in_specs=[SMEM] * 4 + [ANY] * 9 + [VMEM] * 2,
        out_specs=HBM,
        scratch_shapes=[
            pltpu.VMEM(tiles.shape, F32),
            pltpu.VMEM((size, 2 * size), F32),
            pltpu.VMEM((size, 2 * size), F32),
            pltpu.VMEM((size, size), F32),
            pltpu.VMEM((size, head), F32),
            pltpu.VMEM((below, below), F32),
            pltpu.VMEM((size, 2 * size), F32),
            pltpu.VMEM((below, size), F32),
            pltpu.VMEM((2, size, size), BF16),
            pltpu.VMEM((2, size, size), BF16),
            pltpu.VMEM((2, size, size), BF16),
            pltpu.VMEM((2, *tiles.shape), BF16),
            pltpu.VMEM((2, below, 2 * size), BF16),
            pltpu.SemaphoreType.DMA((6,)),
        ],
        compiler_params=pltpu.CompilerParams(vmem_limit_bytes=60 * MIB),
        cost_estimate=pl.CostEstimate(flops=30 * size**3, bytes_accessed=32 * MIB, transcendentals=0),
        name="final_rows",
    )(place, rho, time_diag, scalars, tiles, prior, coupling, *inverses, *earlies, *tails, gain_row, gain_column)


def from_next(x):
    count = lax.axis_size("tm")
    return lax.ppermute(x, "tm", [(i, i - 1) for i in range(1, count)])


def from_other(x):
    return lax.ppermute(x, "tile", [(0, 1), (1, 0)])


def to_partitions(x):
    return lax.all_to_all(x, "tm", split_axis=0, concat_axis=0, tiled=True).reshape(-1, x.shape[-1])


def from_next_core(x, core):
    count = lax.axis_size("tm")
    pairs = [(2 * i + core, 2 * (i - 1) + core) for i in range(1, count)]
    return lax.ppermute(x, ("tm", "tile"), pairs)


def across(x, core):
    return lax.ppermute(x, "tile", [(core, 1 - core)])


def after(x, *others):
    return lax.optimization_barrier((x, *others))[0]


def on_device(prior, node_gain, time_diag, rho, values, weights, steps):
    size, nodes = prior.shape
    head = size // 2
    own = lax.axis_index("tile")
    place = own.reshape(1).astype(jnp.int32)
    interior, separator = reorder(steps[0, 0], weights[0].T, values[0])
    scalars = from_next(jnp.concatenate([rho, time_diag]))
    gain_row = node_gain.reshape(1, nodes)
    gain_column = lax.dynamic_slice_in_dim(node_gain, own * size, size).reshape(size, 1)
    interior = to_partitions(interior)
    interior, scalars, gain_row, gain_column = lax.optimization_barrier((interior, scalars, gain_row, gain_column))
    block, own_inverse, own_log = invert_own(place, time_diag, interior, prior)
    other_inverse = from_other(own_inverse)
    separator = to_partitions(after(separator, own_log))
    next_inverse_1 = from_next_core(own_inverse, 1)
    reached, early, rest, head_log = invert_head(place, time_diag, other_inverse, block, prior, head)
    next_early_0 = from_next_core(early, 0)
    next_inverse_1 = after(next_inverse_1, head_log)
    next_inverse_0 = across(next_inverse_1, 1)
    tail, tail_log = invert_tail(after(rest, next_inverse_1))
    log = jnp.where(own == 0, own_log, head_log + tail_log).reshape(1)
    other_log = from_other(log)
    next_tail_0 = from_next_core(tail, 0)
    coupling = own_rows(place, rho, tail, early, reached, gain_row, gain_column)
    next_early_0, next_tail_0, coupling = lax.optimization_barrier((next_early_0, next_tail_0, coupling))
    next_early_1 = across(next_early_0, 0)
    next_tail_1 = across(next_tail_0, 0)
    coupling_read = after(coupling, other_log)
    reduced = final_rows(
        place, rho, time_diag, scalars, separator, prior, coupling_read,
        (next_inverse_1, next_inverse_0), (next_early_0, next_early_1), (next_tail_0, next_tail_1),
        gain_row, gain_column,
    )
    interior_logdet = (log + other_log) / nodes
    return reduced[None], coupling[None], interior_logdet


def solution(mesh):
    in_specs = (
        P("tile", None),
        P(),
        P("tm"),
        P("tm"),
        P("tile", "tm", None, None),
        P("tile", "tm", None),
        P("tile", "tm", None),
    )
    out_specs = (P("tm", "tile", None), P("tm", "tile", None), P("tm"))
    return jax.shard_map(on_device, mesh=mesh, in_specs=in_specs, out_specs=out_specs, check_vma=False)
```

```python
import functools

import jax
import jax.numpy as jnp
from jax import lax
from jax.experimental import pallas as pl
from jax.experimental.pallas import tpu as pltpu
from jax.sharding import PartitionSpec as P

F32, BF16 = jnp.float32, jnp.bfloat16
BASE = 128
MIB = 1 << 20
ROW_PARTS = 2
SMEM = pl.BlockSpec(memory_space=pltpu.SMEM)
VMEM = pl.BlockSpec(memory_space=pltpu.VMEM)
ANY = pl.BlockSpec(memory_space=pl.ANY)
HBM = pl.BlockSpec(memory_space=pltpu.HBM)
NN = (((1,), (0,)), ((), ()))
NT = (((1,), (1,)), ((), ()))
TN = (((0,), (0,)), ((), ()))


def halves(x):
    high = x.astype(BF16)
    return high, (x - high.astype(F32)).astype(BF16)


def product(a, b, dims):
    dot = functools.partial(lax.dot_general, dimension_numbers=dims, preferred_element_type=F32)
    return dot(a[0], b[0]) + (dot(a[0], b[1]) + dot(a[1], b[0]))


def reorder_kernel(steps, weights_t, values, interior, separator, held, in_sems, out_sems):
    tiles = held.shape[0]
    chunks = in_sems.shape[0]
    per = tiles // chunks
    for chunk in range(chunks):
        rows = pl.ds(chunk * per, per)
        pltpu.make_async_copy(values.at[rows], held.at[rows], in_sems.at[chunk]).start()
    root = jnp.sqrt(weights_t[...])
    for chunk in range(chunks):
        rows = pl.ds(chunk * per, per)
        pltpu.make_async_copy(values.at[rows], held.at[rows], in_sems.at[chunk]).wait()
        for tile in range(chunk * per, (chunk + 1) * per):
            held[tile] = held[tile] * root[:, tile : tile + 1]
            step = steps[tile]
            partition = lax.shift_right_logical(step, 1)
            odd = lax.bitwise_and(step, 1)

            @pl.when(odd == 0)
            def _():
                pltpu.make_async_copy(held.at[tile], interior.at[partition], out_sems.at[0]).start()

            @pl.when(odd == 1)
            def _():
                pltpu.make_async_copy(held.at[tile], separator.at[partition], out_sems.at[1]).start()

    half = pl.ds(0, tiles // 2)
    pltpu.make_async_copy(held.at[half], interior, out_sems.at[0]).wait()
    pltpu.make_async_copy(held.at[half], separator, out_sems.at[1]).wait()


def reorder(steps, weights_t, values):
    tiles, rows, cols = values.shape
    half = jax.ShapeDtypeStruct((tiles // 2, rows, cols), F32)
    return pl.pallas_call(
        reorder_kernel,
        out_shape=(half, half),
        in_specs=[SMEM, VMEM, ANY],
        out_specs=(HBM, HBM),
        scratch_shapes=[
            pltpu.VMEM((tiles, rows, cols), F32),
            pltpu.SemaphoreType.DMA((8,)),
            pltpu.SemaphoreType.DMA((2,)),
        ],
        compiler_params=pltpu.CompilerParams(vmem_limit_bytes=60 * MIB),
        name="reorder",
    )(steps, weights_t, values)


def wide(x):
    return jnp.broadcast_to(x, (8, BASE))


def sweep_small(entries, size):
    at = lambda i, j: (min(i, j), max(i, j))
    dets = []
    for p in range(0, size, 2):
        a, b, d = entries[p, p], entries[p, p + 1], entries[p + 1, p + 1]
        det = a * d - b * b
        dets.append(det)
        scale = 1.0 / det
        inv_a, inv_b, inv_d = d * scale, b * scale, a * scale
        others = [i for i in range(size) if i not in (p, p + 1)]
        u = {i: entries[at(i, p)] for i in others}
        v = {i: entries[at(i, p + 1)] for i in others}
        new_u = {i: inv_a * u[i] - inv_b * v[i] for i in others}
        new_v = {i: inv_d * v[i] - inv_b * u[i] for i in others}
        for i in others:
            for j in others:
                if i <= j:
                    entries[i, j] = entries[i, j] - u[i] * new_u[j] - v[i] * new_v[j]
        for i in others:
            entries[at(i, p)] = new_u[i]
            entries[at(i, p + 1)] = new_v[i]
        entries[p, p], entries[p, p + 1], entries[p + 1, p + 1] = -inv_a, inv_b, -inv_d
    return dets


def total_of(terms):
    while len(terms) > 1:
        terms = [sum(terms[i : i + 2][1:], terms[i]) for i in range(0, len(terms), 2)]
    return terms[0]


def sweep_base(x, columns, marks, beside):
    lane = lax.broadcasted_iota(jnp.int32, (8, BASE), 1)
    sub = lax.broadcasted_iota(jnp.int32, (8, BASE), 0)
    x = list(x)
    groups = len(x)
    dets = jnp.ones((8, BASE), F32)
    for q in range(groups):
        panel = x[q]
        slot = q % 2
        inside = (lane // 8) == q
        first = 8 * q
        for j in range(8):
            columns[slot, j] = wide(panel[:, first + j : first + j + 1])
        entries = {(i, j): wide(columns[slot, j, i : i + 1, :]) for i in range(8) for j in range(i, 8)}
        marks[slot] = jnp.where(inside, jnp.where(lane == first + sub, -1.0, 0.0), panel)
        rows = [wide(marks[slot, j : j + 1, :]) for j in range(8)]
        for at, det in enumerate(sweep_small(entries, 8)):
            dets = jnp.where(lane == 4 * q + at, det, dets)
        new_rows = [
            total_of([entries[min(i, j), max(i, j)] * rows[j] for j in range(8)]) for i in range(8)
        ]
        new_panel = new_rows[7]
        for i in range(7):
            new_panel = jnp.where(sub == i, new_rows[i], new_panel)
        after_this = (q + 1) % groups
        next_panel = x[after_this]
        next_panel = total_of(
            [jnp.where(inside, 0.0, next_panel)]
            + [wide(next_panel[:, first + j : first + j + 1]) * new_rows[j] for j in range(8)]
        )
        high, low = halves(panel)
        new_high, new_low = halves(new_panel)
        change = lax.dot_general(
            jnp.concatenate([high, high, low], axis=0),
            jnp.concatenate([new_high, new_low, new_high], axis=0),
            TN,
            preferred_element_type=F32,
        )
        for i in range(groups):
            x[i] = jnp.where(inside, 0.0, x[i]) + change[8 * i : 8 * i + 8]
        x[after_this] = next_panel
        x[q] = -new_panel
        for piece in beside[q::groups]:
            piece()
    return x, dets


def unit_scales(m, size):
    eye = lax.broadcasted_iota(jnp.int32, (BASE, BASE), 0) == lax.broadcasted_iota(
        jnp.int32, (BASE, BASE), 1
    )
    columns, rows = [], []
    for k in range(size // BASE):
        here = pl.ds(k * BASE, BASE)
        diagonal = jnp.where(eye, m[here, here], 0.0)
        columns.append(lax.rsqrt(jnp.sum(diagonal, axis=1, keepdims=True)))
        rows.append(lax.rsqrt(jnp.sum(diagonal, axis=0, keepdims=True)))
    return columns, jnp.concatenate(rows, axis=1)


def invert(m, panel, left, right, columns, marks, size, pivots):
    dot = functools.partial(lax.dot_general, dimension_numbers=NN, preferred_element_type=F32)
    left[...] = jnp.zeros(left.shape, BF16)
    right[...] = jnp.zeros(right.shape, BF16)

    rows, width = size // ROW_PARTS, 256 if size % 256 == 0 else BASE

    def change(at_row, at_column):
        these = slice(at_row, at_row + rows)
        part = left[these, :]
        tile = slice(at_column, at_column + width)
        m[these, tile] -= dot(part, right[0, :, tile]) + dot(part, right[1, :, tile])

    changes = [
        functools.partial(change, at_row, at_column)
        for at_column in range(0, size, width)
        for at_row in range(0, size, rows)
    ]

    def step(k, logs):
        here = pl.ds(pl.multiple_of(k * BASE, BASE), BASE)
        part = left[here, :]
        m[here, :] -= dot(part, right[0]) + dot(part, right[1])
        left[here, :] = jnp.zeros((BASE, 2 * BASE), BF16)
        groups = [m[pl.ds(pl.multiple_of(k * BASE + 8 * q, 8), 8), here] for q in range(BASE // 8)]
        swept, dets = sweep_base(groups, columns, marks, changes)
        swept = jnp.concatenate(swept, axis=0)
        panel[...] = product(halves(-swept), halves(m[here, :]), NN)
        panel[:, here] = swept
        high, low = halves(panel[...])
        right[0, :BASE], right[0, BASE:] = high, high
        right[1, :BASE], right[1, BASE:] = low, low
        high, low = halves(m[:, here])
        left[:, :BASE], left[:, BASE:] = high, low
        left[here, :] = jnp.zeros((BASE, 2 * BASE), BF16)
        m[:, here] = jnp.zeros((size, BASE), F32)
        m[here, :] = panel[...]
        return logs + jnp.log(dets[0:1, :])

    logs = lax.fori_loop(0, pivots // BASE, step, jnp.zeros((1, BASE), F32))
    for piece in changes:
        piece()
    return jnp.sum(logs, axis=1, keepdims=True)


def begin(source, target, sem):
    copy = pltpu.make_async_copy(source, target, sem)
    copy.start()
    return copy


def own_kernel(
    place, time_diag, tiles_in, prior_in, block_out, inverse_out, logdet,
    tiles, prior, block, inverse, split, panel, left, right, columns, marks, sems,
):
    size = block.shape[0]
    scale = time_diag[0]
    own_columns = pl.ds(pl.multiple_of(place[0] * size, size), size)
    depth = tiles.shape[0]
    per = depth // 4
    tile_copies = [
        begin(tiles_in.at[pl.ds(c * per, per)], tiles.at[pl.ds(c * per, per)], sems.at[c]) for c in range(4)
    ]
    prior_copy = begin(prior_in.at[:, own_columns], prior, sems.at[4])
    for c, copy in enumerate(tile_copies):
        copy.wait()
        here = slice(c * per, (c + 1) * per)
        split[0, here], split[1, here] = halves(tiles[here])
    prior_copy.wait()
    rows = 256
    for first in range(0, size, rows):
        here = slice(first, first + rows)
        gram = product((split[0, :, here], split[1, :, here]), (split[0], split[1]), TN)
        block[here, :] = scale * prior[here, :] + gram
    block_copy = begin(block, block_out, sems.at[0])
    by_row, by_column = unit_scales(block, size)
    for k, row_scale in enumerate(by_row):
        here = pl.ds(k * BASE, BASE)
        inverse[here, :] = block[here, :] * row_scale * by_column
    log_total = invert(inverse, panel, left, right, columns, marks, size, size)
    logdet[...] = log_total - 2.0 * jnp.sum(jnp.log(by_column), axis=1, keepdims=True)
    copies = []
    for k, row_scale in enumerate(by_row):
        here = pl.ds(k * BASE, BASE)
        inverse[here, :] = inverse[here, :] * (-row_scale) * by_column
        copies.append(begin(inverse.at[here], inverse_out.at[here], sems.at[1 + k]))
    for copy in copies + [block_copy]:
        copy.wait()


def scratch_of(size):
    return [
        pltpu.VMEM((BASE, size), F32),
        pltpu.VMEM((size, 2 * BASE), BF16),
        pltpu.VMEM((2, 2 * BASE, size), BF16),
        pltpu.VMEM((2, 8, 8, BASE), F32),
        pltpu.VMEM((2, 8, BASE), F32),
    ]


def shape(*dims):
    return jax.ShapeDtypeStruct(dims, F32)


def invert_own(place, time_diag, tiles, prior):
    size = prior.shape[0]
    return pl.pallas_call(
        own_kernel,
        out_shape=(shape(size, size), shape(size, size), shape(1, 1)),
        in_specs=[SMEM, SMEM, ANY, ANY],
        out_specs=(HBM, HBM, VMEM),
        scratch_shapes=[
            pltpu.VMEM(tiles.shape, F32),
            pltpu.VMEM((size, size), F32),
            pltpu.VMEM((size, size), F32),
            pltpu.VMEM((size, size), F32),
            pltpu.VMEM((2, *tiles.shape), BF16),
        ]
        + scratch_of(size)
        + [pltpu.SemaphoreType.DMA((1 + size // BASE,))],
        compiler_params=pltpu.CompilerParams(vmem_limit_bytes=54 * MIB),
        cost_estimate=pl.CostEstimate(flops=120 * size**3, bytes_accessed=16 * MIB, transcendentals=0),
        name="invert_own",
    )(place, time_diag, tiles, prior)


def head_kernel(
    place, time_diag, other_in, block_in, prior_in, reached_out, early, rest, logdet,
    other_inverse, block, prior, reached, work, split_a, split_b, panel, left, right, columns, marks, sems,
):
    size = block.shape[0]
    head = early.shape[1]
    scale = time_diag[0]
    other_columns = pl.ds(pl.multiple_of((1 - place[0]) * size, size), size)
    copies = [
        begin(prior_in.at[:, other_columns], prior, sems.at[0]),
        begin(other_in, other_inverse, sems.at[1]),
        begin(block_in, block, sems.at[2]),
    ]
    copies[0].wait()
    split_a[0], split_a[1] = halves(scale * prior[...])
    copies[1].wait()
    split_b[0], split_b[1] = halves(other_inverse[...])
    copies[2].wait()
    rows = 256
    for first in range(0, size, rows):
        here = slice(first, first + rows)
        reached[here, :] = product((split_a[0, here], split_a[1, here]), (split_b[0], split_b[1]), NN)
        part = halves(reached[here, :])
        work[here, :] = block[here, :] - product(part, (split_a[0], split_a[1]), NT)
    reached_copy = begin(reached, reached_out, sems.at[0])
    by_row, by_column = unit_scales(work, size)
    for k, row_scale in enumerate(by_row):
        here = pl.ds(k * BASE, BASE)
        work[here, :] = work[here, :] * row_scale * by_column
    log_total = invert(work, panel, left, right, columns, marks, size, head)
    by_head = by_column[:, :head]
    logdet[...] = log_total - 2.0 * jnp.sum(jnp.log(by_head), axis=1, keepdims=True)
    back = 1.0 / by_column[:, head:]
    for k, row_scale in enumerate(by_row):
        here = pl.ds(k * BASE, BASE)
        if k * BASE < head:
            early[here, :] = work[here, :head] * (-row_scale) * by_head
        else:
            row_back = 1.0 / row_scale
            early[here, :] = work[here, :head] * row_back * by_head
            rest[pl.ds(k * BASE - head, BASE), :] = work[here, head:] * row_back * back
    reached_copy.wait()


def invert_head(place, time_diag, other_inverse, block, prior, head):
    size = prior.shape[0]
    return pl.pallas_call(
        head_kernel,
        out_shape=(shape(size, size), shape(size, head), shape(size - head, size - head), shape(1, 1)),
        in_specs=[SMEM, SMEM] + [ANY] * 3,
        out_specs=(HBM, VMEM, VMEM, VMEM),
        scratch_shapes=[pltpu.VMEM((size, size), F32)] * 5
        + [pltpu.VMEM((2, size, size), BF16)] * 2
        + scratch_of(size)
        + [pltpu.SemaphoreType.DMA((3,))],
        compiler_params=pltpu.CompilerParams(vmem_limit_bytes=60 * MIB),
        cost_estimate=pl.CostEstimate(flops=120 * size**3, bytes_accessed=16 * MIB, transcendentals=0),
        name="invert_head",
    )(place, time_diag, other_inverse, block, prior)


def tail_kernel(rest, inverse, logdet, panel, left, right, columns, marks):
    size = rest.shape[0]
    by_row, by_column = unit_scales(rest, size)
    for k, row_scale in enumerate(by_row):
        here = pl.ds(k * BASE, BASE)
        inverse[here, :] = rest[here, :] * row_scale * by_column
    log_total = invert(inverse, panel, left, right, columns, marks, size, size)
    logdet[...] = log_total - 2.0 * jnp.sum(jnp.log(by_column), axis=1, keepdims=True)
    for k, row_scale in enumerate(by_row):
        here = pl.ds(k * BASE, BASE)
        inverse[here, :] = inverse[here, :] * (-row_scale) * by_column


def invert_tail(rest):
    size = rest.shape[0]
    vmem = pl.BlockSpec(memory_space=pltpu.VMEM)
    return pl.pallas_call(
        tail_kernel,
        out_shape=(jax.ShapeDtypeStruct(rest.shape, F32), jax.ShapeDtypeStruct((1, 1), F32)),
        in_specs=[vmem],
        out_specs=(vmem, vmem),
        scratch_shapes=scratch_of(size),
        compiler_params=pltpu.CompilerParams(vmem_limit_bytes=60 * MIB),
        cost_estimate=pl.CostEstimate(flops=100 * size**3, bytes_accessed=4 * MIB, transcendentals=0),
        name="invert_tail",
    )(rest)


def rows_kernel(
    place, rho, tail, early, reached_in, gain_row, gain_column, coupling_out,
    reached, mine, coupling, split, sems,
):
    size, head = early.shape
    own = place[0]
    reached_copy = begin(reached_in, reached, sems.at[0])
    lower = halves(early[head:, :])
    mine[head:, :head] = -product(halves(tail[...]), lower, NN)
    mine[head:, head:] = tail[...]
    mine[:head, :] = -product(lower, halves(mine[head:, :]), TN)
    mine[:head, :head] += early[:head, :]
    own_columns = pl.ds(pl.multiple_of(own * size, size), size)
    other_columns = pl.ds(pl.multiple_of((1 - own) * size, size), size)
    sent = rho[0] * rho[1]
    own_gain = -sent * gain_row[:, own_columns]
    other_gain = sent * gain_row[:, other_columns]
    reached_copy.wait()
    split[0], split[1] = halves(reached[...])
    rows = 256
    copies = []
    for first in range(0, size, rows):
        here = slice(first, first + rows)
        part = mine[here, :] * gain_column[here, :]
        coupling[here, own_columns] = part * own_gain
        coupling[here, other_columns] = product(halves(part), (split[0], split[1]), NN) * other_gain
        place_out = pl.ds(first, rows)
        copies.append(begin(coupling.at[place_out], coupling_out.at[place_out], sems.at[first // rows]))
    for copy in copies:
        copy.wait()


def own_rows(place, rho, tail, early, reached, gain_row, gain_column):
    size = early.shape[0]
    return pl.pallas_call(
        rows_kernel,
        out_shape=shape(size, 2 * size),
        in_specs=[SMEM] * 2 + [VMEM] * 2 + [ANY] + [VMEM] * 2,
        out_specs=HBM,
        scratch_shapes=[
            pltpu.VMEM((size, size), F32),
            pltpu.VMEM((size, size), F32),
            pltpu.VMEM((size, 2 * size), F32),
            pltpu.VMEM((2, size, size), BF16),
            pltpu.SemaphoreType.DMA((size // 256,)),
        ],
        compiler_params=pltpu.CompilerParams(vmem_limit_bytes=60 * MIB),
        cost_estimate=pl.CostEstimate(flops=20 * size**3, bytes_accessed=24 * MIB, transcendentals=0),
        name="own_rows",
    )(place, rho, tail, early, reached, gain_row, gain_column)


def final_kernel(
    place, rho, time_diag, scalars, tiles_in, prior_in, coupling_in, inverse_1, inverse_0, early_0, early_1,
    tail_0, tail_1, gain_row, gain_column, reduced_out,
    tiles, prior, coupling, inverse, early, tail, reduced, last, split_p, split_t, split_l, split_g, split_f, sems,
):
    size, head = early.shape
    own = place[0]
    weight, scale = scalars[0] * scalars[0], scalars[2]
    kept = rho[1] / rho[0]
    rows = 256

    @pl.when(own == 0)
    def _():
        begin(inverse_0, inverse, sems.at[0])
        begin(early_0, early, sems.at[2])
        begin(tail_0, tail, sems.at[3])

    @pl.when(own == 1)
    def _():
        begin(inverse_1, inverse, sems.at[0])
        begin(early_1, early, sems.at[2])
        begin(tail_1, tail, sems.at[3])

    prior_copy = begin(prior_in, prior, sems.at[1])
    tiles_copy = begin(tiles_in, tiles, sems.at[4])
    coupling_copy = begin(coupling_in, coupling, sems.at[5])
    pltpu.make_async_copy(inverse_0, inverse, sems.at[0]).wait()
    prior_copy.wait()
    split_p[0], split_p[1] = halves(inverse[...])
    pltpu.make_async_copy(early_0, early, sems.at[2]).wait()
    pltpu.make_async_copy(tail_0, tail, sems.at[3]).wait()
    gain_0, gain_1 = gain_row[:, :size], gain_row[:, size:]

    def next_part(second):
        columns = slice(0, size) if second else slice(size, 2 * size)
        split_t[0], split_t[1] = halves(scale * prior[:, columns])
        for first in range(0, size, rows):
            here = slice(first, first + rows)
            if second:
                part = product((split_t[0, :, here], split_t[1, :, here]), (split_p[0], split_p[1]), TN)
            else:
                part = product((split_t[0, here], split_t[1, here]), (split_p[0], split_p[1]), NN)
            split_l[0, here], split_l[1, here] = halves(part)
            if first + rows > head:
                skip = max(head - first, 0)
                last[first + skip - head : first + rows - head, :] = part[skip:]
        upper = (split_l[0, :head], split_l[1, :head])
        middle = product(halves(early[:head, :]), upper, NN)
        last[...] -= product(halves(early[head:, :]), upper, NN)
        if second:
            reduced[:, :head] = weight * middle.T * gain_column[...] * gain_0[:, :head]
            reduced[:, head:size] = jnp.zeros((size, size - head), F32)
            middle_parts = halves(middle)
            for first in range(0, size, rows):
                here = slice(first, first + rows)
                term = inverse[here, :] + product(
                    (split_l[0, :head, here], split_l[1, :head, here]), middle_parts, TN
                )
                reduced[here, size:] = term * (-weight * gain_column[here, :]) * gain_1
        else:
            top = weight * gain_column[:head, :]
            reduced[:head, :head] = early[:head, :] * -top * gain_0[:, :head]
            reduced[:head, head:size] = jnp.zeros((head, size - head), F32)
            reduced[:head, size:] = top * middle * gain_1
            reduced[head:, :] = jnp.zeros((size - head, 2 * size), F32)

    @pl.when(own == 0)
    def _():
        next_part(False)

    @pl.when(own == 1)
    def _():
        next_part(True)

    own_columns = pl.ds(pl.multiple_of(own * size, size), size)
    other_columns = pl.ds(pl.multiple_of((1 - own) * size, size), size)
    below = size - head
    eye = lax.broadcasted_iota(jnp.int32, (below, below), 0) == lax.broadcasted_iota(jnp.int32, (below, below), 1)
    split_f[0, :, :head], split_f[1, :, :head] = halves(-early[head:, :] * gain_0[:, :head])
    split_f[0, :, head:size], split_f[1, :, head:size] = halves(jnp.where(eye, 1.0, 0.0) * gain_0[:, head:])
    split_f[0, :, size:], split_f[1, :, size:] = halves(-last[...] * gain_1)
    mine = (split_f[0, :, own_columns], split_f[1, :, own_columns])
    solved = halves(-weight * product(halves(tail[...]), mine, NN))
    tiles_copy.wait()
    split_g[0], split_g[1] = halves(tiles[...])
    coupling_copy.wait()
    copies = []
    for first in range(0, size, rows):
        here = slice(first, first + rows)
        reduced[here, :] += product((solved[0][:, here], solved[1][:, here]), (split_f[0], split_f[1]), TN)
        gram = product((split_g[0, :, here], split_g[1, :, here]), (split_g[0], split_g[1]), TN)
        for columns, term in ((own_columns, gram), (other_columns, 0.0)):
            reduced[here, columns] += time_diag[1] * prior[here, columns] + term + kept * coupling[here, columns]
        place_out = pl.ds(first, rows)
        copies.append(begin(reduced.at[place_out], reduced_out.at[place_out], sems.at[first // rows]))
    for copy in copies:
        copy.wait()


def final_rows(place, rho, time_diag, scalars, tiles, prior, coupling, inverses, earlies, tails, gain_row, gain_column):
    size, head = earlies[0].shape
    below = size - head
    return pl.pallas_call(
        final_kernel,
        out_shape=shape(size, 2 * size),
        in_specs=[SMEM] * 4 + [ANY] * 9 + [VMEM] * 2,
        out_specs=HBM,
        scratch_shapes=[
            pltpu.VMEM(tiles.shape, F32),
            pltpu.VMEM((size, 2 * size), F32),
            pltpu.VMEM((size, 2 * size), F32),
            pltpu.VMEM((size, size), F32),
            pltpu.VMEM((size, head), F32),
            pltpu.VMEM((below, below), F32),
            pltpu.VMEM((size, 2 * size), F32),
            pltpu.VMEM((below, size), F32),
            pltpu.VMEM((2, size, size), BF16),
            pltpu.VMEM((2, size, size), BF16),
            pltpu.VMEM((2, size, size), BF16),
            pltpu.VMEM((2, *tiles.shape), BF16),
            pltpu.VMEM((2, below, 2 * size), BF16),
            pltpu.SemaphoreType.DMA((6,)),
        ],
        compiler_params=pltpu.CompilerParams(vmem_limit_bytes=60 * MIB),
        cost_estimate=pl.CostEstimate(flops=30 * size**3, bytes_accessed=32 * MIB, transcendentals=0),
        name="final_rows",
    )(place, rho, time_diag, scalars, tiles, prior, coupling, *inverses, *earlies, *tails, gain_row, gain_column)


def from_next(x):
    count = lax.axis_size("tm")
    return lax.ppermute(x, "tm", [(i, i - 1) for i in range(1, count)])


def from_other(x):
    return lax.ppermute(x, "tile", [(0, 1), (1, 0)])


def to_partitions(x):
    return lax.all_to_all(x, "tm", split_axis=0, concat_axis=0, tiled=True).reshape(-1, x.shape[-1])


def from_next_core(x, core):
    count = lax.axis_size("tm")
    pairs = [(2 * i + core, 2 * (i - 1) + core) for i in range(1, count)]
    return lax.ppermute(x, ("tm", "tile"), pairs)


def across(x, core):
    return lax.ppermute(x, "tile", [(core, 1 - core)])


def after(x, *others):
    return lax.optimization_barrier((x, *others))[0]


def on_device(prior, node_gain, time_diag, rho, values, weights, steps):
    size, nodes = prior.shape
    head = size // 2
    own = lax.axis_index("tile")
    place = own.reshape(1).astype(jnp.int32)
    interior, separator = reorder(steps[0, 0], weights[0].T, values[0])
    scalars = from_next(jnp.concatenate([rho, time_diag]))
    gain_row = node_gain.reshape(1, nodes)
    gain_column = lax.dynamic_slice_in_dim(node_gain, own * size, size).reshape(size, 1)
    interior = to_partitions(interior)
    interior, separator, scalars, gain_row, gain_column = lax.optimization_barrier(
        (interior, separator, scalars, gain_row, gain_column)
    )
    separator = to_partitions(separator)
    block, own_inverse, own_log = invert_own(place, time_diag, interior, prior)
    other_inverse, separator = lax.optimization_barrier((from_other(own_inverse), separator))
    next_inverse_1 = from_next_core(own_inverse, 1)
    reached, early, rest, head_log = invert_head(place, time_diag, other_inverse, block, prior, head)
    next_early_0 = from_next_core(early, 0)
    next_inverse_1 = after(next_inverse_1, head_log)
    next_inverse_0 = across(next_inverse_1, 1)
    tail, tail_log = invert_tail(after(rest, next_inverse_1))
    log = jnp.where(own == 0, own_log, head_log + tail_log).reshape(1)
    other_log = from_other(log)
    next_tail_0 = from_next_core(tail, 0)
    coupling = own_rows(place, rho, tail, early, reached, gain_row, gain_column)
    next_early_0, next_tail_0, coupling = lax.optimization_barrier((next_early_0, next_tail_0, coupling))
    next_early_1 = across(next_early_0, 0)
    next_tail_1 = across(next_tail_0, 0)
    coupling_read = after(coupling, other_log)
    reduced = final_rows(
        place, rho, time_diag, scalars, separator, prior, coupling_read,
        (next_inverse_1, next_inverse_0), (next_early_0, next_early_1), (next_tail_0, next_tail_1),
        gain_row, gain_column,
    )
    interior_logdet = (log + other_log) / nodes
    return reduced[None], coupling[None], interior_logdet


def solution(mesh):
    in_specs = (
        P("tile", None),
        P(),
        P("tm"),
        P("tm"),
        P("tile", "tm", None, None),
        P("tile", "tm", None),
        P("tile", "tm", None),
    )
    out_specs = (P("tm", "tile", None), P("tm", "tile", None), P("tm"))
    return jax.shard_map(on_device, mesh=mesh, in_specs=in_specs, out_specs=out_specs, check_vma=False)
```

```python
import functools

import jax
import jax.numpy as jnp
from jax import lax
from jax.experimental import pallas as pl
from jax.experimental.pallas import tpu as pltpu
from jax.sharding import PartitionSpec as P

F32, BF16 = jnp.float32, jnp.bfloat16
BASE = 128
MIB = 1 << 20
ROW_PARTS = 2
SMEM = pl.BlockSpec(memory_space=pltpu.SMEM)
VMEM = pl.BlockSpec(memory_space=pltpu.VMEM)
ANY = pl.BlockSpec(memory_space=pl.ANY)
HBM = pl.BlockSpec(memory_space=pltpu.HBM)
NN = (((1,), (0,)), ((), ()))
NT = (((1,), (1,)), ((), ()))
TN = (((0,), (0,)), ((), ()))


def halves(x):
    high = x.astype(BF16)
    return high, (x - high.astype(F32)).astype(BF16)


def product(a, b, dims):
    dot = functools.partial(lax.dot_general, dimension_numbers=dims, preferred_element_type=F32)
    return dot(a[0], b[0]) + (dot(a[0], b[1]) + dot(a[1], b[0]))


def reorder_kernel(steps, weights_t, values, interior, separator, held, in_sems, out_sems):
    tiles = held.shape[0]
    chunks = in_sems.shape[0]
    per = tiles // chunks
    for chunk in range(chunks):
        rows = pl.ds(chunk * per, per)
        pltpu.make_async_copy(values.at[rows], held.at[rows], in_sems.at[chunk]).start()
    root = jnp.sqrt(weights_t[...])
    for chunk in range(chunks):
        rows = pl.ds(chunk * per, per)
        pltpu.make_async_copy(values.at[rows], held.at[rows], in_sems.at[chunk]).wait()
        for tile in range(chunk * per, (chunk + 1) * per):
            held[tile] = held[tile] * root[:, tile : tile + 1]
            step = steps[tile]
            partition = lax.shift_right_logical(step, 1)
            odd = lax.bitwise_and(step, 1)

            @pl.when(odd == 0)
            def _():
                pltpu.make_async_copy(held.at[tile], interior.at[partition], out_sems.at[0]).start()

            @pl.when(odd == 1)
            def _():
                pltpu.make_async_copy(held.at[tile], separator.at[partition], out_sems.at[1]).start()

    half = pl.ds(0, tiles // 2)
    pltpu.make_async_copy(held.at[half], interior, out_sems.at[0]).wait()
    pltpu.make_async_copy(held.at[half], separator, out_sems.at[1]).wait()


def reorder(steps, weights_t, values):
    tiles, rows, cols = values.shape
    half = jax.ShapeDtypeStruct((tiles // 2, rows, cols), F32)
    return pl.pallas_call(
        reorder_kernel,
        out_shape=(half, half),
        in_specs=[SMEM, VMEM, ANY],
        out_specs=(HBM, HBM),
        scratch_shapes=[
            pltpu.VMEM((tiles, rows, cols), F32),
            pltpu.SemaphoreType.DMA((8,)),
            pltpu.SemaphoreType.DMA((2,)),
        ],
        compiler_params=pltpu.CompilerParams(vmem_limit_bytes=60 * MIB),
        name="reorder",
    )(steps, weights_t, values)


def wide(x):
    return jnp.broadcast_to(x, (8, BASE))


def sweep_small(entries, size):
    at = lambda i, j: (min(i, j), max(i, j))
    dets = []
    for p in range(0, size, 2):
        a, b, d = entries[p, p], entries[p, p + 1], entries[p + 1, p + 1]
        det = a * d - b * b
        dets.append(det)
        scale = 1.0 / det
        inv_a, inv_b, inv_d = d * scale, b * scale, a * scale
        others = [i for i in range(size) if i not in (p, p + 1)]
        u = {i: entries[at(i, p)] for i in others}
        v = {i: entries[at(i, p + 1)] for i in others}
        new_u = {i: inv_a * u[i] - inv_b * v[i] for i in others}
        new_v = {i: inv_d * v[i] - inv_b * u[i] for i in others}
        for i in others:
            for j in others:
                if i <= j:
                    entries[i, j] = entries[i, j] - u[i] * new_u[j] - v[i] * new_v[j]
        for i in others:
            entries[at(i, p)] = new_u[i]
            entries[at(i, p + 1)] = new_v[i]
        entries[p, p], entries[p, p + 1], entries[p + 1, p + 1] = -inv_a, inv_b, -inv_d
    return dets


def total_of(terms):
    while len(terms) > 1:
        terms = [sum(terms[i : i + 2][1:], terms[i]) for i in range(0, len(terms), 2)]
    return terms[0]


def sweep_base(x, columns, marks, beside):
    lane = lax.broadcasted_iota(jnp.int32, (8, BASE), 1)
    sub = lax.broadcasted_iota(jnp.int32, (8, BASE), 0)
    x = list(x)
    groups = len(x)
    dets = jnp.ones((8, BASE), F32)
    for q in range(groups):
        panel = x[q]
        slot = q % 2
        inside = (lane // 8) == q
        first = 8 * q
        for j in range(8):
            columns[slot, j] = wide(panel[:, first + j : first + j + 1])
        entries = {(i, j): wide(columns[slot, j, i : i + 1, :]) for i in range(8) for j in range(i, 8)}
        marks[slot] = jnp.where(inside, jnp.where(lane == first + sub, -1.0, 0.0), panel)
        rows = [wide(marks[slot, j : j + 1, :]) for j in range(8)]
        for at, det in enumerate(sweep_small(entries, 8)):
            dets = jnp.where(lane == 4 * q + at, det, dets)
        new_rows = [
            total_of([entries[min(i, j), max(i, j)] * rows[j] for j in range(8)]) for i in range(8)
        ]
        new_panel = new_rows[7]
        for i in range(7):
            new_panel = jnp.where(sub == i, new_rows[i], new_panel)
        after_this = (q + 1) % groups
        next_panel = x[after_this]
        next_panel = total_of(
            [jnp.where(inside, 0.0, next_panel)]
            + [wide(next_panel[:, first + j : first + j + 1]) * new_rows[j] for j in range(8)]
        )
        high, low = halves(panel)
        new_high, new_low = halves(new_panel)
        change = lax.dot_general(
            jnp.concatenate([high, high, low], axis=0),
            jnp.concatenate([new_high, new_low, new_high], axis=0),
            TN,
            preferred_element_type=F32,
        )
        for i in range(groups):
            x[i] = jnp.where(inside, 0.0, x[i]) + change[8 * i : 8 * i + 8]
        x[after_this] = next_panel
        x[q] = -new_panel
        for piece in beside[q::groups]:
            piece()
    return x, dets


def unit_scales(m, size):
    eye = lax.broadcasted_iota(jnp.int32, (BASE, BASE), 0) == lax.broadcasted_iota(
        jnp.int32, (BASE, BASE), 1
    )
    columns, rows = [], []
    for k in range(size // BASE):
        here = pl.ds(k * BASE, BASE)
        diagonal = jnp.where(eye, m[here, here], 0.0)
        columns.append(lax.rsqrt(jnp.sum(diagonal, axis=1, keepdims=True)))
        rows.append(lax.rsqrt(jnp.sum(diagonal, axis=0, keepdims=True)))
    return columns, jnp.concatenate(rows, axis=1)


def invert(m, panel, left, right, columns, marks, size, pivots):
    dot = functools.partial(lax.dot_general, dimension_numbers=NN, preferred_element_type=F32)
    left[...] = jnp.zeros(left.shape, BF16)
    right[...] = jnp.zeros(right.shape, BF16)

    rows, width = size // ROW_PARTS, 256 if size % 256 == 0 else BASE

    def change(at_row, at_column):
        these = slice(at_row, at_row + rows)
        part = left[these, :]
        tile = slice(at_column, at_column + width)
        m[these, tile] -= dot(part, right[0, :, tile]) + dot(part, right[1, :, tile])

    changes = [
        functools.partial(change, at_row, at_column)
        for at_column in range(0, size, width)
        for at_row in range(0, size, rows)
    ]

    def step(k, logs):
        here = pl.ds(pl.multiple_of(k * BASE, BASE), BASE)
        part = left[here, :]
        m[here, :] -= dot(part, right[0]) + dot(part, right[1])
        left[here, :] = jnp.zeros((BASE, 2 * BASE), BF16)
        groups = [m[pl.ds(pl.multiple_of(k * BASE + 8 * q, 8), 8), here] for q in range(BASE // 8)]
        swept, dets = sweep_base(groups, columns, marks, changes)
        swept = jnp.concatenate(swept, axis=0)
        panel[...] = product(halves(-swept), halves(m[here, :]), NN)
        panel[:, here] = swept
        high, low = halves(panel[...])
        right[0, :BASE], right[0, BASE:] = high, high
        right[1, :BASE], right[1, BASE:] = low, low
        high, low = halves(m[:, here])
        left[:, :BASE], left[:, BASE:] = high, low
        left[here, :] = jnp.zeros((BASE, 2 * BASE), BF16)
        m[:, here] = jnp.zeros((size, BASE), F32)
        m[here, :] = panel[...]
        return logs + jnp.log(dets[0:1, :])

    logs = lax.fori_loop(0, pivots // BASE, step, jnp.zeros((1, BASE), F32))
    for piece in changes:
        piece()
    return jnp.sum(logs, axis=1, keepdims=True)


def begin(source, target, sem):
    copy = pltpu.make_async_copy(source, target, sem)
    copy.start()
    return copy


def own_kernel(
    place, time_diag, tiles_in, prior_in, block_out, inverse_out, logdet,
    tiles, prior, block, inverse, split, panel, left, right, columns, marks, sems,
):
    size = block.shape[0]
    scale = time_diag[0]
    own_columns = pl.ds(pl.multiple_of(place[0] * size, size), size)
    depth = tiles.shape[0]
    per = depth // 4
    tile_copies = [
        begin(tiles_in.at[pl.ds(c * per, per)], tiles.at[pl.ds(c * per, per)], sems.at[c]) for c in range(4)
    ]
    for c, copy in enumerate(tile_copies):
        copy.wait()
        if c == 2:
            prior_copy = begin(prior_in.at[:, own_columns], prior, sems.at[4])
        here = slice(c * per, (c + 1) * per)
        split[0, here], split[1, here] = halves(tiles[here])
    rows = 256
    for first in range(0, size, rows):
        here = slice(first, first + rows)
        gram = product((split[0, :, here], split[1, :, here]), (split[0], split[1]), TN)
        if first == 0:
            prior_copy.wait()
        block[here, :] = scale * prior[here, :] + gram
    block_copy = begin(block, block_out, sems.at[0])
    by_row, by_column = unit_scales(block, size)
    for k, row_scale in enumerate(by_row):
        here = pl.ds(k * BASE, BASE)
        inverse[here, :] = block[here, :] * row_scale * by_column
    log_total = invert(inverse, panel, left, right, columns, marks, size, size)
    logdet[...] = log_total - 2.0 * jnp.sum(jnp.log(by_column), axis=1, keepdims=True)
    copies = []
    for k, row_scale in enumerate(by_row):
        here = pl.ds(k * BASE, BASE)
        inverse[here, :] = inverse[here, :] * (-row_scale) * by_column
        copies.append(begin(inverse.at[here], inverse_out.at[here], sems.at[1 + k]))
    for copy in copies + [block_copy]:
        copy.wait()


def scratch_of(size):
    return [
        pltpu.VMEM((BASE, size), F32),
        pltpu.VMEM((size, 2 * BASE), BF16),
        pltpu.VMEM((2, 2 * BASE, size), BF16),
        pltpu.VMEM((2, 8, 8, BASE), F32),
        pltpu.VMEM((2, 8, BASE), F32),
    ]


def shape(*dims):
    return jax.ShapeDtypeStruct(dims, F32)


def invert_own(place, time_diag, tiles, prior):
    size = prior.shape[0]
    return pl.pallas_call(
        own_kernel,
        out_shape=(shape(size, size), shape(size, size), shape(1, 1)),
        in_specs=[SMEM, SMEM, ANY, ANY],
        out_specs=(HBM, HBM, VMEM),
        scratch_shapes=[
            pltpu.VMEM(tiles.shape, F32),
            pltpu.VMEM((size, size), F32),
            pltpu.VMEM((size, size), F32),
            pltpu.VMEM((size, size), F32),
            pltpu.VMEM((2, *tiles.shape), BF16),
        ]
        + scratch_of(size)
        + [pltpu.SemaphoreType.DMA((1 + size // BASE,))],
        compiler_params=pltpu.CompilerParams(vmem_limit_bytes=54 * MIB),
        cost_estimate=pl.CostEstimate(flops=120 * size**3, bytes_accessed=16 * MIB, transcendentals=0),
        name="invert_own",
    )(place, time_diag, tiles, prior)


def head_kernel(
    place, time_diag, other_in, block_in, prior_in, reached_out, early, rest, logdet,
    other_inverse, block, prior, reached, work, split_a, split_b, panel, left, right, columns, marks, sems,
):
    size = block.shape[0]
    head = early.shape[1]
    scale = time_diag[0]
    other_columns = pl.ds(pl.multiple_of((1 - place[0]) * size, size), size)
    copies = [
        begin(prior_in.at[:, other_columns], prior, sems.at[0]),
        begin(other_in, other_inverse, sems.at[1]),
    ]
    copies[0].wait()
    block_copy = begin(block_in, block, sems.at[2])
    split_a[0], split_a[1] = halves(scale * prior[...])
    copies[1].wait()
    split_b[0], split_b[1] = halves(other_inverse[...])
    rows = 256
    for first in range(0, size, rows):
        here = slice(first, first + rows)
        reached[here, :] = product((split_a[0, here], split_a[1, here]), (split_b[0], split_b[1]), NN)
        part = halves(reached[here, :])
        if first == 0:
            block_copy.wait()
        work[here, :] = block[here, :] - product(part, (split_a[0], split_a[1]), NT)
    reached_copy = begin(reached, reached_out, sems.at[0])
    by_row, by_column = unit_scales(work, size)
    for k, row_scale in enumerate(by_row):
        here = pl.ds(k * BASE, BASE)
        work[here, :] = work[here, :] * row_scale * by_column
    log_total = invert(work, panel, left, right, columns, marks, size, head)
    by_head = by_column[:, :head]
    logdet[...] = log_total - 2.0 * jnp.sum(jnp.log(by_head), axis=1, keepdims=True)
    back = 1.0 / by_column[:, head:]
    for k, row_scale in enumerate(by_row):
        here = pl.ds(k * BASE, BASE)
        if k * BASE < head:
            early[here, :] = work[here, :head] * (-row_scale) * by_head
        else:
            row_back = 1.0 / row_scale
            early[here, :] = work[here, :head] * row_back * by_head
            rest[pl.ds(k * BASE - head, BASE), :] = work[here, head:] * row_back * back
    reached_copy.wait()


def invert_head(place, time_diag, other_inverse, block, prior, head):
    size = prior.shape[0]
    return pl.pallas_call(
        head_kernel,
        out_shape=(shape(size, size), shape(size, head), shape(size - head, size - head), shape(1, 1)),
        in_specs=[SMEM, SMEM] + [ANY] * 3,
        out_specs=(HBM, VMEM, VMEM, VMEM),
        scratch_shapes=[pltpu.VMEM((size, size), F32)] * 5
        + [pltpu.VMEM((2, size, size), BF16)] * 2
        + scratch_of(size)
        + [pltpu.SemaphoreType.DMA((3,))],
        compiler_params=pltpu.CompilerParams(vmem_limit_bytes=60 * MIB),
        cost_estimate=pl.CostEstimate(flops=120 * size**3, bytes_accessed=16 * MIB, transcendentals=0),
        name="invert_head",
    )(place, time_diag, other_inverse, block, prior)


def tail_kernel(place, rest, own_log, head_log, inverse, logdet, panel, left, right, columns, marks):
    size = rest.shape[0]
    by_row, by_column = unit_scales(rest, size)
    for k, row_scale in enumerate(by_row):
        here = pl.ds(k * BASE, BASE)
        inverse[here, :] = rest[here, :] * row_scale * by_column
    log_total = invert(inverse, panel, left, right, columns, marks, size, size)
    log_total = head_log[...] + log_total - 2.0 * jnp.sum(jnp.log(by_column), axis=1, keepdims=True)
    logdet[...] = jnp.where(place[0] == 0, own_log[...], log_total)
    for k, row_scale in enumerate(by_row):
        here = pl.ds(k * BASE, BASE)
        inverse[here, :] = inverse[here, :] * (-row_scale) * by_column


def invert_tail(place, rest, own_log, head_log):
    size = rest.shape[0]
    return pl.pallas_call(
        tail_kernel,
        out_shape=(jax.ShapeDtypeStruct(rest.shape, F32), jax.ShapeDtypeStruct((1, 1), F32)),
        in_specs=[SMEM] + [VMEM] * 3,
        out_specs=(VMEM, VMEM),
        scratch_shapes=scratch_of(size),
        compiler_params=pltpu.CompilerParams(vmem_limit_bytes=60 * MIB),
        cost_estimate=pl.CostEstimate(flops=100 * size**3, bytes_accessed=4 * MIB, transcendentals=0),
        name="invert_tail",
    )(place, rest, own_log, head_log)


def own_column(gain_row, own, size):
    eye = lax.broadcasted_iota(jnp.int32, (BASE, BASE), 0) == lax.broadcasted_iota(
        jnp.int32, (BASE, BASE), 1
    )
    parts = []
    for k in range(size // BASE):
        piece = gain_row[:, pl.ds(pl.multiple_of(own * size + k * BASE, BASE), BASE)]
        parts.append(jnp.sum(jnp.where(eye, piece, 0.0), axis=1, keepdims=True))
    return jnp.concatenate(parts, axis=0)


def rows_kernel(
    place, rho, tail, early, reached_in, gain_row, coupling_out,
    reached, mine, coupling, split, sems,
):
    size, head = early.shape
    own = place[0]
    reached_copy = begin(reached_in, reached, sems.at[0])
    lower = halves(early[head:, :])
    mine[head:, :head] = -product(halves(tail[...]), lower, NN)
    mine[head:, head:] = tail[...]
    mine[:head, :] = -product(lower, halves(mine[head:, :]), TN)
    mine[:head, :head] += early[:head, :]
    own_columns = pl.ds(pl.multiple_of(own * size, size), size)
    other_columns = pl.ds(pl.multiple_of((1 - own) * size, size), size)
    sent = rho[0] * rho[1]
    own_gain = -sent * gain_row[:, own_columns]
    other_gain = sent * gain_row[:, other_columns]
    gain_column = own_column(gain_row, own, size)
    reached_copy.wait()
    split[0], split[1] = halves(reached[...])
    rows = 256
    copies = []
    for first in range(0, size, rows):
        here = slice(first, first + rows)
        part = mine[here, :] * gain_column[here]
        coupling[here, own_columns] = part * own_gain
        coupling[here, other_columns] = product(halves(part), (split[0], split[1]), NN) * other_gain
        place_out = pl.ds(first, rows)
        copies.append(begin(coupling.at[place_out], coupling_out.at[place_out], sems.at[first // rows]))
    for copy in copies:
        copy.wait()


def own_rows(place, rho, tail, early, reached, gain_row):
    size = early.shape[0]
    return pl.pallas_call(
        rows_kernel,
        out_shape=shape(size, 2 * size),
        in_specs=[SMEM] * 2 + [VMEM] * 2 + [ANY] + [VMEM],
        out_specs=HBM,
        scratch_shapes=[
            pltpu.VMEM((size, size), F32),
            pltpu.VMEM((size, size), F32),
            pltpu.VMEM((size, 2 * size), F32),
            pltpu.VMEM((2, size, size), BF16),
            pltpu.SemaphoreType.DMA((size // 256,)),
        ],
        compiler_params=pltpu.CompilerParams(vmem_limit_bytes=60 * MIB),
        cost_estimate=pl.CostEstimate(flops=20 * size**3, bytes_accessed=24 * MIB, transcendentals=0),
        name="own_rows",
    )(place, rho, tail, early, reached, gain_row)


def final_kernel(
    place, rho, time_diag, scalars, tiles_in, prior_in, coupling_in, inverse_1, inverse_0, early_0, early_1,
    tail_0, tail_1, gain_row, reduced_out,
    tiles, prior, coupling, inverse, early, tail, reduced, last, split_p, split_t, split_l, split_g, split_f, sems,
):
    size, head = early.shape
    own = place[0]
    weight, scale = scalars[0] * scalars[0], scalars[2]
    kept = rho[1] / rho[0]
    rows = 256

    own_columns = pl.ds(pl.multiple_of(own * size, size), size)
    other_columns = pl.ds(pl.multiple_of((1 - own) * size, size), size)

    @pl.when(own == 0)
    def _():
        begin(inverse_0, inverse, sems.at[0])

    @pl.when(own == 1)
    def _():
        begin(inverse_1, inverse, sems.at[0])

    other_copy = begin(prior_in.at[:, other_columns], prior.at[:, other_columns], sems.at[1])
    gain_column = own_column(gain_row, own, size)
    pltpu.make_async_copy(inverse_0, inverse, sems.at[0]).wait()

    @pl.when(own == 0)
    def _():
        begin(early_0, early, sems.at[2])
        begin(tail_0, tail, sems.at[3])

    @pl.when(own == 1)
    def _():
        begin(early_1, early, sems.at[2])
        begin(tail_1, tail, sems.at[3])

    tiles_copy = begin(tiles_in, tiles, sems.at[4])
    own_copy = begin(prior_in.at[:, own_columns], prior.at[:, own_columns], sems.at[0])
    coupling_copy = begin(coupling_in, coupling, sems.at[5])
    split_p[0], split_p[1] = halves(inverse[...])
    other_copy.wait()
    gain_0, gain_1 = gain_row[:, :size], gain_row[:, size:]

    def next_part(second):
        columns = slice(0, size) if second else slice(size, 2 * size)
        split_t[0], split_t[1] = halves(scale * prior[:, columns])
        for first in range(0, size, rows):
            here = slice(first, first + rows)
            if second:
                part = product((split_t[0, :, here], split_t[1, :, here]), (split_p[0], split_p[1]), TN)
            else:
                part = product((split_t[0, here], split_t[1, here]), (split_p[0], split_p[1]), NN)
            split_l[0, here], split_l[1, here] = halves(part)
            if first + rows > head:
                skip = max(head - first, 0)
                last[first + skip - head : first + rows - head, :] = part[skip:]
        pltpu.make_async_copy(early_0, early, sems.at[2]).wait()
        upper = (split_l[0, :head], split_l[1, :head])
        middle = product(halves(early[:head, :]), upper, NN)
        last[...] -= product(halves(early[head:, :]), upper, NN)
        if second:
            reduced[:, :head] = weight * middle.T * gain_column * gain_0[:, :head]
            reduced[:, head:size] = jnp.zeros((size, size - head), F32)
            middle_parts = halves(middle)
            for first in range(0, size, rows):
                here = slice(first, first + rows)
                term = inverse[here, :] + product(
                    (split_l[0, :head, here], split_l[1, :head, here]), middle_parts, TN
                )
                reduced[here, size:] = term * (-weight * gain_column[here]) * gain_1
        else:
            top = weight * gain_column[:head]
            reduced[:head, :head] = early[:head, :] * -top * gain_0[:, :head]
            reduced[:head, head:size] = jnp.zeros((head, size - head), F32)
            reduced[:head, size:] = top * middle * gain_1
            reduced[head:, :] = jnp.zeros((size - head, 2 * size), F32)

    @pl.when(own == 0)
    def _():
        next_part(False)

    @pl.when(own == 1)
    def _():
        next_part(True)

    pltpu.make_async_copy(tail_0, tail, sems.at[3]).wait()
    below = size - head
    eye = lax.broadcasted_iota(jnp.int32, (below, below), 0) == lax.broadcasted_iota(jnp.int32, (below, below), 1)
    split_f[0, :, :head], split_f[1, :, :head] = halves(-early[head:, :] * gain_0[:, :head])
    split_f[0, :, head:size], split_f[1, :, head:size] = halves(jnp.where(eye, 1.0, 0.0) * gain_0[:, head:])
    split_f[0, :, size:], split_f[1, :, size:] = halves(-last[...] * gain_1)
    mine = (split_f[0, :, own_columns], split_f[1, :, own_columns])
    solved = halves(-weight * product(halves(tail[...]), mine, NN))
    tiles_copy.wait()
    split_g[0], split_g[1] = halves(tiles[...])
    own_copy.wait()
    coupling_copy.wait()
    copies = []
    for first in range(0, size, rows):
        here = slice(first, first + rows)
        reduced[here, :] += product((solved[0][:, here], solved[1][:, here]), (split_f[0], split_f[1]), TN)
        gram = product((split_g[0, :, here], split_g[1, :, here]), (split_g[0], split_g[1]), TN)
        for columns, term in ((own_columns, gram), (other_columns, 0.0)):
            reduced[here, columns] += time_diag[1] * prior[here, columns] + term + kept * coupling[here, columns]
        place_out = pl.ds(first, rows)
        copies.append(begin(reduced.at[place_out], reduced_out.at[place_out], sems.at[first // rows]))
    for copy in copies:
        copy.wait()


def final_rows(place, rho, time_diag, scalars, tiles, prior, coupling, inverses, earlies, tails, gain_row):
    size, head = earlies[0].shape
    below = size - head
    return pl.pallas_call(
        final_kernel,
        out_shape=shape(size, 2 * size),
        in_specs=[SMEM] * 4 + [ANY] * 9 + [VMEM],
        out_specs=HBM,
        scratch_shapes=[
            pltpu.VMEM(tiles.shape, F32),
            pltpu.VMEM((size, 2 * size), F32),
            pltpu.VMEM((size, 2 * size), F32),
            pltpu.VMEM((size, size), F32),
            pltpu.VMEM((size, head), F32),
            pltpu.VMEM((below, below), F32),
            pltpu.VMEM((size, 2 * size), F32),
            pltpu.VMEM((below, size), F32),
            pltpu.VMEM((2, size, size), BF16),
            pltpu.VMEM((2, size, size), BF16),
            pltpu.VMEM((2, size, size), BF16),
            pltpu.VMEM((2, *tiles.shape), BF16),
            pltpu.VMEM((2, below, 2 * size), BF16),
            pltpu.SemaphoreType.DMA((6,)),
        ],
        compiler_params=pltpu.CompilerParams(vmem_limit_bytes=60 * MIB),
        cost_estimate=pl.CostEstimate(flops=30 * size**3, bytes_accessed=32 * MIB, transcendentals=0),
        name="final_rows",
    )(place, rho, time_diag, scalars, tiles, prior, coupling, *inverses, *earlies, *tails, gain_row)


def from_next(x):
    count = lax.axis_size("tm")
    return lax.ppermute(x, "tm", [(i, i - 1) for i in range(1, count)])


def from_other(x):
    return lax.ppermute(x, "tile", [(0, 1), (1, 0)])


def to_partitions(x):
    return lax.all_to_all(x, "tm", split_axis=0, concat_axis=0, tiled=True).reshape(-1, x.shape[-1])


def from_next_core(x, core):
    count = lax.axis_size("tm")
    pairs = [(2 * i + core, 2 * (i - 1) + core) for i in range(1, count)]
    return lax.ppermute(x, ("tm", "tile"), pairs)


def across(x, core):
    return lax.ppermute(x, "tile", [(core, 1 - core)])


def after(x, *others):
    return lax.optimization_barrier((x, *others))[0]


def on_device(prior, node_gain, time_diag, rho, values, weights, steps):
    size, nodes = prior.shape
    head = size // 2
    own = lax.axis_index("tile")
    place = own.reshape(1).astype(jnp.int32)
    interior, separator = reorder(steps[0, 0], weights[0].T, values[0])
    scalars = from_next(jnp.concatenate([rho, time_diag]))
    gain_row = node_gain.reshape(1, nodes)
    interior = to_partitions(interior)
    interior, separator, scalars, gain_row = lax.optimization_barrier((interior, separator, scalars, gain_row))
    separator = to_partitions(separator)
    block, own_inverse, own_log = invert_own(place, time_diag, interior, prior)
    next_inverse_1 = from_next_core(own_inverse, 1)
    other_inverse, separator = lax.optimization_barrier((from_other(own_inverse), separator))
    reached, early, rest, head_log = invert_head(place, time_diag, other_inverse, block, prior, head)
    next_early_0 = from_next_core(early, 0)
    next_inverse_1 = after(next_inverse_1, head_log)
    next_inverse_0 = across(next_inverse_1, 1)
    tail, log = invert_tail(place, after(rest, next_inverse_1), own_log, head_log)
    log = log.reshape(1)
    other_log = from_other(log)
    next_tail_0 = from_next_core(tail, 0)
    next_early_1 = across(after(next_early_0, log), 0)
    coupling = own_rows(place, rho, tail, early, reached, gain_row)
    next_tail_0, coupling, next_early_1, next_inverse_0, other_log = lax.optimization_barrier(
        (next_tail_0, coupling, next_early_1, next_inverse_0, other_log)
    )
    next_tail_1 = across(next_tail_0, 0)
    reduced = final_rows(
        place, rho, time_diag, scalars, separator, prior, coupling,
        (next_inverse_1, next_inverse_0), (next_early_0, next_early_1), (next_tail_0, next_tail_1), gain_row,
    )
    interior_logdet = (log + other_log) / nodes
    return reduced[None], coupling[None], interior_logdet


def solution(mesh):
    in_specs = (
        P("tile", None),
        P(),
        P("tm"),
        P("tm"),
        P("tile", "tm", None, None),
        P("tile", "tm", None),
        P("tile", "tm", None),
    )
    out_specs = (P("tm", "tile", None), P("tm", "tile", None), P("tm"))
    return jax.shard_map(on_device, mesh=mesh, in_specs=in_specs, out_specs=out_specs, check_vma=False)
```

```python
import functools

import jax
import jax.numpy as jnp
from jax import lax
from jax.experimental import pallas as pl
from jax.experimental.pallas import tpu as pltpu
from jax.sharding import PartitionSpec as P

F32, BF16 = jnp.float32, jnp.bfloat16
BASE = 128
MIB = 1 << 20
ROW_PARTS = 2
SMEM = pl.BlockSpec(memory_space=pltpu.SMEM)
VMEM = pl.BlockSpec(memory_space=pltpu.VMEM)
ANY = pl.BlockSpec(memory_space=pl.ANY)
HBM = pl.BlockSpec(memory_space=pltpu.HBM)
NN = (((1,), (0,)), ((), ()))
NT = (((1,), (1,)), ((), ()))
TN = (((0,), (0,)), ((), ()))


def halves(x):
    high = x.astype(BF16)
    return high, (x - high.astype(F32)).astype(BF16)


def product(a, b, dims):
    dot = functools.partial(lax.dot_general, dimension_numbers=dims, preferred_element_type=F32)
    return dot(a[0], b[0]) + (dot(a[0], b[1]) + dot(a[1], b[0]))


def reorder_kernel(steps, weights_t, values, interior, separator, held, in_sems, out_sems):
    tiles = held.shape[0]
    chunks = in_sems.shape[0]
    per = tiles // chunks
    for chunk in range(chunks):
        rows = pl.ds(chunk * per, per)
        pltpu.make_async_copy(values.at[rows], held.at[rows], in_sems.at[chunk]).start()
    root = jnp.sqrt(weights_t[...])
    for chunk in range(chunks):
        rows = pl.ds(chunk * per, per)
        pltpu.make_async_copy(values.at[rows], held.at[rows], in_sems.at[chunk]).wait()
        for tile in range(chunk * per, (chunk + 1) * per):
            held[tile] = held[tile] * root[:, tile : tile + 1]
            step = steps[tile]
            partition = lax.shift_right_logical(step, 1)
            odd = lax.bitwise_and(step, 1)

            @pl.when(odd == 0)
            def _():
                pltpu.make_async_copy(held.at[tile], interior.at[partition], out_sems.at[0]).start()

            @pl.when(odd == 1)
            def _():
                pltpu.make_async_copy(held.at[tile], separator.at[partition], out_sems.at[1]).start()

    half = pl.ds(0, tiles // 2)
    pltpu.make_async_copy(held.at[half], interior, out_sems.at[0]).wait()
    pltpu.make_async_copy(held.at[half], separator, out_sems.at[1]).wait()


def reorder(steps, weights_t, values):
    tiles, rows, cols = values.shape
    half = jax.ShapeDtypeStruct((tiles // 2, rows, cols), F32)
    return pl.pallas_call(
        reorder_kernel,
        out_shape=(half, half),
        in_specs=[SMEM, VMEM, ANY],
        out_specs=(HBM, HBM),
        scratch_shapes=[
            pltpu.VMEM((tiles, rows, cols), F32),
            pltpu.SemaphoreType.DMA((8,)),
            pltpu.SemaphoreType.DMA((2,)),
        ],
        compiler_params=pltpu.CompilerParams(vmem_limit_bytes=60 * MIB),
        name="reorder",
    )(steps, weights_t, values)


def wide(x):
    return jnp.broadcast_to(x, (8, BASE))


def sweep_small(entries, size):
    at = lambda i, j: (min(i, j), max(i, j))
    dets = []
    for p in range(0, size, 2):
        a, b, d = entries[p, p], entries[p, p + 1], entries[p + 1, p + 1]
        det = a * d - b * b
        dets.append(det)
        scale = 1.0 / det
        inv_a, inv_b, inv_d = d * scale, b * scale, a * scale
        others = [i for i in range(size) if i not in (p, p + 1)]
        u = {i: entries[at(i, p)] for i in others}
        v = {i: entries[at(i, p + 1)] for i in others}
        new_u = {i: inv_a * u[i] - inv_b * v[i] for i in others}
        new_v = {i: inv_d * v[i] - inv_b * u[i] for i in others}
        for i in others:
            for j in others:
                if i <= j:
                    entries[i, j] = entries[i, j] - u[i] * new_u[j] - v[i] * new_v[j]
        for i in others:
            entries[at(i, p)] = new_u[i]
            entries[at(i, p + 1)] = new_v[i]
        entries[p, p], entries[p, p + 1], entries[p + 1, p + 1] = -inv_a, inv_b, -inv_d
    return dets


def total_of(terms):
    while len(terms) > 1:
        terms = [sum(terms[i : i + 2][1:], terms[i]) for i in range(0, len(terms), 2)]
    return terms[0]


def sweep_base(x, columns, marks, beside):
    lane = lax.broadcasted_iota(jnp.int32, (8, BASE), 1)
    sub = lax.broadcasted_iota(jnp.int32, (8, BASE), 0)
    x = list(x)
    groups = len(x)
    dets = jnp.ones((8, BASE), F32)
    for q in range(groups):
        panel = x[q]
        slot = q % 2
        inside = (lane // 8) == q
        first = 8 * q
        for j in range(8):
            columns[slot, j] = wide(panel[:, first + j : first + j + 1])
        entries = {(i, j): wide(columns[slot, j, i : i + 1, :]) for i in range(8) for j in range(i, 8)}
        marks[slot] = jnp.where(inside, jnp.where(lane == first + sub, -1.0, 0.0), panel)
        rows = [wide(marks[slot, j : j + 1, :]) for j in range(8)]
        for at, det in enumerate(sweep_small(entries, 8)):
            dets = jnp.where(lane == 4 * q + at, det, dets)
        new_rows = [
            total_of([entries[min(i, j), max(i, j)] * rows[j] for j in range(8)]) for i in range(8)
        ]
        new_panel = new_rows[7]
        for i in range(7):
            new_panel = jnp.where(sub == i, new_rows[i], new_panel)
        after_this = (q + 1) % groups
        next_panel = x[after_this]
        next_panel = total_of(
            [jnp.where(inside, 0.0, next_panel)]
            + [wide(next_panel[:, first + j : first + j + 1]) * new_rows[j] for j in range(8)]
        )
        high, low = halves(panel)
        new_high, new_low = halves(new_panel)
        change = lax.dot_general(
            jnp.concatenate([high, high, low], axis=0),
            jnp.concatenate([new_high, new_low, new_high], axis=0),
            TN,
            preferred_element_type=F32,
        )
        for i in range(groups):
            x[i] = jnp.where(inside, 0.0, x[i]) + change[8 * i : 8 * i + 8]
        x[after_this] = next_panel
        x[q] = -new_panel
        for piece in beside[q::groups]:
            piece()
    return x, dets


def unit_scales(m, size):
    eye = lax.broadcasted_iota(jnp.int32, (BASE, BASE), 0) == lax.broadcasted_iota(
        jnp.int32, (BASE, BASE), 1
    )
    columns, rows = [], []
    for k in range(size // BASE):
        here = pl.ds(k * BASE, BASE)
        diagonal = jnp.where(eye, m[here, here], 0.0)
        columns.append(lax.rsqrt(jnp.sum(diagonal, axis=1, keepdims=True)))
        rows.append(lax.rsqrt(jnp.sum(diagonal, axis=0, keepdims=True)))
    return columns, jnp.concatenate(rows, axis=1)


def invert(m, panel, left, right, columns, marks, size, pivots, extra=lambda k: []):
    dot = functools.partial(lax.dot_general, dimension_numbers=NN, preferred_element_type=F32)
    left[...] = jnp.zeros(left.shape, BF16)
    right[...] = jnp.zeros(right.shape, BF16)

    rows, width = size // ROW_PARTS, 256 if size % 256 == 0 else BASE

    def change(at_row, at_column):
        these = slice(at_row, at_row + rows)
        part = left[these, :]
        tile = slice(at_column, at_column + width)
        m[these, tile] -= dot(part, right[0, :, tile]) + dot(part, right[1, :, tile])

    changes = [
        functools.partial(change, at_row, at_column)
        for at_column in range(0, size, width)
        for at_row in range(0, size, rows)
    ]

    def step(k, logs):
        here = pl.ds(pl.multiple_of(k * BASE, BASE), BASE)
        part = left[here, :]
        first = m[here, here] - (dot(part, right[0, :, here]) + dot(part, right[1, :, here]))
        groups = [first[8 * q : 8 * q + 8] for q in range(BASE // 8)]
        swept, dets = sweep_base(groups, columns, marks, changes + extra(k))
        swept = jnp.concatenate(swept, axis=0)
        panel[...] = product(halves(-swept), halves(m[here, :]), NN)
        panel[:, here] = swept
        high, low = halves(panel[...])
        right[0, :BASE], right[0, BASE:] = high, high
        right[1, :BASE], right[1, BASE:] = low, low
        high, low = halves(m[:, here])
        left[:, :BASE], left[:, BASE:] = high, low
        left[here, :] = jnp.zeros((BASE, 2 * BASE), BF16)
        m[:, here] = jnp.zeros((size, BASE), F32)
        m[here, :] = panel[...]
        return logs + jnp.log(dets[0:1, :])

    logs = lax.fori_loop(0, pivots // BASE, step, jnp.zeros((1, BASE), F32))
    for piece in changes:
        piece()
    return jnp.sum(logs, axis=1, keepdims=True)


def begin(source, target, sem):
    copy = pltpu.make_async_copy(source, target, sem)
    copy.start()
    return copy


def own_kernel(
    place, time_diag, tiles_in, prior_in, block_out, inverse_out, logdet,
    tiles, prior, block, inverse, split, panel, left, right, columns, marks, sems,
):
    size = block.shape[0]
    scale = time_diag[0]
    own_columns = pl.ds(pl.multiple_of(place[0] * size, size), size)
    depth = tiles.shape[0]
    per = depth // 4
    tile_copies = [
        begin(tiles_in.at[pl.ds(c * per, per)], tiles.at[pl.ds(c * per, per)], sems.at[c]) for c in range(4)
    ]
    for c, copy in enumerate(tile_copies):
        copy.wait()
        if c == 2:
            prior_copy = begin(prior_in.at[:, own_columns], prior, sems.at[4])
        here = slice(c * per, (c + 1) * per)
        split[0, here], split[1, here] = halves(tiles[here])
    rows = 256
    for first in range(0, size, rows):
        here = slice(first, first + rows)
        gram = product((split[0, :, here], split[1, :, here]), (split[0], split[1]), TN)
        if first == 0:
            prior_copy.wait()
        block[here, :] = scale * prior[here, :] + gram
    block_copy = begin(block, block_out, sems.at[0])
    by_row, by_column = unit_scales(block, size)
    for k, row_scale in enumerate(by_row):
        here = pl.ds(k * BASE, BASE)
        inverse[here, :] = block[here, :] * row_scale * by_column
    log_total = invert(inverse, panel, left, right, columns, marks, size, size)
    logdet[...] = log_total - 2.0 * jnp.sum(jnp.log(by_column), axis=1, keepdims=True)
    copies = []
    for k, row_scale in enumerate(by_row):
        here = pl.ds(k * BASE, BASE)
        inverse[here, :] = inverse[here, :] * (-row_scale) * by_column
        copies.append(begin(inverse.at[here], inverse_out.at[here], sems.at[1 + k]))
    for copy in copies + [block_copy]:
        copy.wait()


def scratch_of(size):
    return [
        pltpu.VMEM((BASE, size), F32),
        pltpu.VMEM((size, 2 * BASE), BF16),
        pltpu.VMEM((2, 2 * BASE, size), BF16),
        pltpu.VMEM((2, 8, 8, BASE), F32),
        pltpu.VMEM((2, 8, BASE), F32),
    ]


def shape(*dims):
    return jax.ShapeDtypeStruct(dims, F32)


def invert_own(place, time_diag, tiles, prior):
    size = prior.shape[0]
    return pl.pallas_call(
        own_kernel,
        out_shape=(shape(size, size), shape(size, size), shape(1, 1)),
        in_specs=[SMEM, SMEM, ANY, ANY],
        out_specs=(HBM, HBM, VMEM),
        scratch_shapes=[
            pltpu.VMEM(tiles.shape, F32),
            pltpu.VMEM((size, size), F32),
            pltpu.VMEM((size, size), F32),
            pltpu.VMEM((size, size), F32),
            pltpu.VMEM((2, *tiles.shape), BF16),
        ]
        + scratch_of(size)
        + [pltpu.SemaphoreType.DMA((1 + size // BASE,))],
        compiler_params=pltpu.CompilerParams(vmem_limit_bytes=54 * MIB),
        cost_estimate=pl.CostEstimate(flops=120 * size**3, bytes_accessed=16 * MIB, transcendentals=0),
        name="invert_own",
    )(place, time_diag, tiles, prior)


def head_kernel(
    place, time_diag, other_in, block_in, prior_in, tiles_in, reached_out, gram_out, early, rest, logdet,
    tiles, gram, split_g, other_inverse, block, prior, reached, work, split_a, split_b, panel, left, right, columns, marks, sems,
):
    size = block.shape[0]
    head = early.shape[1]
    scale = time_diag[0]
    other_columns = pl.ds(pl.multiple_of((1 - place[0]) * size, size), size)
    copies = [
        begin(prior_in.at[:, other_columns], prior, sems.at[0]),
        begin(other_in, other_inverse, sems.at[1]),
    ]
    copies[0].wait()
    block_copy = begin(block_in, block, sems.at[2])
    tiles_copy = begin(tiles_in, tiles, sems.at[0])
    split_a[0], split_a[1] = halves(scale * prior[...])
    copies[1].wait()
    split_b[0], split_b[1] = halves(other_inverse[...])
    rows = 256
    for first in range(0, size, rows):
        here = slice(first, first + rows)
        reached[here, :] = product((split_a[0, here], split_a[1, here]), (split_b[0], split_b[1]), NN)
        part = halves(reached[here, :])
        if first == 0:
            block_copy.wait()
        work[here, :] = block[here, :] - product(part, (split_a[0], split_a[1]), NT)
    reached_copy = begin(reached, reached_out, sems.at[1])
    by_row, by_column = unit_scales(work, size)
    for k, row_scale in enumerate(by_row):
        here = pl.ds(k * BASE, BASE)
        work[here, :] = work[here, :] * row_scale * by_column
    tiles_copy.wait()
    split_g[0], split_g[1] = halves(tiles[...])
    share = size // (head // BASE)

    def gram_pieces(k):
        these = pl.ds(pl.multiple_of(k * share, share), share)

        def piece(at_column):
            tile = slice(at_column, at_column + rows)
            part = (split_g[0, :, these], split_g[1, :, these])
            gram[these, tile] = product(part, (split_g[0, :, tile], split_g[1, :, tile]), TN)

        return [functools.partial(piece, at_column) for at_column in range(0, size, rows)]

    log_total = invert(work, panel, left, right, columns, marks, size, head, gram_pieces)
    gram_copy = begin(gram, gram_out, sems.at[0])
    by_head = by_column[:, :head]
    logdet[...] = log_total - 2.0 * jnp.sum(jnp.log(by_head), axis=1, keepdims=True)
    back = 1.0 / by_column[:, head:]
    for k, row_scale in enumerate(by_row):
        here = pl.ds(k * BASE, BASE)
        if k * BASE < head:
            early[here, :] = work[here, :head] * (-row_scale) * by_head
        else:
            row_back = 1.0 / row_scale
            early[here, :] = work[here, :head] * row_back * by_head
            rest[pl.ds(k * BASE - head, BASE), :] = work[here, head:] * row_back * back
    reached_copy.wait()
    gram_copy.wait()


def invert_head(place, time_diag, other_inverse, block, prior, tiles, head):
    size = prior.shape[0]
    return pl.pallas_call(
        head_kernel,
        out_shape=(
            shape(size, size), shape(size, size), shape(size, head), shape(size - head, size - head), shape(1, 1)
        ),
        in_specs=[SMEM, SMEM] + [ANY] * 4,
        out_specs=(HBM, HBM, VMEM, VMEM, VMEM),
        scratch_shapes=[
            pltpu.VMEM(tiles.shape, F32),
            pltpu.VMEM((size, size), F32),
            pltpu.VMEM((2, *tiles.shape), BF16),
        ]
        + [pltpu.VMEM((size, size), F32)] * 5
        + [pltpu.VMEM((2, size, size), BF16)] * 2
        + scratch_of(size)
        + [pltpu.SemaphoreType.DMA((3,))],
        compiler_params=pltpu.CompilerParams(vmem_limit_bytes=60 * MIB),
        cost_estimate=pl.CostEstimate(flops=120 * size**3, bytes_accessed=16 * MIB, transcendentals=0),
        name="invert_head",
    )(place, time_diag, other_inverse, block, prior, tiles)


def tail_kernel(place, rest, own_log, head_log, inverse, logdet, panel, left, right, columns, marks):
    size = rest.shape[0]
    by_row, by_column = unit_scales(rest, size)
    for k, row_scale in enumerate(by_row):
        here = pl.ds(k * BASE, BASE)
        inverse[here, :] = rest[here, :] * row_scale * by_column
    log_total = invert(inverse, panel, left, right, columns, marks, size, size)
    log_total = head_log[...] + log_total - 2.0 * jnp.sum(jnp.log(by_column), axis=1, keepdims=True)
    logdet[...] = jnp.where(place[0] == 0, own_log[...], log_total)
    for k, row_scale in enumerate(by_row):
        here = pl.ds(k * BASE, BASE)
        inverse[here, :] = inverse[here, :] * (-row_scale) * by_column


def invert_tail(place, rest, own_log, head_log):
    size = rest.shape[0]
    return pl.pallas_call(
        tail_kernel,
        out_shape=(jax.ShapeDtypeStruct(rest.shape, F32), jax.ShapeDtypeStruct((1, 1), F32)),
        in_specs=[SMEM] + [VMEM] * 3,
        out_specs=(VMEM, VMEM),
        scratch_shapes=scratch_of(size),
        compiler_params=pltpu.CompilerParams(vmem_limit_bytes=60 * MIB),
        cost_estimate=pl.CostEstimate(flops=100 * size**3, bytes_accessed=4 * MIB, transcendentals=0),
        name="invert_tail",
    )(place, rest, own_log, head_log)


def own_column(gain_row, own, size):
    eye = lax.broadcasted_iota(jnp.int32, (BASE, BASE), 0) == lax.broadcasted_iota(
        jnp.int32, (BASE, BASE), 1
    )
    parts = []
    for k in range(size // BASE):
        piece = gain_row[:, pl.ds(pl.multiple_of(own * size + k * BASE, BASE), BASE)]
        parts.append(jnp.sum(jnp.where(eye, piece, 0.0), axis=1, keepdims=True))
    return jnp.concatenate(parts, axis=0)


def rows_kernel(
    place, rho, tail, early, reached_in, gain_row, coupling_out,
    reached, mine, coupling, split, sems,
):
    size, head = early.shape
    own = place[0]
    reached_copy = begin(reached_in, reached, sems.at[0])
    lower = halves(early[head:, :])
    mine[head:, :head] = -product(halves(tail[...]), lower, NN)
    mine[head:, head:] = tail[...]
    mine[:head, :] = -product(lower, halves(mine[head:, :]), TN)
    mine[:head, :head] += early[:head, :]
    own_columns = pl.ds(pl.multiple_of(own * size, size), size)
    other_columns = pl.ds(pl.multiple_of((1 - own) * size, size), size)
    sent = rho[0] * rho[1]
    own_gain = -sent * gain_row[:, own_columns]
    other_gain = sent * gain_row[:, other_columns]
    gain_column = own_column(gain_row, own, size)
    reached_copy.wait()
    split[0], split[1] = halves(reached[...])
    rows = 256
    copies = []
    for first in range(0, size, rows):
        here = slice(first, first + rows)
        part = mine[here, :] * gain_column[here]
        coupling[here, own_columns] = part * own_gain
        coupling[here, other_columns] = product(halves(part), (split[0], split[1]), NN) * other_gain
        place_out = pl.ds(first, rows)
        copies.append(begin(coupling.at[place_out], coupling_out.at[place_out], sems.at[first // rows]))
    for copy in copies:
        copy.wait()


def own_rows(place, rho, tail, early, reached, gain_row):
    size = early.shape[0]
    return pl.pallas_call(
        rows_kernel,
        out_shape=shape(size, 2 * size),
        in_specs=[SMEM] * 2 + [VMEM] * 2 + [ANY] + [VMEM],
        out_specs=HBM,
        scratch_shapes=[
            pltpu.VMEM((size, size), F32),
            pltpu.VMEM((size, size), F32),
            pltpu.VMEM((size, 2 * size), F32),
            pltpu.VMEM((2, size, size), BF16),
            pltpu.SemaphoreType.DMA((size // 256,)),
        ],
        compiler_params=pltpu.CompilerParams(vmem_limit_bytes=60 * MIB),
        cost_estimate=pl.CostEstimate(flops=20 * size**3, bytes_accessed=24 * MIB, transcendentals=0),
        name="own_rows",
    )(place, rho, tail, early, reached, gain_row)


def final_kernel(
    place, rho, time_diag, scalars, gram_in, prior_in, coupling_in, inverse_1, inverse_0, early_0, early_1,
    tail_0, tail_1, gain_row, reduced_out,
    gram, prior, coupling, inverse, early, tail, reduced, last, split_p, split_t, split_l, split_f, sems,
):
    size, head = early.shape
    own = place[0]
    weight, scale = scalars[0] * scalars[0], scalars[2]
    kept = rho[1] / rho[0]
    rows = 256

    own_columns = pl.ds(pl.multiple_of(own * size, size), size)
    other_columns = pl.ds(pl.multiple_of((1 - own) * size, size), size)

    @pl.when(own == 0)
    def _():
        begin(inverse_0, inverse, sems.at[0])

    @pl.when(own == 1)
    def _():
        begin(inverse_1, inverse, sems.at[0])

    other_copy = begin(prior_in.at[:, other_columns], prior.at[:, other_columns], sems.at[1])
    gain_column = own_column(gain_row, own, size)
    pltpu.make_async_copy(inverse_0, inverse, sems.at[0]).wait()

    @pl.when(own == 0)
    def _():
        begin(early_0, early, sems.at[2])
        begin(tail_0, tail, sems.at[3])

    @pl.when(own == 1)
    def _():
        begin(early_1, early, sems.at[2])
        begin(tail_1, tail, sems.at[3])

    gram_copy = begin(gram_in, gram, sems.at[4])
    own_copy = begin(prior_in.at[:, own_columns], prior.at[:, own_columns], sems.at[0])
    coupling_copy = begin(coupling_in, coupling, sems.at[5])
    split_p[0], split_p[1] = halves(inverse[...])
    other_copy.wait()
    gain_0, gain_1 = gain_row[:, :size], gain_row[:, size:]

    def next_part(second):
        columns = slice(0, size) if second else slice(size, 2 * size)
        split_t[0], split_t[1] = halves(scale * prior[:, columns])
        for first in range(0, size, rows):
            here = slice(first, first + rows)
            if second:
                part = product((split_t[0, :, here], split_t[1, :, here]), (split_p[0], split_p[1]), TN)
            else:
                part = product((split_t[0, here], split_t[1, here]), (split_p[0], split_p[1]), NN)
            split_l[0, here], split_l[1, here] = halves(part)
            if first + rows > head:
                skip = max(head - first, 0)
                last[first + skip - head : first + rows - head, :] = part[skip:]
        pltpu.make_async_copy(early_0, early, sems.at[2]).wait()
        upper = (split_l[0, :head], split_l[1, :head])
        middle = product(halves(early[:head, :]), upper, NN)
        last[...] -= product(halves(early[head:, :]), upper, NN)
        if second:
            reduced[:, :head] = weight * middle.T * gain_column * gain_0[:, :head]
            reduced[:, head:size] = jnp.zeros((size, size - head), F32)
            middle_parts = halves(middle)
            for first in range(0, size, rows):
                here = slice(first, first + rows)
                term = inverse[here, :] + product(
                    (split_l[0, :head, here], split_l[1, :head, here]), middle_parts, TN
                )
                reduced[here, size:] = term * (-weight * gain_column[here]) * gain_1
        else:
            top = weight * gain_column[:head]
            reduced[:head, :head] = early[:head, :] * -top * gain_0[:, :head]
            reduced[:head, head:size] = jnp.zeros((head, size - head), F32)
            reduced[:head, size:] = top * middle * gain_1
            reduced[head:, :] = jnp.zeros((size - head, 2 * size), F32)

    @pl.when(own == 0)
    def _():
        next_part(False)

    @pl.when(own == 1)
    def _():
        next_part(True)

    pltpu.make_async_copy(tail_0, tail, sems.at[3]).wait()
    below = size - head
    eye = lax.broadcasted_iota(jnp.int32, (below, below), 0) == lax.broadcasted_iota(jnp.int32, (below, below), 1)
    split_f[0, :, :head], split_f[1, :, :head] = halves(-early[head:, :] * gain_0[:, :head])
    split_f[0, :, head:size], split_f[1, :, head:size] = halves(jnp.where(eye, 1.0, 0.0) * gain_0[:, head:])
    split_f[0, :, size:], split_f[1, :, size:] = halves(-last[...] * gain_1)
    mine = (split_f[0, :, own_columns], split_f[1, :, own_columns])
    solved = halves(-weight * product(halves(tail[...]), mine, NN))
    gram_copy.wait()
    own_copy.wait()
    coupling_copy.wait()
    copies = []
    for first in range(0, size, rows):
        here = slice(first, first + rows)
        reduced[here, :] += product((solved[0][:, here], solved[1][:, here]), (split_f[0], split_f[1]), TN)
        for columns, term in ((own_columns, gram[here, :]), (other_columns, 0.0)):
            reduced[here, columns] += time_diag[1] * prior[here, columns] + term + kept * coupling[here, columns]
        place_out = pl.ds(first, rows)
        copies.append(begin(reduced.at[place_out], reduced_out.at[place_out], sems.at[first // rows]))
    for copy in copies:
        copy.wait()


def final_rows(place, rho, time_diag, scalars, gram, prior, coupling, inverses, earlies, tails, gain_row):
    size, head = earlies[0].shape
    below = size - head
    return pl.pallas_call(
        final_kernel,
        out_shape=shape(size, 2 * size),
        in_specs=[SMEM] * 4 + [ANY] * 9 + [VMEM],
        out_specs=HBM,
        scratch_shapes=[
            pltpu.VMEM((size, size), F32),
            pltpu.VMEM((size, 2 * size), F32),
            pltpu.VMEM((size, 2 * size), F32),
            pltpu.VMEM((size, size), F32),
            pltpu.VMEM((size, head), F32),
            pltpu.VMEM((below, below), F32),
            pltpu.VMEM((size, 2 * size), F32),
            pltpu.VMEM((below, size), F32),
            pltpu.VMEM((2, size, size), BF16),
            pltpu.VMEM((2, size, size), BF16),
            pltpu.VMEM((2, size, size), BF16),
            pltpu.VMEM((2, below, 2 * size), BF16),
            pltpu.SemaphoreType.DMA((6,)),
        ],
        compiler_params=pltpu.CompilerParams(vmem_limit_bytes=60 * MIB),
        cost_estimate=pl.CostEstimate(flops=30 * size**3, bytes_accessed=32 * MIB, transcendentals=0),
        name="final_rows",
    )(place, rho, time_diag, scalars, gram, prior, coupling, *inverses, *earlies, *tails, gain_row)


def from_next(x):
    count = lax.axis_size("tm")
    return lax.ppermute(x, "tm", [(i, i - 1) for i in range(1, count)])


def from_other(x):
    return lax.ppermute(x, "tile", [(0, 1), (1, 0)])


def to_partitions(x):
    return lax.all_to_all(x, "tm", split_axis=0, concat_axis=0, tiled=True).reshape(-1, x.shape[-1])


def from_next_core(x, core):
    count = lax.axis_size("tm")
    pairs = [(2 * i + core, 2 * (i - 1) + core) for i in range(1, count)]
    return lax.ppermute(x, ("tm", "tile"), pairs)


def across(x, core):
    return lax.ppermute(x, "tile", [(core, 1 - core)])


def after(x, *others):
    return lax.optimization_barrier((x, *others))[0]


def on_device(prior, node_gain, time_diag, rho, values, weights, steps):
    size, nodes = prior.shape
    head = size // 2
    own = lax.axis_index("tile")
    place = own.reshape(1).astype(jnp.int32)
    interior, separator = reorder(steps[0, 0], weights[0].T, values[0])
    scalars = from_next(jnp.concatenate([rho, time_diag]))
    gain_row = node_gain.reshape(1, nodes)
    interior = to_partitions(interior)
    interior, separator, scalars, gain_row = lax.optimization_barrier((interior, separator, scalars, gain_row))
    separator = to_partitions(separator)
    block, own_inverse, own_log = invert_own(place, time_diag, interior, prior)
    next_inverse_1 = from_next_core(own_inverse, 1)
    other_inverse, separator = lax.optimization_barrier((from_other(own_inverse), separator))
    reached, gram, early, rest, head_log = invert_head(
        place, time_diag, other_inverse, block, prior, separator, head
    )
    next_early_0 = from_next_core(early, 0)
    next_inverse_1 = after(next_inverse_1, head_log)
    next_inverse_0 = across(next_inverse_1, 1)
    tail, log = invert_tail(place, after(rest, next_inverse_1), own_log, head_log)
    log = log.reshape(1)
    other_log = from_other(log)
    next_tail_0 = from_next_core(tail, 0)
    next_early_1 = across(after(next_early_0, log), 0)
    coupling = own_rows(place, rho, tail, early, reached, gain_row)
    next_tail_0, coupling, next_early_1, next_inverse_0, other_log = lax.optimization_barrier(
        (next_tail_0, coupling, next_early_1, next_inverse_0, other_log)
    )
    next_tail_1 = across(next_tail_0, 0)
    reduced = final_rows(
        place, rho, time_diag, scalars, gram, prior, coupling,
        (next_inverse_1, next_inverse_0), (next_early_0, next_early_1), (next_tail_0, next_tail_1), gain_row,
    )
    interior_logdet = (log + other_log) / nodes
    return reduced[None], coupling[None], interior_logdet


def solution(mesh):
    in_specs = (
        P("tile", None),
        P(),
        P("tm"),
        P("tm"),
        P("tile", "tm", None, None),
        P("tile", "tm", None),
        P("tile", "tm", None),
    )
    out_specs = (P("tm", "tile", None), P("tm", "tile", None), P("tm"))
    return jax.shard_map(on_device, mesh=mesh, in_specs=in_specs, out_specs=out_specs, check_vma=False)
```

```python
import functools

import jax
import jax.numpy as jnp
from jax import lax
from jax.experimental import pallas as pl
from jax.experimental.pallas import tpu as pltpu
from jax.sharding import PartitionSpec as P

F32, BF16 = jnp.float32, jnp.bfloat16
BASE = 128
MIB = 1 << 20
ROW_PARTS = 2
SMEM = pl.BlockSpec(memory_space=pltpu.SMEM)
VMEM = pl.BlockSpec(memory_space=pltpu.VMEM)
ANY = pl.BlockSpec(memory_space=pl.ANY)
HBM = pl.BlockSpec(memory_space=pltpu.HBM)
NN = (((1,), (0,)), ((), ()))
NT = (((1,), (1,)), ((), ()))
TN = (((0,), (0,)), ((), ()))


def halves(x):
    high = x.astype(BF16)
    return high, (x - high.astype(F32)).astype(BF16)


def product(a, b, dims):
    dot = functools.partial(lax.dot_general, dimension_numbers=dims, preferred_element_type=F32)
    return dot(a[0], b[0]) + (dot(a[0], b[1]) + dot(a[1], b[0]))


def reorder_kernel(steps, weights_t, values, interior, separator, held, in_sems, out_sems):
    tiles = held.shape[0]
    chunks = in_sems.shape[0]
    per = tiles // chunks
    for chunk in range(chunks):
        rows = pl.ds(chunk * per, per)
        pltpu.make_async_copy(values.at[rows], held.at[rows], in_sems.at[chunk]).start()
    root = jnp.sqrt(weights_t[...])
    for chunk in range(chunks):
        rows = pl.ds(chunk * per, per)
        pltpu.make_async_copy(values.at[rows], held.at[rows], in_sems.at[chunk]).wait()
        for tile in range(chunk * per, (chunk + 1) * per):
            held[tile] = held[tile] * root[:, tile : tile + 1]
            step = steps[tile]
            partition = lax.shift_right_logical(step, 1)
            odd = lax.bitwise_and(step, 1)

            @pl.when(odd == 0)
            def _():
                pltpu.make_async_copy(held.at[tile], interior.at[partition], out_sems.at[0]).start()

            @pl.when(odd == 1)
            def _():
                pltpu.make_async_copy(held.at[tile], separator.at[partition], out_sems.at[1]).start()

    half = pl.ds(0, tiles // 2)
    pltpu.make_async_copy(held.at[half], interior, out_sems.at[0]).wait()
    pltpu.make_async_copy(held.at[half], separator, out_sems.at[1]).wait()


def reorder(steps, weights_t, values):
    tiles, rows, cols = values.shape
    half = jax.ShapeDtypeStruct((tiles // 2, rows, cols), F32)
    return pl.pallas_call(
        reorder_kernel,
        out_shape=(half, half),
        in_specs=[SMEM, VMEM, ANY],
        out_specs=(HBM, HBM),
        scratch_shapes=[
            pltpu.VMEM((tiles, rows, cols), F32),
            pltpu.SemaphoreType.DMA((8,)),
            pltpu.SemaphoreType.DMA((2,)),
        ],
        compiler_params=pltpu.CompilerParams(vmem_limit_bytes=60 * MIB),
        name="reorder",
    )(steps, weights_t, values)


def wide(x):
    return jnp.broadcast_to(x, (8, BASE))


def sweep_small(entries, size):
    at = lambda i, j: (min(i, j), max(i, j))
    dets = []
    for p in range(0, size, 2):
        a, b, d = entries[p, p], entries[p, p + 1], entries[p + 1, p + 1]
        det = a * d - b * b
        dets.append(det)
        scale = 1.0 / det
        inv_a, inv_b, inv_d = d * scale, b * scale, a * scale
        others = [i for i in range(size) if i not in (p, p + 1)]
        u = {i: entries[at(i, p)] for i in others}
        v = {i: entries[at(i, p + 1)] for i in others}
        new_u = {i: inv_a * u[i] - inv_b * v[i] for i in others}
        new_v = {i: inv_d * v[i] - inv_b * u[i] for i in others}
        for i in others:
            for j in others:
                if i <= j:
                    entries[i, j] = entries[i, j] - u[i] * new_u[j] - v[i] * new_v[j]
        for i in others:
            entries[at(i, p)] = new_u[i]
            entries[at(i, p + 1)] = new_v[i]
        entries[p, p], entries[p, p + 1], entries[p + 1, p + 1] = -inv_a, inv_b, -inv_d
    return dets


def total_of(terms):
    while len(terms) > 1:
        terms = [sum(terms[i : i + 2][1:], terms[i]) for i in range(0, len(terms), 2)]
    return terms[0]


def sweep_base(x, columns, marks, beside):
    lane = lax.broadcasted_iota(jnp.int32, (8, BASE), 1)
    sub = lax.broadcasted_iota(jnp.int32, (8, BASE), 0)
    x = list(x)
    groups = len(x)
    dets = jnp.ones((8, BASE), F32)
    for q in range(groups):
        panel = x[q]
        slot = q % 2
        inside = (lane // 8) == q
        first = 8 * q
        for j in range(8):
            columns[slot, j] = wide(panel[:, first + j : first + j + 1])
        entries = {(i, j): wide(columns[slot, j, i : i + 1, :]) for i in range(8) for j in range(i, 8)}
        marks[slot] = jnp.where(inside, jnp.where(lane == first + sub, -1.0, 0.0), panel)
        rows = [wide(marks[slot, j : j + 1, :]) for j in range(8)]
        for at, det in enumerate(sweep_small(entries, 8)):
            dets = jnp.where(lane == 4 * q + at, det, dets)
        new_rows = [
            total_of([entries[min(i, j), max(i, j)] * rows[j] for j in range(8)]) for i in range(8)
        ]
        new_panel = new_rows[7]
        for i in range(7):
            new_panel = jnp.where(sub == i, new_rows[i], new_panel)
        after_this = (q + 1) % groups
        next_panel = x[after_this]
        next_panel = total_of(
            [jnp.where(inside, 0.0, next_panel)]
            + [wide(next_panel[:, first + j : first + j + 1]) * new_rows[j] for j in range(8)]
        )
        high, low = halves(panel)
        new_high, new_low = halves(new_panel)
        change = lax.dot_general(
            jnp.concatenate([high, high, low], axis=0),
            jnp.concatenate([new_high, new_low, new_high], axis=0),
            TN,
            preferred_element_type=F32,
        )
        for i in range(groups):
            x[i] = jnp.where(inside, 0.0, x[i]) + change[8 * i : 8 * i + 8]
        x[after_this] = next_panel
        x[q] = -new_panel
        for piece in beside[q::groups]:
            piece()
    return x, dets


def unit_scales(m, size):
    eye = lax.broadcasted_iota(jnp.int32, (BASE, BASE), 0) == lax.broadcasted_iota(
        jnp.int32, (BASE, BASE), 1
    )
    columns, rows = [], []
    for k in range(size // BASE):
        here = pl.ds(k * BASE, BASE)
        diagonal = jnp.where(eye, m[here, here], 0.0)
        columns.append(lax.rsqrt(jnp.sum(diagonal, axis=1, keepdims=True)))
        rows.append(lax.rsqrt(jnp.sum(diagonal, axis=0, keepdims=True)))
    return columns, jnp.concatenate(rows, axis=1)


def invert(m, panel, left, right, columns, marks, size, pivots):
    dot = functools.partial(lax.dot_general, dimension_numbers=NN, preferred_element_type=F32)
    left[...] = jnp.zeros(left.shape, BF16)
    right[...] = jnp.zeros(right.shape, BF16)

    rows, width = size // ROW_PARTS, 256 if size % 256 == 0 else BASE

    def change(at_row, at_column):
        these = slice(at_row, at_row + rows)
        part = left[these, :]
        tile = slice(at_column, at_column + width)
        m[these, tile] -= dot(part, right[0, :, tile]) + dot(part, right[1, :, tile])

    changes = [
        functools.partial(change, at_row, at_column)
        for at_column in range(0, size, width)
        for at_row in range(0, size, rows)
    ]

    def step(k, logs):
        here = pl.ds(pl.multiple_of(k * BASE, BASE), BASE)
        part = left[here, :]
        first = m[here, here] - (dot(part, right[0, :, here]) + dot(part, right[1, :, here]))
        groups = [first[8 * q : 8 * q + 8] for q in range(BASE // 8)]
        swept, dets = sweep_base(groups, columns, marks, changes)
        swept = jnp.concatenate(swept, axis=0)
        panel[...] = product(halves(-swept), halves(m[here, :]), NN)
        panel[:, here] = swept
        high, low = halves(panel[...])
        right[0, :BASE], right[0, BASE:] = high, high
        right[1, :BASE], right[1, BASE:] = low, low
        high, low = halves(m[:, here])
        left[:, :BASE], left[:, BASE:] = high, low
        left[here, :] = jnp.zeros((BASE, 2 * BASE), BF16)
        m[:, here] = jnp.zeros((size, BASE), F32)
        m[here, :] = panel[...]
        return logs + jnp.log(dets[0:1, :])

    logs = lax.fori_loop(0, pivots // BASE, step, jnp.zeros((1, BASE), F32))
    for piece in changes:
        piece()
    return jnp.sum(logs, axis=1, keepdims=True)


def begin(source, target, sem):
    copy = pltpu.make_async_copy(source, target, sem)
    copy.start()
    return copy


def own_kernel(
    place, time_diag, tiles_in, prior_in, block_out, inverse_out, logdet,
    tiles, prior, block, inverse, split, panel, left, right, columns, marks, sems,
):
    size = block.shape[0]
    scale = time_diag[0]
    own_columns = pl.ds(pl.multiple_of(place[0] * size, size), size)
    depth = tiles.shape[0]
    per = depth // 4
    tile_copies = [
        begin(tiles_in.at[pl.ds(c * per, per)], tiles.at[pl.ds(c * per, per)], sems.at[c]) for c in range(4)
    ]
    for c, copy in enumerate(tile_copies):
        copy.wait()
        if c == 2:
            prior_copy = begin(prior_in.at[:, own_columns], prior, sems.at[4])
        here = slice(c * per, (c + 1) * per)
        split[0, here], split[1, here] = halves(tiles[here])
    rows = 256
    for first in range(0, size, rows):
        here = slice(first, first + rows)
        gram = product((split[0, :, here], split[1, :, here]), (split[0], split[1]), TN)
        if first == 0:
            prior_copy.wait()
        block[here, :] = scale * prior[here, :] + gram
    block_copy = begin(block, block_out, sems.at[0])
    by_row, by_column = unit_scales(block, size)
    for k, row_scale in enumerate(by_row):
        here = pl.ds(k * BASE, BASE)
        inverse[here, :] = block[here, :] * row_scale * by_column
    log_total = invert(inverse, panel, left, right, columns, marks, size, size)
    logdet[...] = log_total - 2.0 * jnp.sum(jnp.log(by_column), axis=1, keepdims=True)
    copies = []
    for k, row_scale in enumerate(by_row):
        here = pl.ds(k * BASE, BASE)
        inverse[here, :] = inverse[here, :] * (-row_scale) * by_column
        copies.append(begin(inverse.at[here], inverse_out.at[here], sems.at[1 + k]))
    for copy in copies + [block_copy]:
        copy.wait()


def scratch_of(size):
    return [
        pltpu.VMEM((BASE, size), F32),
        pltpu.VMEM((size, 2 * BASE), BF16),
        pltpu.VMEM((2, 2 * BASE, size), BF16),
        pltpu.VMEM((2, 8, 8, BASE), F32),
        pltpu.VMEM((2, 8, BASE), F32),
    ]


def shape(*dims):
    return jax.ShapeDtypeStruct(dims, F32)


def invert_own(place, time_diag, tiles, prior):
    size = prior.shape[0]
    return pl.pallas_call(
        own_kernel,
        out_shape=(shape(size, size), shape(size, size), shape(1, 1)),
        in_specs=[SMEM, SMEM, ANY, ANY],
        out_specs=(HBM, HBM, VMEM),
        scratch_shapes=[
            pltpu.VMEM(tiles.shape, F32),
            pltpu.VMEM((size, size), F32),
            pltpu.VMEM((size, size), F32),
            pltpu.VMEM((size, size), F32),
            pltpu.VMEM((2, *tiles.shape), BF16),
        ]
        + scratch_of(size)
        + [pltpu.SemaphoreType.DMA((1 + size // BASE,))],
        compiler_params=pltpu.CompilerParams(vmem_limit_bytes=54 * MIB),
        cost_estimate=pl.CostEstimate(flops=120 * size**3, bytes_accessed=16 * MIB, transcendentals=0),
        name="invert_own",
    )(place, time_diag, tiles, prior)


def head_kernel(
    place, time_diag, other_in, block_in, prior_in, reached_out, early, rest, logdet,
    other_inverse, block, prior, reached, work, split_a, split_b, panel, left, right, columns, marks, sems,
):
    size = block.shape[0]
    head = early.shape[1]
    scale = time_diag[0]
    other_columns = pl.ds(pl.multiple_of((1 - place[0]) * size, size), size)
    copies = [
        begin(prior_in.at[:, other_columns], prior, sems.at[0]),
        begin(other_in, other_inverse, sems.at[1]),
    ]
    copies[0].wait()
    block_copy = begin(block_in, block, sems.at[2])
    split_a[0], split_a[1] = halves(scale * prior[...])
    copies[1].wait()
    split_b[0], split_b[1] = halves(other_inverse[...])
    rows = 256
    for first in range(0, size, rows):
        here = slice(first, first + rows)
        reached[here, :] = product((split_a[0, here], split_a[1, here]), (split_b[0], split_b[1]), NN)
        part = halves(reached[here, :])
        if first == 0:
            block_copy.wait()
        work[here, :] = block[here, :] - product(part, (split_a[0], split_a[1]), NT)
    reached_copy = begin(reached, reached_out, sems.at[0])
    by_row, by_column = unit_scales(work, size)
    for k, row_scale in enumerate(by_row):
        here = pl.ds(k * BASE, BASE)
        work[here, :] = work[here, :] * row_scale * by_column
    log_total = invert(work, panel, left, right, columns, marks, size, head)
    by_head = by_column[:, :head]
    logdet[...] = log_total - 2.0 * jnp.sum(jnp.log(by_head), axis=1, keepdims=True)
    back = 1.0 / by_column[:, head:]
    for k, row_scale in enumerate(by_row):
        here = pl.ds(k * BASE, BASE)
        if k * BASE < head:
            early[here, :] = work[here, :head] * (-row_scale) * by_head
        else:
            row_back = 1.0 / row_scale
            early[here, :] = work[here, :head] * row_back * by_head
            rest[pl.ds(k * BASE - head, BASE), :] = work[here, head:] * row_back * back
    reached_copy.wait()


def invert_head(place, time_diag, other_inverse, block, prior, head):
    size = prior.shape[0]
    return pl.pallas_call(
        head_kernel,
        out_shape=(shape(size, size), shape(size, head), shape(size - head, size - head), shape(1, 1)),
        in_specs=[SMEM, SMEM] + [ANY] * 3,
        out_specs=(HBM, VMEM, VMEM, VMEM),
        scratch_shapes=[pltpu.VMEM((size, size), F32)] * 5
        + [pltpu.VMEM((2, size, size), BF16)] * 2
        + scratch_of(size)
        + [pltpu.SemaphoreType.DMA((3,))],
        compiler_params=pltpu.CompilerParams(vmem_limit_bytes=60 * MIB),
        cost_estimate=pl.CostEstimate(flops=120 * size**3, bytes_accessed=16 * MIB, transcendentals=0),
        name="invert_head",
    )(place, time_diag, other_inverse, block, prior)


def tail_kernel(place, rest, own_log, head_log, inverse, logdet, panel, left, right, columns, marks):
    size = rest.shape[0]
    by_row, by_column = unit_scales(rest, size)
    for k, row_scale in enumerate(by_row):
        here = pl.ds(k * BASE, BASE)
        inverse[here, :] = rest[here, :] * row_scale * by_column
    log_total = invert(inverse, panel, left, right, columns, marks, size, size)
    log_total = head_log[...] + log_total - 2.0 * jnp.sum(jnp.log(by_column), axis=1, keepdims=True)
    logdet[...] = jnp.where(place[0] == 0, own_log[...], log_total)
    for k, row_scale in enumerate(by_row):
        here = pl.ds(k * BASE, BASE)
        inverse[here, :] = inverse[here, :] * (-row_scale) * by_column


def invert_tail(place, rest, own_log, head_log):
    size = rest.shape[0]
    return pl.pallas_call(
        tail_kernel,
        out_shape=(jax.ShapeDtypeStruct(rest.shape, F32), jax.ShapeDtypeStruct((1, 1), F32)),
        in_specs=[SMEM] + [VMEM] * 3,
        out_specs=(VMEM, VMEM),
        scratch_shapes=scratch_of(size),
        compiler_params=pltpu.CompilerParams(vmem_limit_bytes=60 * MIB),
        cost_estimate=pl.CostEstimate(flops=100 * size**3, bytes_accessed=4 * MIB, transcendentals=0),
        name="invert_tail",
    )(place, rest, own_log, head_log)


def own_column(gain_row, own, size):
    eye = lax.broadcasted_iota(jnp.int32, (BASE, BASE), 0) == lax.broadcasted_iota(
        jnp.int32, (BASE, BASE), 1
    )
    parts = []
    for k in range(size // BASE):
        piece = gain_row[:, pl.ds(pl.multiple_of(own * size + k * BASE, BASE), BASE)]
        parts.append(jnp.sum(jnp.where(eye, piece, 0.0), axis=1, keepdims=True))
    return jnp.concatenate(parts, axis=0)


def rows_kernel(
    place, rho, tail, early, reached_in, gain_row, coupling_out,
    reached, mine, coupling, split, sems,
):
    size, head = early.shape
    own = place[0]
    reached_copy = begin(reached_in, reached, sems.at[0])
    lower = halves(early[head:, :])
    mine[head:, :head] = -product(halves(tail[...]), lower, NN)
    mine[head:, head:] = tail[...]
    mine[:head, :] = -product(lower, halves(mine[head:, :]), TN)
    mine[:head, :head] += early[:head, :]
    own_columns = pl.ds(pl.multiple_of(own * size, size), size)
    other_columns = pl.ds(pl.multiple_of((1 - own) * size, size), size)
    sent = rho[0] * rho[1]
    own_gain = -sent * gain_row[:, own_columns]
    other_gain = sent * gain_row[:, other_columns]
    gain_column = own_column(gain_row, own, size)
    reached_copy.wait()
    split[0], split[1] = halves(reached[...])
    rows = 256
    copies = []
    for first in range(0, size, rows):
        here = slice(first, first + rows)
        part = mine[here, :] * gain_column[here]
        coupling[here, own_columns] = part * own_gain
        coupling[here, other_columns] = product(halves(part), (split[0], split[1]), NN) * other_gain
        place_out = pl.ds(first, rows)
        copies.append(begin(coupling.at[place_out], coupling_out.at[place_out], sems.at[first // rows]))
    for copy in copies:
        copy.wait()


def own_rows(place, rho, tail, early, reached, gain_row):
    size = early.shape[0]
    return pl.pallas_call(
        rows_kernel,
        out_shape=shape(size, 2 * size),
        in_specs=[SMEM] * 2 + [VMEM] * 2 + [ANY] + [VMEM],
        out_specs=HBM,
        scratch_shapes=[
            pltpu.VMEM((size, size), F32),
            pltpu.VMEM((size, size), F32),
            pltpu.VMEM((size, 2 * size), F32),
            pltpu.VMEM((2, size, size), BF16),
            pltpu.SemaphoreType.DMA((size // 256,)),
        ],
        compiler_params=pltpu.CompilerParams(vmem_limit_bytes=60 * MIB),
        cost_estimate=pl.CostEstimate(flops=20 * size**3, bytes_accessed=24 * MIB, transcendentals=0),
        name="own_rows",
    )(place, rho, tail, early, reached, gain_row)


def final_kernel(
    place, rho, time_diag, scalars, tiles_in, prior_in, coupling_in, inverse_1, inverse_0, early_0, early_1,
    tail_0, tail_1, gain_row, reduced_out,
    tiles, prior, coupling, inverse, early, tail, reduced, last, split_p, split_t, split_l, split_g, split_f, sems,
):
    size, head = early.shape
    own = place[0]
    weight, scale = scalars[0] * scalars[0], scalars[2]
    kept = rho[1] / rho[0]
    rows = 256

    own_columns = pl.ds(pl.multiple_of(own * size, size), size)
    other_columns = pl.ds(pl.multiple_of((1 - own) * size, size), size)

    @pl.when(own == 0)
    def _():
        begin(inverse_0, inverse, sems.at[0])

    @pl.when(own == 1)
    def _():
        begin(inverse_1, inverse, sems.at[0])

    other_copy = begin(prior_in.at[:, other_columns], prior.at[:, other_columns], sems.at[1])
    gain_column = own_column(gain_row, own, size)
    pltpu.make_async_copy(inverse_0, inverse, sems.at[0]).wait()

    @pl.when(own == 0)
    def _():
        begin(early_0, early, sems.at[2])
        begin(tail_0, tail, sems.at[3])

    @pl.when(own == 1)
    def _():
        begin(early_1, early, sems.at[2])
        begin(tail_1, tail, sems.at[3])

    tiles_copy = begin(tiles_in, tiles, sems.at[4])
    own_copy = begin(prior_in.at[:, own_columns], prior.at[:, own_columns], sems.at[0])
    coupling_copy = begin(coupling_in, coupling, sems.at[5])
    split_p[0], split_p[1] = halves(inverse[...])
    other_copy.wait()
    gain_0, gain_1 = gain_row[:, :size], gain_row[:, size:]

    def next_part(second):
        columns = slice(0, size) if second else slice(size, 2 * size)
        split_t[0], split_t[1] = halves(scale * prior[:, columns])
        for first in range(0, size, rows):
            here = slice(first, first + rows)
            if second:
                part = product((split_t[0, :, here], split_t[1, :, here]), (split_p[0], split_p[1]), TN)
            else:
                part = product((split_t[0, here], split_t[1, here]), (split_p[0], split_p[1]), NN)
            split_l[0, here], split_l[1, here] = halves(part)
            if first + rows > head:
                skip = max(head - first, 0)
                last[first + skip - head : first + rows - head, :] = part[skip:]
        pltpu.make_async_copy(early_0, early, sems.at[2]).wait()
        upper = (split_l[0, :head], split_l[1, :head])
        middle = product(halves(early[:head, :]), upper, NN)
        last[...] -= product(halves(early[head:, :]), upper, NN)
        if second:
            reduced[:, :head] = weight * middle.T * gain_column * gain_0[:, :head]
            reduced[:, head:size] = jnp.zeros((size, size - head), F32)
            middle_parts = halves(middle)
            for first in range(0, size, rows):
                here = slice(first, first + rows)
                term = inverse[here, :] + product(
                    (split_l[0, :head, here], split_l[1, :head, here]), middle_parts, TN
                )
                reduced[here, size:] = term * (-weight * gain_column[here]) * gain_1
        else:
            top = weight * gain_column[:head]
            reduced[:head, :head] = early[:head, :] * -top * gain_0[:, :head]
            reduced[:head, head:size] = jnp.zeros((head, size - head), F32)
            reduced[:head, size:] = top * middle * gain_1
            reduced[head:, :] = jnp.zeros((size - head, 2 * size), F32)

    @pl.when(own == 0)
    def _():
        next_part(False)

    @pl.when(own == 1)
    def _():
        next_part(True)

    pltpu.make_async_copy(tail_0, tail, sems.at[3]).wait()
    below = size - head
    eye = lax.broadcasted_iota(jnp.int32, (below, below), 0) == lax.broadcasted_iota(jnp.int32, (below, below), 1)
    split_f[0, :, :head], split_f[1, :, :head] = halves(-early[head:, :] * gain_0[:, :head])
    split_f[0, :, head:size], split_f[1, :, head:size] = halves(jnp.where(eye, 1.0, 0.0) * gain_0[:, head:])
    split_f[0, :, size:], split_f[1, :, size:] = halves(-last[...] * gain_1)
    mine = (split_f[0, :, own_columns], split_f[1, :, own_columns])
    solved = halves(-weight * product(halves(tail[...]), mine, NN))
    tiles_copy.wait()
    split_g[0], split_g[1] = halves(tiles[...])
    own_copy.wait()
    coupling_copy.wait()
    copies = []
    for first in range(0, size, rows):
        here = slice(first, first + rows)
        reduced[here, :] += product((solved[0][:, here], solved[1][:, here]), (split_f[0], split_f[1]), TN)
        gram = product((split_g[0, :, here], split_g[1, :, here]), (split_g[0], split_g[1]), TN)
        for columns, term in ((own_columns, gram), (other_columns, 0.0)):
            reduced[here, columns] += time_diag[1] * prior[here, columns] + term + kept * coupling[here, columns]
        place_out = pl.ds(first, rows)
        copies.append(begin(reduced.at[place_out], reduced_out.at[place_out], sems.at[first // rows]))
    for copy in copies:
        copy.wait()


def final_rows(place, rho, time_diag, scalars, tiles, prior, coupling, inverses, earlies, tails, gain_row):
    size, head = earlies[0].shape
    below = size - head
    return pl.pallas_call(
        final_kernel,
        out_shape=shape(size, 2 * size),
        in_specs=[SMEM] * 4 + [ANY] * 9 + [VMEM],
        out_specs=HBM,
        scratch_shapes=[
            pltpu.VMEM(tiles.shape, F32),
            pltpu.VMEM((size, 2 * size), F32),
            pltpu.VMEM((size, 2 * size), F32),
            pltpu.VMEM((size, size), F32),
            pltpu.VMEM((size, head), F32),
            pltpu.VMEM((below, below), F32),
            pltpu.VMEM((size, 2 * size), F32),
            pltpu.VMEM((below, size), F32),
            pltpu.VMEM((2, size, size), BF16),
            pltpu.VMEM((2, size, size), BF16),
            pltpu.VMEM((2, size, size), BF16),
            pltpu.VMEM((2, *tiles.shape), BF16),
            pltpu.VMEM((2, below, 2 * size), BF16),
            pltpu.SemaphoreType.DMA((6,)),
        ],
        compiler_params=pltpu.CompilerParams(vmem_limit_bytes=60 * MIB),
        cost_estimate=pl.CostEstimate(flops=30 * size**3, bytes_accessed=32 * MIB, transcendentals=0),
        name="final_rows",
    )(place, rho, time_diag, scalars, tiles, prior, coupling, *inverses, *earlies, *tails, gain_row)


def from_next(x):
    count = lax.axis_size("tm")
    return lax.ppermute(x, "tm", [(i, i - 1) for i in range(1, count)])


def from_other(x):
    return lax.ppermute(x, "tile", [(0, 1), (1, 0)])


def to_partitions(x):
    return lax.all_to_all(x, "tm", split_axis=0, concat_axis=0, tiled=True).reshape(-1, x.shape[-1])


def from_next_core(x, core):
    count = lax.axis_size("tm")
    pairs = [(2 * i + core, 2 * (i - 1) + core) for i in range(1, count)]
    return lax.ppermute(x, ("tm", "tile"), pairs)


def across(x, core):
    return lax.ppermute(x, "tile", [(core, 1 - core)])


def after(x, *others):
    return lax.optimization_barrier((x, *others))[0]


def on_device(prior, node_gain, time_diag, rho, values, weights, steps):
    size, nodes = prior.shape
    head = size // 2
    own = lax.axis_index("tile")
    place = own.reshape(1).astype(jnp.int32)
    interior, separator = reorder(steps[0, 0], weights[0].T, values[0])
    scalars = from_next(jnp.concatenate([rho, time_diag]))
    gain_row = node_gain.reshape(1, nodes)
    interior = to_partitions(interior)
    interior, separator, scalars, gain_row = lax.optimization_barrier((interior, separator, scalars, gain_row))
    separator = to_partitions(separator)
    block, own_inverse, own_log = invert_own(place, time_diag, interior, prior)
    next_inverse_1 = from_next_core(own_inverse, 1)
    other_inverse, separator = lax.optimization_barrier((from_other(own_inverse), separator))
    reached, early, rest, head_log = invert_head(place, time_diag, other_inverse, block, prior, head)
    next_early_0 = from_next_core(early, 0)
    next_inverse_1 = after(next_inverse_1, head_log)
    next_inverse_0 = across(next_inverse_1, 1)
    tail, log = invert_tail(place, after(rest, next_inverse_1), own_log, head_log)
    log = log.reshape(1)
    other_log = from_other(log)
    next_tail_0 = from_next_core(tail, 0)
    next_early_1 = across(after(next_early_0, log), 0)
    coupling = own_rows(place, rho, tail, early, reached, gain_row)
    next_tail_0, coupling, next_early_1, next_inverse_0, other_log = lax.optimization_barrier(
        (next_tail_0, coupling, next_early_1, next_inverse_0, other_log)
    )
    next_tail_1 = across(next_tail_0, 0)
    reduced = final_rows(
        place, rho, time_diag, scalars, separator, prior, coupling,
        (next_inverse_1, next_inverse_0), (next_early_0, next_early_1), (next_tail_0, next_tail_1), gain_row,
    )
    interior_logdet = (log + other_log) / nodes
    return reduced[None], coupling[None], interior_logdet


def solution(mesh):
    in_specs = (
        P("tile", None),
        P(),
        P("tm"),
        P("tm"),
        P("tile", "tm", None, None),
        P("tile", "tm", None),
        P("tile", "tm", None),
    )
    out_specs = (P("tm", "tile", None), P("tm", "tile", None), P("tm"))
    return jax.shard_map(on_device, mesh=mesh, in_specs=in_specs, out_specs=out_specs, check_vma=False)
```
